32 devices in a mesh: dp: 8 (over y, x, core), seq: 4 (over z).
Axes of the slice: x: 2, y: 2, z: 4, core: 2. Of those that a mesh axis runs over, the one named last changes fastest.
Arguments:
- token_ids: int32 [32, 1024], P('dp', 'seq'), may hold values from 0 to 31
- positions: int32 [32, 1024], P('dp', 'seq'), may hold values from 0 to 4095, as said below
- embed: bfloat16 [32, 1024], replicated, may hold values from -6 to 6
- ln_gain: float32 [1024], replicated, may hold values from 0.1 to 1.9
- ln_shift: float32 [1024], replicated, may hold values from -3 to 3
- w_qkv: bfloat16 [1024, 3072], replicated, may hold values from -0.1875 to 0.1875
- w_out: bfloat16 [1024, 1024], replicated, may hold values from -1.5 to 1.5
- w_up: bfloat16 [1024, 4096], replicated, may hold values from -0.1875 to 0.1875
- b_up: float32 [4096], replicated, may hold values from -3 to 3
- w_down: bfloat16 [4096, 1024], replicated, may hold values from -0.09375 to 0.09375
- b_down: float32 [1024], replicated, may hold values from -3 to 3
- cotangent: bfloat16 [32, 1024, 1024], P('dp', 'seq'), may hold values from -6 to 6
Outputs:
- output: bfloat16 [32, 1024, 1024], P('dp', 'seq')
- embed_grad: float32 [1024, 32], P(('dp', 'seq'))
- gain_grad: float32 [1024], P(('dp', 'seq'))
- shift_grad: float32 [1024], P(('dp', 'seq'))
- qkv_grad: float32 [1024, 3072], P(('dp', 'seq'))
- out_grad: float32 [1024, 1024], P(('dp', 'seq'))
- up_grad: float32 [1024, 4096], P(('dp', 'seq'))
- up_bias_grad: float32 [4096], P(('dp', 'seq'))
- down_grad: float32 [4096, 1024], P(('dp', 'seq'))
- down_bias_grad: float32 [1024], P(('dp', 'seq'))
The draws below stay inside these ranges and needn't reach their ends.
Inputs may be any that keep to these rules, and one draw needn't show every extreme that they name: Within each window, positions rise by 1, 2 or 3 from each token to the next; some window ends at the largest value.
All inputs are finite; a program needn't handle non-finite values.
Results may differ from the reference program's by a relative error of at most 0.0087.
Values may be sent and summed in bfloat16 or wider, within the bound.
A program may use at most 192 MiB of HBM per device.

```python
import jax
import jax.numpy as jnp
from jax import lax

D = 1024
HEADS = 16
HEAD_DIM = 64
ROT = 32
FF = 4096
VOCAB = 32
LEN = 1024
WINDOWS = 32


def draw_positions(key, part):
    key = jax.random.fold_in(key, 7)
    end_key, stride_key, pick_key = jax.random.split(key, 3)
    ends = jax.random.randint(end_key, (WINDOWS,), 0, 1024) + 3 * LEN
    chosen = jax.random.randint(pick_key, (), 0, WINDOWS)
    ends = jnp.where(jnp.arange(WINDOWS) == chosen, 3 * LEN + 1023, ends)
    strides = jax.random.randint(stride_key, (WINDOWS, LEN), 1, 4)
    running = jnp.cumsum(strides, axis=1)
    after = running[:, -1:] - running
    return (ends[:, None] - after).astype(jnp.int32)


def place_ends(drawn, stream_key, low, largest):
    index_at = [jax.random.randint(jax.random.fold_in(stream_key, axis), (), 0, length) for axis, length in enumerate(drawn.shape)]
    widest = drawn.shape.index(max(drawn.shape))
    beside = index_at[:widest] + [(index_at[widest] + 1) % drawn.shape[widest]] + index_at[widest + 1:]
    return drawn.at[tuple(index_at)].set(low).at[tuple(beside)].set(largest)


def spiked(entries, own_key, source, target, shards_of, factor):
    owner, partner = [(jnp.arange(entries.shape[dim]) // (entries.shape[dim] // shards_of)).reshape([-1 if axis == dim else 1 for axis in range(entries.ndim)]) for dim in (source, target)]
    chosen = jax.random.permutation(own_key, shards_of)[partner]
    strong = (owner == chosen) | (owner == (partner + shards_of // 2) % shards_of)
    return jnp.where(strong, factor * entries, entries)


def levels(key, shape, pieces, low, largest):
    level = 1.0
    for position, shards_of in pieces:
        heights = jax.random.uniform(jax.random.fold_in(jax.random.fold_in(key, 6), position), (shards_of,), jnp.float32, low / len(pieces), largest / len(pieces))
        level = level * jnp.repeat(jnp.exp(heights), shape[position] // shards_of).reshape((-1,) + (1,) * (len(shape) - 1 - position))
    return level


def gaussian(stream_key, shape, scale, most, pieces=(), kind=jnp.bfloat16):
    factor_of = levels(stream_key, shape, pieces, -0.22, 0.18) if pieces else 1.0
    values = jax.random.normal(stream_key, shape, jnp.float32) * scale * factor_of
    return jnp.minimum(jnp.maximum(values, -most), most).astype(kind)


def noise_with(rng, dims, scale, limit, shards, heavy, dtype=jnp.bfloat16):
    values = scale * jax.random.normal(rng, dims, jnp.float32)
    if shards:
        values = values * levels(rng, dims, shards, -0.22, 0.18)
    return jnp.clip(spiked(values, jax.random.fold_in(rng, 3), *heavy), -limit, limit).astype(dtype)


def setup_inputs(seed: int = 0) -> dict:
    keys = jax.random.split(jax.random.key(seed), 13)
    token_ids = place_ends(jax.random.randint(keys[0], (WINDOWS, LEN), 0, VOCAB), jax.random.fold_in(keys[0], 1), 0, VOCAB - 1).astype(jnp.int32)
    positions = draw_positions(jax.random.fold_in(keys[12], 71), 0)
    embed = gaussian(keys[2], (VOCAB, D), 1.0, 6.0)
    ln_gain = jnp.clip(1.0 + 0.18 * jax.random.normal(keys[3], (D,), jnp.float32), 0.1, 1.9)
    ln_shift = gaussian(keys[4], (D,), 0.5, 3.0, (), jnp.float32)
    w_qkv = gaussian(keys[5], (D, 3 * D), D ** -0.5, 0.1875)
    w_out = gaussian(keys[6], (D, D), (D * 16 // LEN) ** -0.5, 1.5)
    w_up = gaussian(keys[7], (D, FF), D ** -0.5, 0.1875)
    b_up = gaussian(keys[8], (FF,), 0.5, 3.0, (), jnp.float32)
    w_down = gaussian(keys[9], (FF, D), FF ** -0.5, 0.09375)
    b_down = gaussian(keys[10], (D,), 0.5, 3.0, (), jnp.float32)
    cotangent = noise_with(keys[11], (WINDOWS, LEN, D), 1.0, 6.0, ((0, 8), (1, 4)), (0, 2, 8, 2.0))
    return {"token_ids": token_ids, "positions": positions, "embed": embed, "ln_gain": ln_gain, "ln_shift": ln_shift, "w_qkv": w_qkv, "w_out": w_out, "w_up": w_up, "b_up": b_up, "w_down": w_down, "b_down": b_down, "cotangent": cotangent}


ln_epsilon = 1e-05

@jax.custom_vjp
def low(v):
    return lax.optimization_barrier(v.astype(jnp.bfloat16)).astype(jnp.float32)

@jax.custom_vjp
def low_back(v):
    return v

def low_keep(v):
    return (low(v), None)

def low_pass(kept, grad):
    return (grad,)

def back_keep(v):
    return (v, None)

def back_low(kept, grad):
    return (low(grad),)
low.defvjp(low_keep, low_pass)
low_back.defvjp(back_keep, back_low)

def layer_norm(inputs, gain, shift):
    center = inputs - lax.optimization_barrier(jnp.mean(inputs, axis=-1, keepdims=True))
    spread = lax.optimization_barrier(jnp.mean(center * center, axis=-1, keepdims=True))
    return center * lax.rsqrt(spread + ln_epsilon) * gain + shift

def rotary_tables(positions, heads, head_dim, rot_dim):
    pair_index = jnp.arange(head_dim // 2)
    inverse = jnp.where(pair_index < rot_dim // 2, 10000.0 ** (-2.0 * pair_index.astype(jnp.float32) / rot_dim), 0.0)
    angles = jnp.repeat(positions.astype(jnp.float32)[..., None] * inverse, 2, axis=-1)
    cosine = jnp.tile(jnp.cos(angles), heads)
    sine = jnp.tile(jnp.sin(angles), heads)
    return (cosine, sine)

def rotate(values, cosine, sine):
    paired = values.reshape(values.shape[:-1] + (values.shape[-1] // 2, 2))
    partner = jnp.stack([-paired[..., 1], paired[..., 0]], axis=-1).reshape(values.shape)
    return values * cosine + partner * sine

def gelu_tanh(values):
    return jax.nn.gelu(values, approximate=True)

def attend_window(query, keys_rot, values_low):
    length = query.shape[0]
    head_shape = (length, HEADS, HEAD_DIM)
    scores = jnp.einsum('qhd,khd->hqk', query.reshape(head_shape), keys_rot.reshape(head_shape), precision=lax.Precision.HIGHEST) * HEAD_DIM ** (-0.5)
    scores = low_back(scores)
    causal = jnp.arange(length)[:, None] >= jnp.arange(length)[None, :]
    scores = jnp.where(causal[None], scores, -1e+30)
    probs = low(jax.nn.softmax(scores, axis=-1))
    mixed = jnp.einsum('hqk,khd->qhd', probs, values_low.reshape(head_shape), precision=lax.Precision.HIGHEST)
    return mixed.reshape(length, HEADS * HEAD_DIM)

def window_forward(embed, ln_gain, ln_shift, w_qkv, w_out, w_up, b_up, w_down, b_down, token_row, position_row):
    width = embed.shape[1]
    inputs = embed[token_row]
    normed = low(layer_norm(inputs, ln_gain, ln_shift))
    projected = low_back(jnp.dot(normed, w_qkv, precision=lax.Precision.HIGHEST))
    cosine, sine = rotary_tables(position_row, HEADS, HEAD_DIM, ROT)
    query = low(low_back(rotate(projected[:, :width], cosine, sine)))
    keys_rot = low(low_back(rotate(projected[:, width:2 * width], cosine, sine)))
    values_low = low(low_back(projected[:, 2 * width:]))
    attended = low(low_back(jax.checkpoint(attend_window)(query, keys_rot, values_low)))
    up_proj = low_back(jnp.dot(normed, w_up, precision=lax.Precision.HIGHEST) + b_up)
    activated = low(gelu_tanh(up_proj))
    mixed_attn = jnp.dot(attended, w_out, precision=lax.Precision.HIGHEST)
    mixed_mlp = jnp.dot(activated, w_down, precision=lax.Precision.HIGHEST)
    return inputs + mixed_attn + mixed_mlp + b_down

def reference(token_ids, positions, embed, ln_gain, ln_shift, w_qkv, w_out, w_up, b_up, w_down, b_down, cotangent):
    params = tuple((p.astype(jnp.float32) for p in (embed, ln_gain, ln_shift, w_qkv, w_out, w_up, b_up, w_down, b_down)))

    def one_window(totals, window_item):
        token_row, position_row, grad_row = window_item

        def forward(*weights):
            return window_forward(*weights, token_row, position_row)
        result, pull = jax.vjp(forward, *params)
        grads = pull(grad_row.astype(jnp.float32))
        return (tuple((t + g for t, g in zip(totals, grads))), result.astype(jnp.bfloat16))
    zeros = tuple((jnp.zeros_like(p) for p in params))
    totals, output = lax.scan(one_window, zeros, (token_ids, positions, cotangent))
    return (output, totals[0].T, totals[1], totals[2], totals[3], totals[4], totals[5], totals[6], totals[7], totals[8])
```

```python
from functools import partial

import jax
import jax.numpy as jnp
from jax import lax
from jax.experimental import pallas as pl
from jax.experimental.pallas import tpu as pltpu
from jax.sharding import PartitionSpec as P

HEADS = 16
HEAD_DIM = 64
ROT = 32
GROUP = 4

ln_epsilon = 1e-05
LOG2E = 1.4426950408889634
F32 = jnp.float32
BF16 = jnp.bfloat16


def dot(a, b):
    return lax.dot_general(a, b, (((1,), (0,)), ((), ())), preferred_element_type=F32)


def dot_t(a, b):
    return lax.dot_general(a, b, (((1,), (1,)), ((), ())), preferred_element_type=F32)


def exact_dot(a, b, dims=(((1,), (0,)), ((), ()))):
    return lax.dot_general(a, b, dims, precision=lax.Precision.HIGHEST, preferred_element_type=F32)


def terms(value, count):
    parts = []
    for _ in range(count):
        high = lax.reduce_precision(value, 8, 7)
        parts.append(high.astype(BF16))
        value = value - high
    return parts


def swap_pairs(values):
    paired = values.reshape(values.shape[:-1] + (values.shape[-1] // 2, 2))
    return jnp.stack([-paired[..., 1], paired[..., 0]], axis=-1).reshape(values.shape)


def swap_pairs_back(values):
    paired = values.reshape(values.shape[:-1] + (values.shape[-1] // 2, 2))
    return jnp.stack([paired[..., 1], -paired[..., 0]], axis=-1).reshape(values.shape)


def attention_kernel(
    place_ref, oh_ref, oh_t_ref, cos_ref, sin_ref, cos_t_ref, sin_t_ref, tab_ref, grad_ref,
    po_ref, agg_ref, keys_ref, probs_ref, grads_ref,
):
    vocab = oh_t_ref.shape[1]
    length = oh_ref.shape[1]
    rows = grad_ref.shape[2]
    width = GROUP * HEAD_DIM
    window = pl.program_id(1)
    place = place_ref[0]

    @pl.when(window == 0)
    def _():
        agg_ref[...] = jnp.zeros_like(agg_ref)

    def run(first):
        span = first + rows
        lane_head = lax.broadcasted_iota(jnp.int32, (rows, width), 1) // HEAD_DIM
        twice = lambda v: jnp.concatenate([v] * (width // v.shape[-1]), axis=-1)

        def turned(tokens, part):
            oh = oh_ref[0, tokens, :]
            return (
                dot(oh, tab_ref[0, :, 2 * part * width : (2 * part + 1) * width]) * twice(cos_ref[0, tokens, :])
                + dot(oh, tab_ref[0, :, (2 * part + 1) * width : (2 * part + 2) * width])
                * twice(sin_ref[0, tokens, :])
            ).astype(BF16)

        query = turned(slice(first, span), 0)
        for lower in range(0, span, rows):
            keys_ref[lower : lower + rows, :] = turned(slice(lower, lower + rows), 1)
        keys = keys_ref[:span, :]
        keys_t = keys.T
        oh = oh_ref[0, :span, :vocab]
        oh_t = oh_t_ref[0, :, :span]
        key_at = lax.broadcasted_iota(jnp.int32, (rows, rows), 0)
        query_at = lax.broadcasted_iota(jnp.int32, (rows, rows), 1)
        kept = key_at <= query_at
        grad_keys = None
        for head in range(GROUP):
            own = jnp.where(lane_head == head, query, jnp.zeros_like(query))
            scores = dot_t(keys, own) * (HEAD_DIM**-0.5 * LOG2E)
            last = jnp.where(kept, scores[first:, :], -1e30)
            if first:
                scores = jnp.concatenate([scores[:first, :], last], axis=0)
            else:
                scores = last
            top = jnp.max(scores, axis=0, keepdims=True)
            weights = jnp.exp2(scores - top)
            low = weights.astype(BF16)
            summed = dot(oh_t, low)
            inverse = 1.0 / jnp.sum(summed, axis=0, keepdims=True)
            share = summed * inverse
            po_ref[0, head * vocab : (head + 1) * vocab, :] = share.astype(BF16)
            grad = grad_ref[0, head * vocab : (head + 1) * vocab, :]
            inner = jnp.sum(share * grad, axis=0, keepdims=True)
            centered = ((grad - inner) * inverse).astype(BF16)
            d_scores = (weights * dot(oh, centered)).astype(BF16)
            d_query = dot(keys_t[head * HEAD_DIM : (head + 1) * HEAD_DIM, :], d_scores)
            grads_ref[head * HEAD_DIM : (head + 1) * HEAD_DIM, :] = d_query
            term = dot(d_scores, own)
            grad_keys = term if grad_keys is None else grad_keys + term
        agg_ref[0, :, 2 * width : 3 * width] += dot(oh_t, (grad_keys * twice(cos_ref[0, :span, :])).astype(BF16))
        agg_ref[0, :, 3 * width :] += dot(oh_t, (grad_keys * twice(sin_ref[0, :span, :])).astype(BF16))
        grad_query = grads_ref[...]
        cos_t = jnp.concatenate([cos_t_ref[0]] * (width // cos_t_ref.shape[1]), axis=0)
        sin_t = jnp.concatenate([sin_t_ref[0]] * (width // cos_t_ref.shape[1]), axis=0)
        own_oh_t = oh_t_ref[0, :, first:span]
        agg_ref[0, :, :width] += dot_t(own_oh_t, (grad_query * cos_t).astype(BF16))
        agg_ref[0, :, width : 2 * width] += dot_t(own_oh_t, (grad_query * sin_t).astype(BF16))

    for part in range(length // rows):
        pl.when(place == part)(partial(run, part * rows))


def attention(place, one_hot4, one_hot_t, cosine, sine, cosine_t, sine_t, tables, grad_t):
    windows, length, _ = one_hot4.shape
    vocab = one_hot_t.shape[1]
    rows = grad_t.shape[2]
    groups = tables.shape[0]
    width = GROUP * HEAD_DIM
    by_window = lambda g, w, *_: (w, 0, 0)
    return pl.pallas_call(
        attention_kernel,
        grid_spec=pltpu.PrefetchScalarGridSpec(
            num_scalar_prefetch=1,
            grid=(groups, windows),
            in_specs=[
                pl.BlockSpec((1, length, 128), by_window),
                pl.BlockSpec((1, vocab, length), by_window),
                pl.BlockSpec((1, length, 128), by_window),
                pl.BlockSpec((1, length, 128), by_window),
                pl.BlockSpec((1, 128, rows), by_window),
                pl.BlockSpec((1, 128, rows), by_window),
                pl.BlockSpec((1, 128, 4 * width), lambda g, w, *_: (g, 0, 0)),
                pl.BlockSpec((1, GROUP * vocab, rows), lambda g, w, *_: (w, g, 0)),
            ],
            out_specs=[
                pl.BlockSpec((1, GROUP * vocab, rows), lambda g, w, *_: (w, g, 0)),
                pl.BlockSpec((1, vocab, 4 * width), lambda g, w, *_: (g, 0, 0)),
            ],
            scratch_shapes=[
                pltpu.VMEM((length, width), BF16),
                pltpu.VMEM((length, rows), BF16),
                pltpu.VMEM((width, rows), F32),
            ],
        ),
        out_shape=[
            jax.ShapeDtypeStruct((windows, groups * GROUP * vocab, rows), BF16),
            jax.ShapeDtypeStruct((groups, vocab, 4 * width), F32),
        ],
        compiler_params=pltpu.CompilerParams(
            vmem_limit_bytes=48 * 1024 * 1024, dimension_semantics=("arbitrary", "arbitrary")
        ),
    )(place, one_hot4, one_hot_t, cosine, sine, cosine_t, sine_t, tables, grad_t)


def own_slice(value, index, size, axis):
    return lax.dynamic_slice_in_dim(value, index * size, size, axis)


def per_device(
    token_ids, positions, embed, ln_gain, ln_shift, w_qkv, w_out, w_up, b_up, w_down, b_down, cotangent
):
    vocab, width = embed.shape
    hidden = w_up.shape[1]
    windows, rows = token_ids.shape
    place = lax.axis_index("seq")
    devices = lax.axis_size("dp") * lax.axis_size("seq")
    index = lax.axis_index("dp") * lax.axis_size("seq") + place
    groups = HEADS // GROUP
    names = ("dp", "seq")

    both = lax.all_gather(jnp.stack([token_ids, positions]), "seq", axis=2, tiled=True)
    all_ids, all_positions = both[0], both[1]
    length = all_ids.shape[1]

    inputs = embed.astype(F32)
    center = inputs - jnp.mean(inputs, axis=-1, keepdims=True)
    spread = jnp.mean(center * center, axis=-1, keepdims=True)
    rstd = lax.rsqrt(spread + ln_epsilon)
    xhat = center * rstd
    normed = (xhat * ln_gain + ln_shift).astype(BF16)
    projected = dot(normed, w_qkv)
    query_tab, key_tab, value_tab = jnp.split(projected, 3, axis=1)
    value_low = value_tab.astype(BF16)
    value_heads = value_low.reshape(vocab, HEADS, HEAD_DIM)
    w_out_heads = w_out.reshape(HEADS, HEAD_DIM, width)
    mixed_tab = jnp.einsum("vhd,hde->hve", value_heads, w_out_heads, preferred_element_type=F32)
    mixed_low = mixed_tab.reshape(HEADS * vocab, width).astype(BF16)

    ids = jnp.arange(vocab, dtype=jnp.int32)
    one_hot4 = (all_ids[..., None] == jnp.tile(ids, 128 // vocab)).astype(BF16)
    one_hot_t = (all_ids[:, None, :] == ids[:, None]).astype(BF16)
    pair = jnp.arange(HEAD_DIM // 2)
    inverse = jnp.where(pair < ROT // 2, 10000.0 ** (-2.0 * pair.astype(F32) / ROT), 0.0)

    def tables(at, axis):
        shape = [1, 1, 1]
        shape[axis] = inverse.shape[0]
        angles = jnp.expand_dims(at.astype(F32), axis) * inverse.reshape(shape)
        wide = lambda v: jnp.concatenate([jnp.repeat(v, 2, axis=axis)] * (128 // HEAD_DIM), axis=axis)
        return wide(jnp.cos(angles)), wide(jnp.sin(angles))

    cosine, sine = tables(all_positions, 2)
    cosine_t, sine_t = tables(positions, 1)

    flat = cotangent.reshape(windows * rows, width)
    own_t = (token_ids.reshape(-1)[None, :] == ids[:, None]).astype(BF16)
    cot_sum = lax.psum(dot(own_t, flat), names)
    grad_t = jnp.einsum("hd,wtd->wht", mixed_low, cotangent, preferred_element_type=F32)

    def packed(table):
        high, mid, low = terms(table, 3)
        return jnp.concatenate([high, mid, low] + [jnp.zeros_like(high)] * (128 // vocab - 3), axis=0)

    parts = [packed(t).reshape(128, groups, GROUP * HEAD_DIM) for t in (
        query_tab, swap_pairs(query_tab), key_tab, swap_pairs(key_tab))]
    attn_tab = jnp.stack(parts, axis=2).transpose(1, 0, 2, 3).reshape(groups, 128, 4 * GROUP * HEAD_DIM)
    po_t, agg = attention(place[None], one_hot4, one_hot_t, cosine, sine, cosine_t, sine_t, attn_tab, grad_t)

    agg = agg.reshape(groups, vocab, 4, GROUP * HEAD_DIM).transpose(2, 1, 0, 3).reshape(4, vocab, width)
    scale = HEAD_DIM**-0.5
    query_sum = (agg[0] + swap_pairs_back(agg[1])) * scale
    key_sum = (agg[2] + swap_pairs_back(agg[3])) * scale
    mixes = jnp.einsum("wht,wtd->hd", po_t, cotangent, preferred_element_type=F32)
    mixes_low = mixes.astype(BF16).reshape(HEADS, vocab, width)
    value_sum = jnp.einsum("hve,hde->vhd", mixes_low, w_out_heads, preferred_element_type=F32)
    out_grad = jnp.einsum("vhd,hve->hde", value_heads, mixes_low, preferred_element_type=F32).reshape(width, width)
    out_grad = lax.psum_scatter(out_grad, names, scatter_dimension=0, tiled=True)
    qkv_sum = lax.psum(
        jnp.concatenate([query_sum, key_sum, value_sum.reshape(vocab, width)], axis=1), names
    )

    up = dot(normed, w_up) + b_up
    activated, gelu_pull = jax.vjp(lambda u: jax.nn.gelu(u, approximate=True), up)
    act_low = activated.astype(BF16)
    mlp_tab = dot(act_low, w_down)
    grad_act = sum(dot_t(t, w_down) for t in terms(cot_sum, 2))
    d_up = gelu_pull(grad_act)[0]
    d_normed = sum(dot_t(t, w_up) for t in terms(d_up, 2)) + sum(dot_t(t, w_qkv) for t in terms(qkv_sum, 2))

    base = inputs + mlp_tab + b_down
    own_oh4 = (token_ids[..., None] == jnp.tile(ids, 2)).astype(BF16)
    output = (
        jnp.einsum("wht,hd->wtd", po_t, mixed_low, preferred_element_type=F32)
        + jnp.einsum("wtv,vd->wtd", own_oh4, jnp.concatenate(terms(base, 2), axis=0), preferred_element_type=F32)
    ).astype(BF16)

    over_ids = (((0,), (0,)), ((), ()))
    d_rows = width // devices
    f_rows = hidden // devices
    normed_own = own_slice(normed, index, d_rows, 1).astype(F32)
    act_own = own_slice(act_low, index, f_rows, 1).astype(F32)
    qkv_grad = exact_dot(normed_own, qkv_sum, over_ids)
    up_grad = exact_dot(normed_own, d_up, over_ids)
    down_grad = exact_dot(act_own, cot_sum, over_ids)
    up_bias_grad = jnp.sum(own_slice(d_up, index, f_rows, 1), axis=0)
    down_bias_grad = jnp.sum(own_slice(cot_sum, index, d_rows, 1), axis=0)
    scaled = d_normed * ln_gain
    d_input = cot_sum + rstd * (
        scaled
        - jnp.mean(scaled, axis=-1, keepdims=True)
        - xhat * jnp.mean(scaled * xhat, axis=-1, keepdims=True)
    )
    embed_grad = own_slice(d_input, index, d_rows, 1).T
    d_normed_own = own_slice(d_normed, index, d_rows, 1)
    gain_grad = jnp.sum(d_normed_own * own_slice(xhat, index, d_rows, 1), axis=0)
    shift_grad = jnp.sum(d_normed_own, axis=0)
    return (
        output, embed_grad, gain_grad, shift_grad, qkv_grad, out_grad, up_grad, up_bias_grad, down_grad,
        down_bias_grad,
    )


def solution(mesh):
    in_specs = (P("dp", "seq"), P("dp", "seq")) + (P(),) * 9 + (P("dp", "seq", None),)
    both = ("dp", "seq")
    out_specs = (
        P("dp", "seq", None),
        P(both, None),
        P(both),
        P(both),
        P(both, None),
        P(both, None),
        P(both, None),
        P(both),
        P(both, None),
        P(both),
    )
    return jax.shard_map(per_device, mesh=mesh, in_specs=in_specs, out_specs=out_specs, check_vma=False)
```

```python
from functools import partial
import jax
import jax.numpy as jnp
from jax import lax
from jax.experimental import pallas as pl
from jax.experimental.pallas import tpu as pltpu
from jax.sharding import PartitionSpec as P

HEADS = 16
HEAD_DIM = 64
ROT = 32
GROUP = 4
PAIR = 2
ln_epsilon = 1e-05
LOG2E = 1.4426950408889634
F32 = jnp.float32
BF16 = jnp.bfloat16
LANES = 128

def dot(a, b):
    return lax.dot_general(a, b, (((1,), (0,)), ((), ())), preferred_element_type=F32)

def dot_t(a, b):
    return lax.dot_general(a, b, (((1,), (1,)), ((), ())), preferred_element_type=F32)

def t_dot(a, b):
    return lax.dot_general(a, b, (((0,), (0,)), ((), ())), preferred_element_type=F32)

def iota(shape, axis):
    return lax.broadcasted_iota(jnp.int32, shape, axis)

def three_terms(value):
    parts = []
    for _ in range(3):
        high = value.astype(BF16)
        parts.append(high)
        value = value - high.astype(F32)
    return jnp.concatenate(parts, axis=0)

def cat(parts, axis):
    return parts[0] if len(parts) == 1 else jnp.concatenate(parts, axis=axis)

def roll_pairs(values):
    even = iota(values.shape, 1) % 2 == 0
    return jnp.where(even, -pltpu.roll(values, values.shape[1] - 1, 1), pltpu.roll(values, 1, 1))

def attention_kernel(
    both_ref, inverse_ref, tab_ref, mixed_ref, cot_ref, w_out_ref,
    po_ref, mixes_ref, x_ref,
    oh_t_ref, oh_ref, cos_ref, sin_ref, cos_t_ref, sin_t_ref, e_ref, m_ref, agg_q_ref, agg_k_ref, cot_sum_ref,
    place_ref=None,
):
    shards, twice_windows, rows = both_ref.shape
    windows = twice_windows // 2
    vocab = cot_sum_ref.shape[0]
    pairs = inverse_ref.shape[0]
    place = lax.axis_index("seq") if place_ref is None else place_ref[0]
    quarter = LANES // GROUP
    per_step = GROUP * PAIR
    steps = HEADS // per_step
    some = per_step * vocab

    for ref in (e_ref, m_ref, agg_q_ref, agg_k_ref, cot_sum_ref):
        ref[...] = jnp.zeros_like(ref)

    def run(part):
        first = part * rows
        span = first + rows

        def window_step(window, _):
            row = lambda at: cat([both_ref[s, pl.ds(at, 1), :] for s in range(part + 1)], 1)
            oh_t = (iota((vocab, span), 0) == row(window)).astype(F32).astype(BF16)
            oh_t_ref[:, :span] = oh_t
            tiles = (iota((vocab, LANES), 1) % vocab == iota((vocab, LANES), 0)).astype(F32).astype(BF16)
            oh_ref[:span, :] = t_dot(oh_t, tiles).astype(BF16)
            angles = inverse_ref[...] * row(window + windows).astype(F32)
            spread = (iota((3 * pairs, LANES), 0) % pairs == iota((3 * pairs, LANES), 1) % ROT // 2).astype(F32).astype(BF16)
            spread_t = (iota((LANES, 3 * pairs), 1) % pairs == iota((LANES, 3 * pairs), 0) % ROT // 2).astype(F32).astype(BF16)
            for value, ref, ref_t in ((jnp.cos(angles), cos_ref, cos_t_ref), (jnp.sin(angles), sin_ref, sin_t_ref)):
                terms = three_terms(value)
                ref[:span, :] = t_dot(terms, spread)
                ref_t[...] = dot(spread_t, terms[:, first:])
            cot = cot_ref[window]
            cot_sum_ref[...] += dot(oh_t[:, first:], cot)

            def group_step(step, _):
                lane_head = iota((rows, 2 * LANES), 1) % LANES // quarter
                halves = range(PAIR)
                owns, keys, keys_t = [], [], []
                cos, sin = cos_ref[:span, :], sin_ref[:span, :]
                for half in halves:
                    table = tab_ref[step * PAIR + half]
                    oh = oh_ref[first:span, :]
                    raw = dot(oh, table[:, : 3 * LANES])
                    turned = raw[:, :LANES] * cos[first:, :] + raw[:, 2 * LANES :] * sin[first:, :]
                    query = jnp.concatenate([turned, raw[:, LANES : 2 * LANES]], axis=1).astype(BF16)
                    owns.append(jnp.concatenate(
                        [jnp.where(lane_head == head, query, jnp.zeros_like(query)) for head in range(GROUP)], axis=0))
                    raw = dot(oh_ref[:span, :], table[:, 3 * LANES :])
                    turned = (raw[:, :LANES] * cos + raw[:, 2 * LANES :] * sin).astype(BF16)
                    keys.append(jnp.concatenate([turned, raw[:, LANES : 2 * LANES].astype(BF16)], axis=1))
                    keys_t.append(turned.T)
                mixed = mixed_ref[pl.ds(pl.multiple_of(step * some, some), some), :]
                grad = dot_t(mixed, cot_ref[window])
                lanes_of = lambda v, half: jnp.concatenate(
                    [v[(half * GROUP + h) * vocab : (half * GROUP + h + 1) * vocab, :] for h in range(GROUP)], axis=1)
                rows_of = lambda v: [v[:, h * rows : (h + 1) * rows] for h in range(GROUP)]
                kept = iota((rows, GROUP * rows), 0) <= iota((rows, GROUP * rows), 1) % rows
                weights = []
                for half in halves:
                    scores = dot_t(keys[half], owns[half]) * (HEAD_DIM**-0.5 * LOG2E)
                    last = jnp.where(kept, scores[first:, :], -1e30)
                    scores = jnp.concatenate([scores[:first, :], last], axis=0) if first else last
                    weights.append(jnp.exp2(scores - jnp.max(scores, axis=0, keepdims=True)))
                shares, terms, centered = [], [], []
                for half in halves:
                    summed = dot(oh_t_ref[:, :span], weights[half].astype(BF16))
                    inverse = 1.0 / jnp.sum(summed, axis=0, keepdims=True)
                    share = summed * inverse
                    own_grad = lanes_of(grad, half)
                    off = own_grad - jnp.sum(share * own_grad, axis=0, keepdims=True)
                    shares += rows_of(share)
                    terms += rows_of(share * off)
                    centered.append((off * inverse).astype(BF16))
                d_scores = [(weights[half] * dot(oh_ref[:span, :vocab], centered[half])).astype(BF16) for half in halves]
                shares = jnp.concatenate(shares, axis=0).astype(BF16)
                at = pl.ds(pl.multiple_of(step * some, some), some)
                po_ref[window, at, :] = shares
                e_ref[at, :] += dot(shares, cot_ref[window])
                m_ref[at, :] += dot(jnp.concatenate(terms, axis=0).astype(BF16), oh_ref[first:span, :])
                d_query, d_keys = [], []
                for half in halves:
                    for head in range(GROUP):
                        d_query.append(dot(
                            keys_t[half][head * quarter : (head + 1) * quarter, :],
                            d_scores[half][:, head * rows : (head + 1) * rows]))
                    d_keys.append(dot(d_scores[half], owns[half][:, :LANES]))
                parts = [(d * turn).astype(BF16) for turn in (cos, sin) for d in d_keys]
                agg_k_ref[step] += dot(oh_t_ref[:, :span], jnp.concatenate(parts, axis=1))
                d_query = [jnp.concatenate(d_query[h : h + GROUP], axis=0) for h in range(0, per_step, GROUP)]
                parts = [(d * ref[...]).astype(BF16) for ref in (cos_t_ref, sin_t_ref) for d in d_query]
                agg_q_ref[step] += dot_t(oh_t_ref[:, first:span], jnp.concatenate(parts, axis=0))
                return 0

            lax.fori_loop(0, steps, group_step, 0)
            return 0

        lax.fori_loop(0, windows, window_step, 0)

    for part in range(shards):
        pl.when(place == part)(partial(run, part))

    width = cot_sum_ref.shape[1]
    x_ref[:, :width] = cot_sum_ref[...]
    lane_block = iota((vocab, LANES), 1) // quarter
    for group in range(HEADS // GROUP):
        step, half = divmod(group, PAIR)
        table = tab_ref[group, :vocab, :]
        query_plain = table[:, LANES : 2 * LANES]
        key_plain = table[:, 4 * LANES : 5 * LANES]
        mass = m_ref[group * GROUP * vocab : (group + 1) * GROUP * vocab, :].astype(BF16)
        block = iota((GROUP * vocab, LANES), 0) // vocab == iota((GROUP * vocab, LANES), 1) // quarter
        stacked = jnp.concatenate([key_plain] * GROUP, axis=0)
        plain_q = t_dot(mass, jnp.where(block, stacked, jnp.zeros_like(stacked)))[:vocab, :]
        mixed_k = dot(mass[:, :vocab], query_plain)
        plain_k = sum(
            jnp.where(lane_block == h, mixed_k[h * vocab : (h + 1) * vocab, :], 0.0) for h in range(GROUP))
        for at, ref, plain in ((1, agg_q_ref, plain_q), (2, agg_k_ref, plain_k)):
            cosine = ref[step, :, half * LANES : (half + 1) * LANES]
            sine = ref[step, :, (PAIR + half) * LANES : (PAIR + half + 1) * LANES]
            turned = cosine - roll_pairs(sine)
            pieces = []
            for h in range(GROUP):
                pieces += [turned[:, h * quarter : (h + 1) * quarter], plain[:, h * quarter : (h + 1) * quarter]]
            x_ref[:, at * width + group * 2 * LANES : at * width + (group + 1) * 2 * LANES] = (
                jnp.concatenate(pieces, axis=1) * HEAD_DIM**-0.5)
    low = e_ref[...].astype(BF16)
    mixes_ref[...] = low
    lane_head = iota((vocab, LANES), 1) // HEAD_DIM
    for at in range(HEADS // 2):
        both = dot_t(low[2 * at * vocab : 2 * (at + 1) * vocab, :], w_out_ref[at * LANES : (at + 1) * LANES, :])
        x_ref[:, 3 * width + at * LANES : 3 * width + (at + 1) * LANES] = jnp.where(
            lane_head == 0, both[:vocab, :], both[vocab:, :])


def attention(both, inverse, tables, mixed, cotangent, w_out, place=None):
    shards, twice_windows, rows = both.shape
    windows = twice_windows // 2
    length = shards * rows
    width = cotangent.shape[2]
    vocab = mixed.shape[0] // HEADS
    steps = HEADS // (GROUP * PAIR)
    vmem = pl.BlockSpec(memory_space=pltpu.VMEM)
    operands = (both, inverse, tables, mixed, cotangent, w_out)
    specs = [vmem] * len(operands)
    kernel = attention_kernel
    if place is not None:
        operands = (place,) + operands
        specs = [pl.BlockSpec(memory_space=pltpu.SMEM)] + specs
        kernel = lambda place_ref, *refs: attention_kernel(*refs, place_ref=place_ref)
    return pl.pallas_call(
        kernel,
        in_specs=specs,
        out_specs=[vmem] * 3,
        out_shape=[
            jax.ShapeDtypeStruct((windows, HEADS * vocab, rows), BF16),
            jax.ShapeDtypeStruct((HEADS * vocab, width), BF16),
            jax.ShapeDtypeStruct((vocab, 4 * width), F32),
        ],
        scratch_shapes=[
            pltpu.VMEM((vocab, length), BF16),
            pltpu.VMEM((length, LANES), BF16),
            pltpu.VMEM((length, LANES), F32),
            pltpu.VMEM((length, LANES), F32),
            pltpu.VMEM((LANES, rows), F32),
            pltpu.VMEM((LANES, rows), F32),
            pltpu.VMEM((HEADS * vocab, width), F32),
            pltpu.VMEM((HEADS * vocab, LANES), F32),
            pltpu.VMEM((steps, vocab, 2 * PAIR * LANES), F32),
            pltpu.VMEM((steps, vocab, 2 * PAIR * LANES), F32),
            pltpu.VMEM((vocab, width), F32),
        ],
        compiler_params=pltpu.CompilerParams(vmem_limit_bytes=56 * 1024 * 1024),
    )(*operands)

def peer(axis, index):
    return {axis: index}


def greet(axes):
    barrier = pltpu.get_barrier_semaphore()
    count = 0
    for axis in axes:
        size = lax.axis_size(axis)
        me = lax.axis_index(axis)
        for step in range(1, size):
            pl.semaphore_signal(
                barrier, inc=1, device_id={axis: lax.rem(me + step, size)}, device_id_type=pl.DeviceIdType.MESH
            )
        count += size - 1
    pl.semaphore_wait(barrier, count)


def layer_norm_rows(embed_ref):
    inputs = embed_ref[...].astype(F32)
    center = inputs - jnp.mean(inputs, axis=1, keepdims=True)
    spread = jnp.mean(center * center, axis=1, keepdims=True)
    rstd = lax.rsqrt(spread + ln_epsilon)
    return inputs, center * rstd, rstd


def table_kernel(
    ids_ref, positions_ref, embed_ref, gain_ref, shift_ref, w_qkv_ref, w_out_ref,
    both_ref, normed_ref, values_ref, tab_ref, mixed_ref,
    w_qkv, w_out, weight_sem, send_sem, recv_sem,
):
    windows = ids_ref.shape[0]
    vocab, width = embed_ref.shape
    place = lax.axis_index("seq")
    shards = lax.axis_size("seq")
    quarter = LANES // GROUP
    loads = [
        pltpu.make_async_copy(w_qkv_ref.at[:, pl.ds(at * width, width)], w_qkv.at[at], weight_sem.at[at])
        for at in range(3)
    ]
    loads.append(pltpu.make_async_copy(w_out_ref, w_out, weight_sem.at[3]))
    for load in loads:
        load.start()
    both_ref[place, :windows, :] = ids_ref[...]
    both_ref[place, windows:, :] = positions_ref[...]
    greet(("seq",))
    sends = []
    for step in range(1, shards):
        sends.append(pltpu.make_async_remote_copy(
            src_ref=both_ref.at[place], dst_ref=both_ref.at[place],
            send_sem=send_sem.at[step], recv_sem=recv_sem.at[step],
            device_id={"seq": lax.rem(place + step, shards)}, device_id_type=pl.DeviceIdType.MESH,
        ))
    for send in sends:
        send.start()
    _, xhat, _ = layer_norm_rows(embed_ref)
    normed = (xhat * gain_ref[...] + shift_ref[...]).astype(BF16)
    normed_ref[...] = normed
    projected = []
    for at in range(3):
        loads[at].wait()
        projected.append(dot(normed, w_qkv[at]))
    values = projected[2].astype(BF16)
    values_ref[...] = values
    fill = jnp.zeros((LANES - 3 * vocab, 6 * LANES), BF16)
    for group in range(HEADS // GROUP):
        columns = []
        for table in projected[:2]:
            heads = [table[:, (group * GROUP + h) * HEAD_DIM : (group * GROUP + h + 1) * HEAD_DIM] for h in range(GROUP)]
            turned = jnp.concatenate([h[:, :ROT] for h in heads], axis=1)
            plain = jnp.concatenate([h[:, ROT:] for h in heads], axis=1)
            columns += [turned, plain, roll_pairs(turned)]
        tab_ref[group] = jnp.concatenate([three_terms(jnp.concatenate(columns, axis=1)), fill], axis=0)
    loads[3].wait()
    lane_head = iota((vocab, LANES), 1) // HEAD_DIM
    for at in range(HEADS // 2):
        some = values[:, at * LANES : (at + 1) * LANES]
        none = jnp.zeros_like(some)
        spread = jnp.concatenate([jnp.where(lane_head == 0, some, none), jnp.where(lane_head == 1, some, none)], axis=0)
        mixed_ref[2 * at * vocab : 2 * (at + 1) * vocab, :] = dot(
            spread, w_out[at * LANES : (at + 1) * LANES, :]).astype(BF16)
    for send in sends:
        send.wait()


def make_tables(ids, positions, embed, gain, shift, w_qkv, w_out):
    windows, rows = ids.shape
    vocab, width = embed.shape
    shards = lax.axis_size("seq")
    vmem = pl.BlockSpec(memory_space=pltpu.VMEM)
    hbm = pl.BlockSpec(memory_space=pl.ANY)
    return pl.pallas_call(
        table_kernel,
        in_specs=[vmem] * 5 + [hbm] * 2,
        out_specs=[vmem] * 5,
        out_shape=[
            jax.ShapeDtypeStruct((shards, 2 * windows, rows), jnp.int32),
            jax.ShapeDtypeStruct((vocab, width), BF16),
            jax.ShapeDtypeStruct((vocab, width), BF16),
            jax.ShapeDtypeStruct((HEADS // GROUP, LANES, 6 * LANES), BF16),
            jax.ShapeDtypeStruct((HEADS * vocab, width), BF16),
        ],
        scratch_shapes=[
            pltpu.VMEM((3, width, width), BF16),
            pltpu.VMEM((width, width), BF16),
            pltpu.SemaphoreType.DMA((4,)),
            pltpu.SemaphoreType.DMA((shards,)),
            pltpu.SemaphoreType.DMA((shards,)),
        ],
        compiler_params=pltpu.CompilerParams(
            vmem_limit_bytes=24 * 1024 * 1024, collective_id=1, has_side_effects=True
        ),
    )(ids, positions, embed, gain[None, :], shift[None, :], w_qkv, w_out)


def gelu_and_slope(u):
    c = 0.7978845608028654
    t = jnp.tanh(c * (u + 0.044715 * u * u * u))
    return 0.5 * u * (1.0 + t), 0.5 * (1.0 + t) + 0.5 * u * (1.0 - t * t) * c * (1.0 + 3 * 0.044715 * u * u)


def two_terms(value):
    high = value.astype(BF16)
    return jnp.concatenate([high, (value - high.astype(F32)).astype(BF16)], axis=0)


def to_all(axis, source, target, send_sem, recv_sem):
    size = lax.axis_size(axis)
    me = lax.axis_index(axis)
    copies = []
    for step in range(1, size):
        other = lax.rem(me + step, size)
        copies.append(pltpu.make_async_remote_copy(
            src_ref=source(other), dst_ref=target(step), send_sem=send_sem.at[step], recv_sem=recv_sem.at[step],
            device_id={axis: other}, device_id_type=pl.DeviceIdType.MESH,
        ))
    return copies


def final_kernel(
    x_ref, mixes_ref, po_ref, both_ref, normed_ref, values_ref, mixed_ref, embed_ref, gain_ref, shift_ref,
    b_up_ref, b_down_ref, w_up_ref, w_down_ref, w_qkv_ref,
    output_ref, embed_grad_ref, gain_grad_ref, shift_grad_ref, qkv_grad_ref, out_grad_ref, up_grad_ref,
    up_bias_grad_ref, down_grad_ref, down_bias_grad_ref,
    w_up, w_down, w_qkv, up_tab, act_tab, d_up_tab,
    x_own, x_low, x_in, x_part, x_in2, x_all, e_in, e_part, e_in2,
    weight_sem, x1_send, x1_recv, x2_send, x2_recv, x3_send, x3_recv, e1_send, e1_recv, e2_send, e2_recv,
):
    vocab, width = embed_ref.shape
    blocks, _, some = w_up.shape
    hidden = blocks * some
    windows, _, rows = po_ref.shape
    dp, seq = lax.axis_size("dp"), lax.axis_size("seq")
    column, place = lax.axis_index("dp"), lax.axis_index("seq")
    index = column * seq + place
    d_rows, f_rows = width // (dp * seq), hidden // (dp * seq)
    chunk = x_low.shape[2]

    loads = []
    for at in range(blocks):
        loads.append((
            pltpu.make_async_copy(w_up_ref.at[:, pl.ds(at * some, some)], w_up.at[at], weight_sem.at[0, at]),
            pltpu.make_async_copy(w_down_ref.at[pl.ds(at * some, some), :], w_down.at[at], weight_sem.at[1, at]),
        ))
    for pair in loads:
        for load in pair:
            load.start()
    qkv_load = pltpu.make_async_copy(w_qkv_ref, w_qkv, weight_sem.at[2, 0])
    qkv_load.start()
    for at in range(dp):
        piece = x_ref[:, at * chunk : (at + 1) * chunk]
        x_own[at] = piece
        x_low[at] = piece.astype(BF16)
    greet(("dp", "seq"))
    x1 = to_all("dp", lambda other: x_low.at[other], lambda step: x_in.at[step], x1_send, x1_recv)
    for copy in x1:
        copy.start()
    e_rows = e_part.shape[0]
    first_head = lambda other: other * HEADS // dp
    e_slice = lambda other: pl.ds(pl.multiple_of(first_head(other) * vocab, vocab), e_rows)
    e1 = to_all("dp", lambda other: mixes_ref.at[e_slice(other), :], lambda step: e_in.at[step], e1_send, e1_recv)
    for copy in e1:
        copy.start()

    normed = normed_ref[...]
    mlp = jnp.zeros((vocab, width), F32)
    for at in range(blocks):
        loads[at][0].wait()
        up = dot(normed, w_up[at]) + b_up_ref[:, at * some : (at + 1) * some]
        up_tab[at] = up
        act = gelu_and_slope(up)[0].astype(BF16)
        act_tab[:, at * some : (at + 1) * some] = act
        loads[at][1].wait()
        mlp += dot(act, w_down[at])

    for copy in x1:
        copy.wait_recv()
    total = x_own[column]
    for step in range(1, dp):
        total += x_in[step].astype(F32)
    x_part[...] = total.astype(BF16)
    x2 = to_all("seq", lambda other: x_part, lambda step: x_in2.at[step], x2_send, x2_recv)
    for copy in x2:
        copy.start()

    inputs, xhat, rstd = layer_norm_rows(embed_ref)
    base = two_terms(inputs + mlp + b_down_ref[...])
    right = jnp.concatenate([mixed_ref[...], base], axis=0)
    for window in range(windows):
        ids = both_ref[place, window : window + 1, :]
        oh_t = (iota((vocab, rows), 0) == ids).astype(F32).astype(BF16)
        output_ref[window] = t_dot(jnp.concatenate([po_ref[window], oh_t, oh_t], axis=0), right).astype(BF16)

    for copy in x2:
        copy.wait_recv()
    for step in range(1, seq):
        total += x_in2[step].astype(F32)
    x_all[column] = total.astype(BF16)
    x3 = to_all("dp", lambda other: x_all.at[column], lambda step: x_all.at[column], x3_send, x3_recv)
    for copy in x3:
        copy.start()

    for copy in e1:
        copy.wait_recv()
    mixes = mixes_ref[e_slice(column), :].astype(F32)
    for step in range(1, dp):
        mixes += e_in[step].astype(F32)
    e_part[...] = mixes.astype(BF16)
    own_rows = e_in2.shape[1]
    head_of = lambda other: (column * seq + other) * d_rows // HEAD_DIM - first_head(column)
    own_slice = lambda other: pl.ds(pl.multiple_of(head_of(other) * vocab, vocab), own_rows)
    e2 = to_all("seq", lambda other: e_part.at[own_slice(other), :], lambda step: e_in2.at[step], e2_send, e2_recv)
    for copy in e2:
        copy.start()

    for copy in x3:
        copy.wait_recv()
    sums = jnp.concatenate([x_all[at] for at in range(dp)], axis=1)
    cot_sum = sums[:, :width]
    d_normed = jnp.zeros((2 * vocab, width), F32)
    for at in range(blocks):
        slope = gelu_and_slope(up_tab[at])[1]
        d_up = slope * dot_t(cot_sum, w_down[at])
        terms = two_terms(d_up)
        d_up_tab[:, at * some : (at + 1) * some] = terms
        d_normed += dot_t(terms, w_up[at])
    d_normed = d_normed[:vocab, :] + d_normed[vocab:, :]
    qkv_load.wait()
    d_normed += dot_t(sums[:, width:], w_qkv[...])

    pick = (iota((d_rows, width), 1) == iota((d_rows, width), 0) + index * d_rows).astype(F32).astype(BF16)
    pick_f = (iota((f_rows, hidden), 1) == iota((f_rows, hidden), 0) + index * f_rows).astype(F32).astype(BF16)
    normed_own = dot_t(pick, normed).astype(BF16)
    act_own = dot_t(pick_f, act_tab[...]).astype(BF16)
    qkv_grad_ref[...] = dot(normed_own, sums[:, width:])
    up_grad_ref[...] = dot(jnp.concatenate([normed_own, normed_own], axis=1), d_up_tab[...])
    down_grad_ref[...] = dot(act_own, cot_sum)
    d_up_sum = jnp.sum(d_up_tab[...].astype(F32), axis=0, keepdims=True)
    up_bias_grad_ref[...] = jnp.sum(dot_t(three_terms(jnp.concatenate([d_up_sum] * 16, axis=0)), pick_f), axis=0, keepdims=True) / 16.0
    cot_f32 = cot_sum.astype(F32)
    scaled = d_normed * gain_ref[...]
    d_input = cot_f32 + rstd * (
        scaled
        - jnp.mean(scaled, axis=1, keepdims=True)
        - xhat * jnp.mean(scaled * xhat, axis=1, keepdims=True)
    )
    wide = dot_t(pick, three_terms(d_input))
    embed_grad_ref[...] = wide[:, :vocab] + wide[:, vocab : 2 * vocab] + wide[:, 2 * vocab :]
    for ref, value in ((gain_grad_ref, d_normed * xhat), (shift_grad_ref, d_normed), (down_bias_grad_ref, cot_f32)):
        ref[...] = jnp.sum(dot_t(three_terms(value), pick), axis=0, keepdims=True)

    for copy in e2:
        copy.wait_recv()
    own = e_part[own_slice(place), :].astype(F32)
    for step in range(1, seq):
        own += e_in2[step].astype(F32)
    values_own = dot_t(pick, values_ref[...]).astype(BF16)
    row_head = iota((d_rows, vocab), 0) // HEAD_DIM
    left = jnp.concatenate(
        [jnp.where(row_head == h, values_own, jnp.zeros_like(values_own)) for h in range(own_rows // vocab)], axis=1)
    out_grad_ref[...] = dot(left, own.astype(BF16))
    for copies in (x1, x2, x3, e1, e2):
        for copy in copies:
            copy.wait_send()


def finish(x, mixes, po, both, normed, values, mixed, embed, gain, shift, b_up, b_down, w_up, w_down, w_qkv):
    vocab, width = embed.shape
    hidden = w_up.shape[1]
    windows, _, rows = po.shape
    dp, seq = lax.axis_size("dp"), lax.axis_size("seq")
    d_rows, f_rows = width // (dp * seq), hidden // (dp * seq)
    some = 512
    blocks = hidden // some
    chunk = x.shape[1] // dp
    e_rows = max(1, HEADS // dp) * vocab
    own_rows = max(1, d_rows // HEAD_DIM) * vocab
    vmem = pl.BlockSpec(memory_space=pltpu.VMEM)
    hbm = pl.BlockSpec(memory_space=pl.ANY)
    shape = jax.ShapeDtypeStruct
    return pl.pallas_call(
        final_kernel,
        in_specs=[vmem] * 12 + [hbm] * 3,
        out_specs=[vmem] * 10,
        out_shape=[
            shape((windows, rows, width), BF16),
            shape((d_rows, vocab), F32),
            shape((1, d_rows), F32),
            shape((1, d_rows), F32),
            shape((d_rows, 3 * width), F32),
            shape((d_rows, width), F32),
            shape((d_rows, hidden), F32),
            shape((1, f_rows), F32),
            shape((f_rows, width), F32),
            shape((1, d_rows), F32),
        ],
        scratch_shapes=[
            pltpu.VMEM((blocks, width, some), BF16),
            pltpu.VMEM((blocks, some, width), BF16),
            pltpu.VMEM((width, 3 * width), BF16),
            pltpu.VMEM((blocks, vocab, some), F32),
            pltpu.VMEM((vocab, hidden), BF16),
            pltpu.VMEM((2 * vocab, hidden), BF16),
            pltpu.VMEM((dp, vocab, chunk), F32),
            pltpu.VMEM((dp, vocab, chunk), BF16),
            pltpu.VMEM((dp, vocab, chunk), BF16),
            pltpu.VMEM((vocab, chunk), BF16),
            pltpu.VMEM((seq, vocab, chunk), BF16),
            pltpu.VMEM((dp, vocab, chunk), BF16),
            pltpu.VMEM((dp, e_rows, width), BF16),
            pltpu.VMEM((e_rows, width), BF16),
            pltpu.VMEM((seq, own_rows, width), BF16),
            pltpu.SemaphoreType.DMA((3, blocks)),
        ] + [pltpu.SemaphoreType.DMA((size,)) for size in (dp, dp, seq, seq, dp, dp, dp, dp, seq, seq)],
        compiler_params=pltpu.CompilerParams(
            vmem_limit_bytes=56 * 1024 * 1024, collective_id=2, has_side_effects=True
        ),
    )(x, mixes, po, both, normed, values, mixed, embed, gain[None, :], shift[None, :], b_up[None, :],
      b_down[None, :], w_up, w_down, w_qkv)


def per_device(
    token_ids, positions, embed, ln_gain, ln_shift, w_qkv, w_out, w_up, b_up, w_down, b_down, cotangent
):
    both, normed, values, tables, mixed = make_tables(
        token_ids, positions, embed, ln_gain, ln_shift, w_qkv, w_out)
    pair = jnp.arange(ROT // 2)
    inverse = (10000.0 ** (-2.0 * pair.astype(F32) / ROT))[:, None]
    po, mixes, x = attention(both, inverse, tables, mixed, cotangent, w_out)
    outs = finish(x, mixes, po, both, normed, values, mixed, embed, ln_gain, ln_shift, b_up, b_down, w_up, w_down, w_qkv)
    flat = lambda v: v.reshape(-1)
    return (
        outs[0], outs[1], flat(outs[2]), flat(outs[3]), outs[4], outs[5], outs[6], flat(outs[7]), outs[8], flat(outs[9]),
    )


def solution(mesh):
    in_specs = (P("dp", "seq"), P("dp", "seq")) + (P(),) * 9 + (P("dp", "seq", None),)
    both = ("dp", "seq")
    out_specs = (
        P("dp", "seq", None),
        P(both, None),
        P(both),
        P(both),
        P(both, None),
        P(both, None),
        P(both, None),
        P(both),
        P(both, None),
        P(both),
    )
    return jax.shard_map(per_device, mesh=mesh, in_specs=in_specs, out_specs=out_specs, check_vma=False)
```

```python
from functools import partial

import jax
import jax.numpy as jnp
from jax import lax
from jax.experimental import pallas as pl
from jax.experimental.pallas import tpu as pltpu
from jax.sharding import PartitionSpec as P

HEADS = 16
HEAD_DIM = 64
ROT = 32
GROUP = 4
PHASES = 2
EACH = HEADS // PHASES
HALVES = EACH // GROUP
LANES = 128
ln_epsilon = 1e-05
LOG2E = 1.4426950408889634
F32 = jnp.float32
BF16 = jnp.bfloat16
MESH = pl.DeviceIdType.MESH


def dot(a, b):
    return lax.dot_general(a, b, (((1,), (0,)), ((), ())), preferred_element_type=F32)


def dot_t(a, b):
    return lax.dot_general(a, b, (((1,), (1,)), ((), ())), preferred_element_type=F32)


def t_dot(a, b):
    return lax.dot_general(a, b, (((0,), (0,)), ((), ())), preferred_element_type=F32)


def iota(shape, axis):
    return lax.broadcasted_iota(jnp.int32, shape, axis)


def ones_where(mask):
    return mask.astype(F32).astype(BF16)


def terms_of(value, count):
    parts = []
    for _ in range(count):
        high = value.astype(BF16)
        parts.append(high)
        value = value - high.astype(F32)
    return jnp.concatenate(parts, axis=0)


def roll_pairs(values):
    even = iota(values.shape, 1) % 2 == 0
    return jnp.where(even, -pltpu.roll(values, values.shape[1] - 1, 1), pltpu.roll(values, 1, 1))


def gelu_and_slope(u):
    c = 0.7978845608028654
    t = jnp.tanh(c * (u + 0.044715 * u * u * u))
    return 0.5 * u * (1.0 + t), 0.5 * (1.0 + t) + 0.5 * u * (1.0 - t * t) * c * (1.0 + 3 * 0.044715 * u * u)


def greet(axes):
    barrier = pltpu.get_barrier_semaphore()
    count = 0
    for axis in axes:
        size = lax.axis_size(axis)
        me = lax.axis_index(axis)
        for step in range(1, size):
            pl.semaphore_signal(barrier, inc=1, device_id={axis: lax.rem(me + step, size)}, device_id_type=MESH)
        count += size - 1
    pl.semaphore_wait(barrier, count)


def to_all(axis, source, target, send_sem, recv_sem):
    size = lax.axis_size(axis)
    me = lax.axis_index(axis)
    copies = []
    for step in range(1, size):
        other = lax.rem(me + step, size)
        copies.append(pltpu.make_async_remote_copy(
            src_ref=source(other), dst_ref=target(step), send_sem=send_sem.at[step], recv_sem=recv_sem.at[step],
            device_id={axis: other}, device_id_type=MESH,
        ))
    return copies


def start_all(copies):
    for copy in copies:
        copy.start()


def arrived(copies):
    for copy in copies:
        copy.wait_recv()


class Total:
    def __init__(self, own, low, first, part, second, whole, sems):
        self.own, self.low, self.first, self.part = own, low, first, part
        self.second, self.whole, self.sems = second, whole, sems
        self.columns = low.shape[2]
        self.column = lax.axis_index("dp")

    def send(self, at, piece):
        self.own[at] = piece
        self.low[at] = piece.astype(BF16)

    def step1(self):
        self.one = to_all("dp", lambda other: self.low.at[other], lambda step: self.first.at[step], *self.sems[0:2])
        start_all(self.one)

    def step2(self):
        arrived(self.one)
        value = self.own[self.column]
        for step in range(1, lax.axis_size("dp")):
            value += self.first[step].astype(F32)
        self.own[self.column] = value
        self.part[...] = value.astype(BF16)
        self.two = to_all("seq", lambda other: self.part, lambda step: self.second.at[step], *self.sems[2:4])
        start_all(self.two)

    def step3(self):
        arrived(self.two)
        value = self.own[self.column]
        for step in range(1, lax.axis_size("seq")):
            value += self.second[step].astype(F32)
        self.whole[self.column] = value.astype(BF16)
        self.three = to_all(
            "dp", lambda other: self.whole.at[self.column], lambda step: self.whole.at[self.column], *self.sems[4:6])
        start_all(self.three)

    def result(self):
        arrived(self.three)
        return jnp.concatenate([self.whole[at] for at in range(self.whole.shape[0])], axis=1)

    def end(self):
        for copies in (self.one, self.two, self.three):
            for copy in copies:
                copy.wait_send()


def total_scratch(dp, seq, rows, columns):
    return [
        pltpu.VMEM((dp, rows, columns), F32),
        pltpu.VMEM((dp, rows, columns), BF16),
        pltpu.VMEM((dp, rows, columns), BF16),
        pltpu.VMEM((rows, columns), BF16),
        pltpu.VMEM((seq, rows, columns), BF16),
        pltpu.VMEM((dp, rows, columns), BF16),
    ] + [pltpu.SemaphoreType.DMA((size,)) for size in (dp, dp, seq, seq, dp, dp)]


def layer_norm_rows(embed):
    inputs = embed.astype(F32)
    center = inputs - jnp.mean(inputs, axis=1, keepdims=True)
    spread = jnp.mean(center * center, axis=1, keepdims=True)
    rstd = lax.rsqrt(spread + ln_epsilon)
    return inputs, center * rstd, rstd


def head_at(slot):
    return slot % EACH * PHASES + slot // EACH


def gifts(shards, windows):
    counts = []
    for place in range(shards):
        mirror = shards - 1 - place
        spare = PHASES * windows * (place - mirror) / (2.0 * (place + 2))
        counts.append(min(windows, max(0, int(spare + 0.5))))
    return counts


def main_kernel(
    ids_hbm, positions_hbm, embed_hbm, gain_hbm, shift_hbm, b_up_hbm, b_down_hbm, cot_hbm, w_qkv_hbm, w_out_hbm,
    w_up_hbm, w_down_hbm,
    po_ref, normed_ref, values_ref, mixed_ref, base_ref, sums_ref, cot_sum_ref, act_tab, d_up_tab, d_normed_ref, e_own_ref,
    both, embed_ref, gain_ref, shift_ref, b_up_ref, b_down_ref, cot_ref, w_qkv, w_out, w_up, w_down,
    tab_ref, grad_ref, po_in, oh_t_ref, oh_ref, cos_ref, sin_ref, turn_ref, low_ref, m_ref, agg_q_ref, agg_k_ref, up_tab,
    e_in, e_part, e_in2,
    load_sem, weight_sem, seq_send, seq_recv, gift_send, gift_recv, back_send, back_recv, e1_send, e1_recv, e2_send, e2_recv,
    *totals,
):
    shards, twice_windows, rows = both.shape
    windows = twice_windows // 2
    vocab, width = embed_ref.shape
    length = shards * rows
    blocks, _, some = w_up.shape
    dp = lax.axis_size("dp")
    column, place = lax.axis_index("dp"), lax.axis_index("seq")
    mirror = shards - 1 - place
    pairs = ROT // 2
    quarter = LANES // GROUP
    per_phase = EACH * vocab
    give_of = gifts(shards, windows)
    most = max(give_of)
    pick_count = lambda where: sum(
        jnp.where(where == at, jnp.int32(count), jnp.int32(0)) for at, count in enumerate(give_of) if count)
    give, take = pick_count(place), pick_count(mirror)

    small = [
        pltpu.make_async_copy(source, target, load_sem.at[at])
        for at, (source, target) in enumerate((
            (ids_hbm, both.at[place, pl.ds(0, windows), :]),
            (positions_hbm, both.at[place, pl.ds(windows, windows), :]),
            (embed_hbm, embed_ref), (gain_hbm, gain_ref), (shift_hbm, shift_ref), (b_up_hbm, b_up_ref),
            (b_down_hbm, b_down_ref)))
    ]
    qkv_loads = [
        pltpu.make_async_copy(w_qkv_hbm.at[:, pl.ds(at * width, width)], w_qkv.at[at], load_sem.at[8 + at])
        for at in range(3)
    ]
    out_load = pltpu.make_async_copy(w_out_hbm, w_out, load_sem.at[11])
    cot_load = pltpu.make_async_copy(cot_hbm, cot_ref, load_sem.at[12])
    mlp_loads = [(
        pltpu.make_async_copy(w_up_hbm.at[:, pl.ds(at * some, some)], w_up.at[at], weight_sem.at[0, at]),
        pltpu.make_async_copy(w_down_hbm.at[pl.ds(at * some, some), :], w_down.at[at], weight_sem.at[1, at]),
    ) for at in range(blocks)]
    start_all(small + qkv_loads + [out_load, cot_load])
    for pair in mlp_loads:
        start_all(pair)
    for copy in small:
        copy.wait()
    greet(("dp", "seq"))
    exchange = to_all("seq", lambda other: both.at[place], lambda step: both.at[place], seq_send, seq_recv)
    start_all(exchange)

    _, xhat, _ = layer_norm_rows(embed_ref[...])
    normed = (xhat * gain_ref[...] + shift_ref[...]).astype(BF16)
    normed_ref[...] = normed
    projected = []
    for at in range(3):
        qkv_loads[at].wait()
        projected.append(dot(normed, w_qkv[at]))
    values = projected[2].astype(BF16)
    values_ref[...] = values
    fill = jnp.zeros((LANES - 3 * vocab, 6 * LANES), BF16)
    for group in range(HEADS // GROUP):
        columns = []
        for table in projected[:2]:
            heads = [head_at(group * GROUP + h) * HEAD_DIM for h in range(GROUP)]
            turned = jnp.concatenate([table[:, h : h + ROT] for h in heads], axis=1)
            plain = jnp.concatenate([table[:, h + ROT : h + HEAD_DIM] for h in heads], axis=1)
            columns += [turned, plain, roll_pairs(turned)]
        tab_ref[group] = jnp.concatenate([terms_of(jnp.concatenate(columns, axis=1), 3), fill], axis=0)
    out_load.wait()
    lane_head = iota((vocab, LANES), 1) // HEAD_DIM
    for at in range(EACH):
        part = values[:, at * LANES : (at + 1) * LANES]
        none = jnp.zeros_like(part)
        stacked = jnp.concatenate([jnp.where(lane_head == h, part, none) for h in range(PHASES)], axis=0)
        mixed = dot(stacked, w_out[at * LANES : (at + 1) * LANES, :]).astype(BF16)
        for h in range(PHASES):
            mixed_ref[(h * EACH + at) * vocab : (h * EACH + at + 1) * vocab, :] = mixed[h * vocab : (h + 1) * vocab, :]
    cot_load.wait()
    give_copy = lambda k: pltpu.make_async_remote_copy(
        src_ref=grad_ref.at[k], dst_ref=grad_ref.at[windows + k], send_sem=gift_send.at[k], recv_sem=gift_recv.at[k],
        device_id={"seq": mirror}, device_id_type=MESH)
    back_copy = lambda k: pltpu.make_async_remote_copy(
        src_ref=po_ref.at[windows + k, pl.ds(0, per_phase), :], dst_ref=po_in.at[k], send_sem=back_send.at[k],
        recv_sem=back_recv.at[k], device_id={"seq": mirror}, device_id_type=MESH)
    for window in range(windows):
        grad_ref[window] = dot_t(mixed_ref[:per_phase, :], cot_ref[window]).astype(BF16)
        if window < most:
            @pl.when(window < give)
            def _(window=window):
                give_copy(window).start()

    arrived(exchange)
    inverse = sum(
        jnp.where(iota((pairs, 1), 0) == p, F32(10000.0 ** (-2.0 * p / ROT)), 0.0) for p in range(pairs))
    tiles = ones_where(iota((vocab, LANES), 1) % vocab == iota((vocab, LANES), 0))
    spread = ones_where(iota((3 * pairs, LANES), 0) % pairs == iota((3 * pairs, LANES), 1) % ROT // 2)
    spread_t = ones_where(iota((LANES, 3 * pairs), 1) % pairs == iota((LANES, 3 * pairs), 0) % ROT // 2)
    cot_total = Total(*totals[:6], totals[6:12])
    sum_total = Total(*totals[12:18], totals[18:24])
    cot_sum = jnp.zeros((vocab, width), F32)
    for window in range(windows):
        row = lambda at: jnp.concatenate([both[s, at : at + 1, :] for s in range(shards)], axis=1)
        oh_t = ones_where(iota((vocab, length), 0) == row(window))
        oh_t_ref[window] = oh_t
        oh_ref[window] = t_dot(oh_t, tiles).astype(BF16)
        angles = inverse * row(window + windows).astype(F32)
        for at, (value, ref) in enumerate(((jnp.cos(angles), cos_ref), (jnp.sin(angles), sin_ref))):
            terms = terms_of(value, 3)
            turn_ref[at, window] = terms
            ref[window] = t_dot(terms, spread)
        own_t = ones_where(iota((vocab, rows), 0) == both[place, window : window + 1, :])
        cot_sum += dot(own_t, cot_ref[window])
    for at in range(dp):
        cot_total.send(at, cot_sum[:, at * cot_total.columns : (at + 1) * cot_total.columns])
    cot_total.step1()
    for ref in (m_ref, agg_q_ref, agg_k_ref):
        ref[...] = jnp.zeros_like(ref)

    def item(part, phase, window, slot):
        first = part * rows
        span = first + rows
        lane_head = iota((rows, 2 * LANES), 1) % LANES // quarter
        halves = range(HALVES)
        owns, keys, keys_t = [], [], []
        cos, sin = cos_ref[window, :span, :], sin_ref[window, :span, :]
        for half in halves:
            table = tab_ref[phase * HALVES + half]
            raw = dot(oh_ref[window, first:span, :], table[:, : 3 * LANES])
            turned = raw[:, :LANES] * cos[first:, :] + raw[:, 2 * LANES :] * sin[first:, :]
            query = jnp.concatenate([turned, raw[:, LANES : 2 * LANES]], axis=1).astype(BF16)
            owns.append(jnp.concatenate(
                [jnp.where(lane_head == head, query, jnp.zeros_like(query)) for head in range(GROUP)], axis=0))
            raw = dot(oh_ref[window, :span, :], table[:, 3 * LANES :])
            turned = (raw[:, :LANES] * cos + raw[:, 2 * LANES :] * sin).astype(BF16)
            keys.append(jnp.concatenate([turned, raw[:, LANES : 2 * LANES].astype(BF16)], axis=1))
            keys_t.append(turned.T)
        grad = grad_ref[slot].astype(F32)
        lanes_of = lambda v, half: jnp.concatenate(
            [v[(half * GROUP + h) * vocab : (half * GROUP + h + 1) * vocab, :] for h in range(GROUP)], axis=1)
        rows_of = lambda v: [v[:, h * rows : (h + 1) * rows] for h in range(GROUP)]
        kept = iota((rows, GROUP * rows), 0) <= iota((rows, GROUP * rows), 1) % rows
        weights = []
        for half in halves:
            scores = dot_t(keys[half], owns[half]) * (HEAD_DIM**-0.5 * LOG2E)
            last = jnp.where(kept, scores[first:, :], -1e30)
            scores = jnp.concatenate([scores[:first, :], last], axis=0) if first else last
            weights.append(jnp.exp2(scores - jnp.max(scores, axis=0, keepdims=True)).astype(BF16))
        shares, terms, centered = [], [], []
        for half in halves:
            summed = dot(oh_t_ref[window, :, :span], weights[half])
            inverse = 1.0 / jnp.sum(summed, axis=0, keepdims=True)
            share = summed * inverse
            own_grad = lanes_of(grad, half)
            off = own_grad - jnp.sum(share * own_grad, axis=0, keepdims=True)
            shares += rows_of(share)
            terms += rows_of(share * off)
            centered.append((off * inverse).astype(BF16))
        d_scores = [
            (weights[half].astype(F32) * dot(oh_ref[window, :span, :vocab], centered[half])).astype(BF16)
            for half in halves]
        at = pl.ds(pl.multiple_of(phase * per_phase, per_phase), per_phase)
        po_ref[slot, at, :] = jnp.concatenate(shares, axis=0).astype(BF16)
        m_ref[at, :] += dot(jnp.concatenate(terms, axis=0).astype(BF16), oh_ref[window, first:span, :])
        d_query, d_keys = [], []
        for half in halves:
            for head in range(GROUP):
                d_query.append(dot(
                    keys_t[half][head * quarter : (head + 1) * quarter, :],
                    d_scores[half][:, head * rows : (head + 1) * rows]))
            d_keys.append(dot(d_scores[half], owns[half][:, :LANES]))
        parts = [(d * turn).astype(BF16) for turn in (cos, sin) for d in d_keys]
        agg_k_ref[phase] += dot(oh_t_ref[window, :, :span], jnp.concatenate(parts, axis=1))
        d_query = [jnp.concatenate(d_query[h : h + GROUP], axis=0) for h in range(0, EACH, GROUP)]
        turns = [dot(spread_t, turn_ref[at, window, :, first:span]) for at in range(2)]
        parts = [(d * turn).astype(BF16) for turn in turns for d in d_query]
        agg_q_ref[phase] += dot_t(oh_t_ref[window, :, first:span], jnp.concatenate(parts, axis=0))

    def items(phase, lower, upper, taken):
        own = upper - lower

        def step(at, _):
            mine = jnp.where(at < own, jnp.int32(1), jnp.int32(0))
            window = mine * (lower + at) + (1 - mine) * (at - own)
            slot = window + (1 - mine) * windows
            whose = mine * place + (1 - mine) * mirror
            for part in range(shards):
                pl.when(whose == part)(partial(item, part, phase, window, slot))
            return 0

        lax.fori_loop(0, own + taken, step, 0)

    for k in range(most):
        @pl.when(k < take)
        def _(k=k):
            give_copy(k).wait_recv()
    items(0, give, windows, take)
    for k in range(most):
        @pl.when(k < take)
        def _(k=k):
            back_copy(k).start()

        @pl.when(k < give)
        def _(k=k):
            give_copy(k).wait_send()
    cot_total.step2()
    for window in range(windows):
        grad_ref[window] = dot_t(mixed_ref[per_phase:, :], cot_ref[window]).astype(BF16)

    two_sends = e_in.shape[0] > 1
    e_rows = e_part.shape[1]

    def mixes_of(phase):
        at = slice(phase * per_phase, (phase + 1) * per_phase)
        total = dot(po_ref[0, at, :], cot_ref[0])
        for window in range(1, windows):
            total += dot(po_ref[window, at, :], cot_ref[window])
        low_ref[at, :] = total.astype(BF16)

    def e_slice(phase, other):
        if two_sends:
            start = phase * per_phase + other * e_rows
        else:
            head = other * HEADS // dp
            start = (head % PHASES * EACH + head // PHASES) * vocab
        return pl.ds(pl.multiple_of(start, vocab), e_rows)

    e1 = []

    def send_mixes(phase):
        copies = to_all(
            "dp", lambda other: low_ref.at[e_slice(phase, other), :], lambda step: e_in.at[phase, step],
            e1_send.at[phase], e1_recv.at[phase])
        start_all(copies)
        e1.append(copies)

    items(1, 0, windows - 1, 0)
    for k in range(most):
        @pl.when(k < give)
        def _(k=k):
            back_copy(k).wait_recv()
            po_ref[k, :per_phase, :] = po_in[k]
    mixes_of(0)
    if two_sends:
        send_mixes(0)
    cot_total.step3()
    items(1, windows - 1, windows, 0)
    mixes_of(1)
    send_mixes(1 if two_sends else 0)

    lane_block = iota((vocab, LANES), 1) // quarter
    of_head = [[None] * HEADS for _ in range(3)]
    for group in range(HEADS // GROUP):
        phase, half = divmod(group, HALVES)
        query_plain = tab_ref[group, :vocab, LANES : 2 * LANES]
        key_plain = tab_ref[group, :vocab, 4 * LANES : 5 * LANES]
        mass = m_ref[group * GROUP * vocab : (group + 1) * GROUP * vocab, :].astype(BF16)
        block = iota((GROUP * vocab, LANES), 0) // vocab == iota((GROUP * vocab, LANES), 1) // quarter
        stacked = jnp.concatenate([key_plain] * GROUP, axis=0)
        plain_q = t_dot(mass, jnp.where(block, stacked, jnp.zeros_like(stacked)))[:vocab, :]
        mixed_k = dot(mass[:, :vocab], query_plain)
        plain_k = sum(
            jnp.where(lane_block == h, mixed_k[h * vocab : (h + 1) * vocab, :], 0.0) for h in range(GROUP))
        for at, ref, plain in ((0, agg_q_ref, plain_q), (1, agg_k_ref, plain_k)):
            cosine = ref[phase, :, half * LANES : (half + 1) * LANES]
            sine = ref[phase, :, (HALVES + half) * LANES : (HALVES + half + 1) * LANES]
            turned = cosine - roll_pairs(sine)
            for h in range(GROUP):
                of_head[at][head_at(group * GROUP + h)] = jnp.concatenate(
                    [turned[:, h * quarter : (h + 1) * quarter], plain[:, h * quarter : (h + 1) * quarter]], axis=1)
    columns = [jnp.concatenate(of_head[at], axis=1) * HEAD_DIM**-0.5 for at in range(2)]
    pieces = []
    lane_head = iota((vocab, LANES), 1) // HEAD_DIM
    for at in range(EACH):
        low = jnp.concatenate(
            [low_ref[(h * EACH + at) * vocab : (h * EACH + at + 1) * vocab, :] for h in range(PHASES)], axis=0)
        both_heads = dot_t(low, w_out[at * LANES : (at + 1) * LANES, :])
        pieces.append(jnp.where(lane_head == 0, both_heads[:vocab, :], both_heads[vocab:, :]))
    columns = jnp.concatenate(columns + pieces, axis=1)
    for at in range(dp):
        sum_total.send(at, columns[:, at * sum_total.columns : (at + 1) * sum_total.columns])
    sum_total.step1()

    mlp = jnp.zeros((vocab, width), F32)
    for at in range(blocks):
        mlp_loads[at][0].wait()
        up = dot(normed_ref[...], w_up[at]) + b_up_ref[:, at * some : (at + 1) * some]
        up_tab[at] = up
        act = gelu_and_slope(up)[0].astype(BF16)
        act_tab[:, at * some : (at + 1) * some] = act
        mlp_loads[at][1].wait()
        mlp += dot(act, w_down[at])
    inputs, _, _ = layer_norm_rows(embed_ref[...])
    base_ref[...] = terms_of(inputs + mlp + b_down_ref[...], 2)
    sum_total.step2()

    cot_sum = cot_total.result()
    cot_sum_ref[...] = cot_sum
    d_normed = jnp.zeros((2 * vocab, width), F32)
    for at in range(blocks):
        d_up = gelu_and_slope(up_tab[at])[1] * dot_t(cot_sum, w_down[at])
        terms = terms_of(d_up, 2)
        d_up_tab[:, at * some : (at + 1) * some] = terms
        d_normed += dot_t(terms, w_up[at])
        if at == blocks // 2:
            sum_total.step3()
    d_normed = d_normed[:vocab, :] + d_normed[vocab:, :]

    for phase, copies in enumerate(e1):
        arrived(copies)
        total = low_ref[e_slice(phase, column), :].astype(F32)
        for step in range(1, dp):
            total += e_in[phase, step].astype(F32)
        e_part[phase] = total.astype(BF16)
    d_rows = width // (dp * shards)
    kinds, own_rows = e_in2.shape[1:3]

    def e_own(other):
        head = (column * shards + other) * d_rows // HEAD_DIM - column * HEADS // dp
        if not two_sends:
            return pl.ds(0, 1), pl.ds(0, own_rows)
        first_kind = 0 if kinds == PHASES else lax.rem(head, PHASES)
        return pl.ds(first_kind, kinds), pl.ds(pl.multiple_of(head // PHASES * vocab, vocab), own_rows)

    e2 = to_all("seq", lambda other: e_part.at[e_own(other)], lambda step: e_in2.at[step], e2_send, e2_recv)
    start_all(e2)
    sums = sum_total.result()
    sums_ref[...] = sums
    for at in range(3):
        d_normed += dot_t(sums[:, at * width : (at + 1) * width], w_qkv[at])
    d_normed_ref[...] = d_normed
    arrived(e2)
    total = e_part[e_own(place)].astype(F32)
    for step in range(1, shards):
        total += e_in2[step].astype(F32)
    e_own_ref[...] = total.astype(BF16)
    for copies in [exchange, e2] + e1:
        for copy in copies:
            copy.wait_send()
    for k in range(most):
        @pl.when(k < take)
        def _(k=k):
            back_copy(k).wait_send()
    cot_total.end()
    sum_total.end()


def last_kernel(
    po_ref, ids_ref, normed_ref, values_ref, mixed_ref, base_ref, sums_ref, cot_sum_ref, act_tab, d_up_tab, d_normed_ref,
    e_own_ref, embed_ref, gain_ref,
    output_ref, embed_grad_ref, gain_grad_ref, shift_grad_ref, qkv_grad_ref, out_grad_ref, up_grad_ref,
    up_bias_grad_ref, down_grad_ref, down_bias_grad_ref,
):
    vocab, width = embed_ref.shape
    windows, rows = ids_ref.shape
    hidden = act_tab.shape[1]
    d_rows, f_rows = qkv_grad_ref.shape[0], down_grad_ref.shape[0]
    index = lax.axis_index("dp") * lax.axis_size("seq") + lax.axis_index("seq")
    right = jnp.concatenate([mixed_ref[...], base_ref[...]], axis=0)
    for window in range(windows):
        oh_t = ones_where(iota((vocab, rows), 0) == ids_ref[window : window + 1, :])
        output_ref[window] = t_dot(jnp.concatenate([po_ref[window], oh_t, oh_t], axis=0), right).astype(BF16)
    pick = ones_where(iota((d_rows, width), 1) == iota((d_rows, width), 0) + index * d_rows)
    pick_f = ones_where(iota((f_rows, hidden), 1) == iota((f_rows, hidden), 0) + index * f_rows)
    normed_own = dot_t(pick, normed_ref[...]).astype(BF16)
    act_own = dot_t(pick_f, act_tab[...]).astype(BF16)
    qkv_grad_ref[...] = dot(normed_own, sums_ref[...])
    up_grad_ref[...] = dot(jnp.concatenate([normed_own, normed_own], axis=1), d_up_tab[...])
    down_grad_ref[...] = dot(act_own, cot_sum_ref[...])
    up_bias_grad_ref[...] = jnp.sum(dot_t(d_up_tab[...], pick_f), axis=0, keepdims=True)
    d_normed = d_normed_ref[...]
    cot_sum = cot_sum_ref[...].astype(F32)
    _, xhat, rstd = layer_norm_rows(embed_ref[...])
    scaled = d_normed * gain_ref[...]
    d_input = cot_sum + rstd * (
        scaled
        - jnp.mean(scaled, axis=1, keepdims=True)
        - xhat * jnp.mean(scaled * xhat, axis=1, keepdims=True)
    )
    wide = dot_t(pick, terms_of(d_input, 3))
    embed_grad_ref[...] = wide[:, :vocab] + wide[:, vocab : 2 * vocab] + wide[:, 2 * vocab :]
    for ref, value in ((gain_grad_ref, d_normed * xhat), (shift_grad_ref, d_normed), (down_bias_grad_ref, cot_sum)):
        ref[...] = jnp.sum(dot_t(terms_of(value, 3), pick), axis=0, keepdims=True)
    own = e_own_ref[...]
    kinds, own_rows = own.shape[:2]
    values_own = dot_t(pick, values_ref[...]).astype(BF16)
    row_head = iota((d_rows, vocab), 0) // HEAD_DIM
    left = jnp.concatenate([
        jnp.where(row_head == at * kinds + kind, values_own, jnp.zeros_like(values_own))
        for kind in range(kinds) for at in range(own_rows // vocab)], axis=1)
    out_grad_ref[...] = dot(left, own.reshape(kinds * own_rows, width))


def per_device(
    token_ids, positions, embed, ln_gain, ln_shift, w_qkv, w_out, w_up, b_up, w_down, b_down, cotangent
):
    vocab, width = embed.shape
    hidden = w_up.shape[1]
    windows, rows = token_ids.shape
    dp, seq = lax.axis_size("dp"), lax.axis_size("seq")
    length = seq * rows
    d_rows, f_rows = width // (dp * seq), hidden // (dp * seq)
    some = 512
    blocks = hidden // some
    most = max(gifts(seq, windows))
    two_sends = dp <= EACH
    sends = PHASES if two_sends else 1
    e_rows = EACH // dp * vocab if two_sends else vocab
    own_heads = max(1, d_rows // HEAD_DIM)
    kinds = PHASES if own_heads > 1 else 1
    own_rows = own_heads // kinds * vocab
    vmem = pl.BlockSpec(memory_space=pltpu.VMEM)
    hbm = pl.BlockSpec(memory_space=pl.ANY)
    shape = jax.ShapeDtypeStruct
    sems = lambda *sizes: pltpu.SemaphoreType.DMA(sizes)
    gain, shift = ln_gain[None, :], ln_shift[None, :]
    po, normed, values, mixed, base, sums, cot_sum, act_tab, d_up_tab, d_normed, e_own = pl.pallas_call(
        main_kernel,
        in_specs=[hbm] * 12,
        out_specs=[vmem] * 11,
        out_shape=[
            shape((windows + most, HEADS * vocab, rows), BF16),
            shape((vocab, width), BF16),
            shape((vocab, width), BF16),
            shape((HEADS * vocab, width), BF16),
            shape((2 * vocab, width), BF16),
            shape((vocab, 3 * width), BF16),
            shape((vocab, width), BF16),
            shape((vocab, hidden), BF16),
            shape((2 * vocab, hidden), BF16),
            shape((vocab, width), F32),
            shape((kinds, own_rows, width), BF16),
        ],
        scratch_shapes=[
            pltpu.VMEM((seq, 2 * windows, rows), jnp.int32),
            pltpu.VMEM((vocab, width), BF16),
            pltpu.VMEM((1, width), F32),
            pltpu.VMEM((1, width), F32),
            pltpu.VMEM((1, hidden), F32),
            pltpu.VMEM((1, width), F32),
            pltpu.VMEM((windows, rows, width), BF16),
            pltpu.VMEM((3, width, width), BF16),
            pltpu.VMEM((width, width), BF16),
            pltpu.VMEM((blocks, width, some), BF16),
            pltpu.VMEM((blocks, some, width), BF16),
            pltpu.VMEM((HEADS // GROUP, LANES, 6 * LANES), BF16),
            pltpu.VMEM((windows + most, EACH * vocab, rows), BF16),
            pltpu.VMEM((max(most, 1), EACH * vocab, rows), BF16),
            pltpu.VMEM((windows, vocab, length), BF16),
            pltpu.VMEM((windows, length, LANES), BF16),
            pltpu.VMEM((windows, length, LANES), F32),
            pltpu.VMEM((windows, length, LANES), F32),
            pltpu.VMEM((2, windows, 3 * ROT // 2, length), BF16),
            pltpu.VMEM((HEADS * vocab, width), BF16),
            pltpu.VMEM((HEADS * vocab, LANES), F32),
            pltpu.VMEM((PHASES, vocab, 2 * HALVES * LANES), F32),
            pltpu.VMEM((PHASES, vocab, 2 * HALVES * LANES), F32),
            pltpu.VMEM((blocks, vocab, some), F32),
            pltpu.VMEM((sends, dp, e_rows, width), BF16),
            pltpu.VMEM((sends, e_rows, width), BF16),
            pltpu.VMEM((seq, kinds, own_rows, width), BF16),
            sems(13),
            sems(2, blocks),
            sems(seq),
            sems(seq),
            sems(max(most, 1)),
            sems(max(most, 1)),
            sems(max(most, 1)),
            sems(max(most, 1)),
            sems(sends, dp),
            sems(sends, dp),
            sems(seq),
            sems(seq),
        ]
        + total_scratch(dp, seq, vocab, width // dp)
        + total_scratch(dp, seq, vocab, 3 * width // dp),
        compiler_params=pltpu.CompilerParams(
            vmem_limit_bytes=60 * 1024 * 1024, collective_id=1, has_side_effects=True),
    )(token_ids, positions, embed, gain, shift, b_up[None, :], b_down[None, :], cotangent, w_qkv, w_out, w_up, w_down)
    outs = pl.pallas_call(
        last_kernel,
        in_specs=[vmem] * 14,
        out_specs=[vmem] * 10,
        out_shape=[
            shape((windows, rows, width), BF16),
            shape((d_rows, vocab), F32),
            shape((1, d_rows), F32),
            shape((1, d_rows), F32),
            shape((d_rows, 3 * width), F32),
            shape((d_rows, width), F32),
            shape((d_rows, hidden), F32),
            shape((1, f_rows), F32),
            shape((f_rows, width), F32),
            shape((1, d_rows), F32),
        ],
        compiler_params=pltpu.CompilerParams(vmem_limit_bytes=24 * 1024 * 1024),
    )(po, token_ids, normed, values, mixed, base, sums, cot_sum, act_tab, d_up_tab, d_normed, e_own, embed, gain)
    flat = lambda v: v.reshape(-1)
    return (
        outs[0], outs[1], flat(outs[2]), flat(outs[3]), outs[4], outs[5], outs[6], flat(outs[7]), outs[8], flat(outs[9]),
    )


def solution(mesh):
    in_specs = (P("dp", "seq"), P("dp", "seq")) + (P(),) * 9 + (P("dp", "seq", None),)
    both = ("dp", "seq")
    out_specs = (
        P("dp", "seq", None),
        P(both, None),
        P(both),
        P(both),
        P(both, None),
        P(both, None),
        P(both, None),
        P(both),
        P(both, None),
        P(both),
    )
    return jax.shard_map(per_device, mesh=mesh, in_specs=in_specs, out_specs=out_specs, check_vma=False)
```

```python
from functools import partial

import jax
import jax.numpy as jnp
from jax import lax
from jax.experimental import pallas as pl
from jax.experimental.pallas import tpu as pltpu
from jax.sharding import PartitionSpec as P

HEADS = 16
HEAD_DIM = 64
ROT = 32
GROUP = 4
PHASES = 2
EACH = HEADS // PHASES
HALVES = EACH // GROUP
LANES = 128
ln_epsilon = 1e-05
LOG2E = 1.4426950408889634
F32 = jnp.float32
BF16 = jnp.bfloat16
MESH = pl.DeviceIdType.MESH


def dot(a, b):
    return lax.dot_general(a, b, (((1,), (0,)), ((), ())), preferred_element_type=F32)


def dot_t(a, b):
    return lax.dot_general(a, b, (((1,), (1,)), ((), ())), preferred_element_type=F32)


def t_dot(a, b):
    return lax.dot_general(a, b, (((0,), (0,)), ((), ())), preferred_element_type=F32)


def iota(shape, axis):
    return lax.broadcasted_iota(jnp.int32, shape, axis)


def ones_where(mask):
    return mask.astype(F32).astype(BF16)


def terms_of(value, count):
    parts = []
    for _ in range(count):
        high = value.astype(BF16)
        parts.append(high)
        value = value - high.astype(F32)
    return jnp.concatenate(parts, axis=0)


def roll_pairs(values):
    even = iota(values.shape, 1) % 2 == 0
    return jnp.where(even, -pltpu.roll(values, values.shape[1] - 1, 1), pltpu.roll(values, 1, 1))


def gelu_and_slope(u):
    c = 0.7978845608028654
    t = jnp.tanh(c * (u + 0.044715 * u * u * u))
    return 0.5 * u * (1.0 + t), 0.5 * (1.0 + t) + 0.5 * u * (1.0 - t * t) * c * (1.0 + 3 * 0.044715 * u * u)


def greet(axes):
    barrier = pltpu.get_barrier_semaphore()
    count = 0
    for axis in axes:
        size = lax.axis_size(axis)
        me = lax.axis_index(axis)
        for step in range(1, size):
            pl.semaphore_signal(barrier, inc=1, device_id={axis: lax.rem(me + step, size)}, device_id_type=MESH)
        count += size - 1
    return count


def to_all(axis, source, target, send_sem, recv_sem):
    size = lax.axis_size(axis)
    me = lax.axis_index(axis)
    copies = []
    for step in range(1, size):
        other = lax.rem(me + step, size)
        copies.append(pltpu.make_async_remote_copy(
            src_ref=source(other), dst_ref=target(step), send_sem=send_sem.at[step], recv_sem=recv_sem.at[step],
            device_id={axis: other}, device_id_type=MESH,
        ))
    return copies


def start_all(copies):
    for copy in copies:
        copy.start()


def arrived(copies):
    for copy in copies:
        copy.wait_recv()


class Total:
    def __init__(self, own, low, first, part, second, whole, sems):
        self.own, self.low, self.first, self.part = own, low, first, part
        self.second, self.whole, self.sems = second, whole, sems
        self.columns = low.shape[2]

    def load(self, value):
        for at in range(self.own.shape[0]):
            piece = value[:, at * self.columns : (at + 1) * self.columns]
            self.own[at] = piece
            self.low[at] = piece.astype(BF16)

    def one(self):
        return to_all("dp", lambda other: self.low.at[other], lambda step: self.first.at[step], *self.sems[0:2])

    def two(self):
        return to_all("seq", lambda other: self.part, lambda step: self.second.at[step], *self.sems[2:4])

    def three(self):
        column = lax.axis_index("dp")
        return to_all("dp", lambda other: self.whole.at[column], lambda step: self.whole.at[column], *self.sems[4:6])

    def step1(self):
        start_all(self.one())

    def step2(self):
        column = lax.axis_index("dp")
        arrived(self.one())
        value = self.own[column]
        for step in range(1, lax.axis_size("dp")):
            value += self.first[step].astype(F32)
        self.own[column] = value
        self.part[...] = value.astype(BF16)
        start_all(self.two())

    def step3(self):
        column = lax.axis_index("dp")
        arrived(self.two())
        value = self.own[column]
        for step in range(1, lax.axis_size("seq")):
            value += self.second[step].astype(F32)
        self.whole[column] = value.astype(BF16)
        start_all(self.three())

    def finish(self):
        arrived(self.three())

    def sums(self, start, size):
        whole = jnp.concatenate([self.whole[at] for at in range(self.whole.shape[0])], axis=1)
        return whole[:, start : start + size]

    def end(self):
        for copies in (self.one(), self.two(), self.three()):
            for copy in copies:
                copy.wait_send()


def total_scratch(dp, seq, rows, columns):
    return [
        pltpu.VMEM((dp, rows, columns), F32),
        pltpu.VMEM((dp, rows, columns), BF16),
        pltpu.VMEM((dp, rows, columns), BF16),
        pltpu.VMEM((rows, columns), BF16),
        pltpu.VMEM((seq, rows, columns), BF16),
        pltpu.VMEM((dp, rows, columns), BF16),
    ] + [pltpu.SemaphoreType.DMA((size,)) for size in (dp, dp, seq, seq, dp, dp)]


def layer_norm_rows(embed):
    inputs = embed.astype(F32)
    center = inputs - jnp.mean(inputs, axis=1, keepdims=True)
    spread = jnp.mean(center * center, axis=1, keepdims=True)
    rstd = lax.rsqrt(spread + ln_epsilon)
    return inputs, center * rstd, rstd


def head_at(slot):
    return slot % EACH * PHASES + slot // EACH


def gifts(shards, windows):
    counts = []
    for place in range(shards):
        mirror = shards - 1 - place
        spare = PHASES * windows * (place - mirror) / (2.0 * (place + 2))
        counts.append(min(windows, max(0, int(spare + 0.5))))
    return counts


def main_kernel(
    ids_hbm, positions_hbm, embed_hbm, gain_hbm, shift_hbm, b_up_hbm, b_down_hbm, cot_hbm, w_qkv_hbm, w_out_hbm,
    w_up_hbm, w_down_hbm,
    output_hbm, embed_grad_hbm, gain_grad_hbm, shift_grad_hbm, qkv_grad_hbm, out_grad_hbm, up_grad_hbm,
    up_bias_grad_hbm, down_grad_hbm, down_bias_grad_hbm,
    output_ref, embed_grad_ref, gain_grad_ref, shift_grad_ref, qkv_grad_ref, out_grad_ref, up_grad_ref,
    up_bias_grad_ref, down_grad_ref, down_bias_grad_ref,
    po_ref, normed_ref, values_ref, mixed_ref, base_ref,
    both, embed_ref, gain_ref, shift_ref, b_up_ref, b_down_ref, cot_ref, w_qkv, w_out, w_up, w_down,
    tab_ref, grad_ref, po_in, oh_t_ref, oh_ref, cos_ref, sin_ref, turn_ref, projected_ref, low_ref, m_ref, agg_q_ref, agg_k_ref,
    cot_own_ref, act_ref, slope_ref, d_up_ref, e_in, e_part, e_in2,
    load_sem, store_sem, seq_send, seq_recv, gift_send, gift_recv, back_send, back_recv, e1_send, e1_recv, e2_send, e2_recv,
    d_up_send, d_up_recv, *totals,
):
    shards, twice_windows, rows = both.shape
    windows = twice_windows // 2
    vocab, width = embed_ref.shape
    length = shards * rows
    some = w_up.shape[1]
    dp = lax.axis_size("dp")
    column, place = lax.axis_index("dp"), lax.axis_index("seq")
    mirror = shards - 1 - place
    index = column * shards + place
    pairs = ROT // 2
    quarter = LANES // GROUP
    per_phase = EACH * vocab
    give_of = gifts(shards, windows)
    most = max(give_of)
    pick_count = lambda where: sum(
        jnp.where(where == at, jnp.int32(count), jnp.int32(0)) for at, count in enumerate(give_of) if count)
    give, take = pick_count(place), pick_count(mirror)

    small = [
        pltpu.make_async_copy(source, target, load_sem.at[at])
        for at, (source, target) in enumerate((
            (ids_hbm, both.at[place, pl.ds(0, windows), :]),
            (positions_hbm, both.at[place, pl.ds(windows, windows), :]),
            (embed_hbm, embed_ref), (gain_hbm, gain_ref), (shift_hbm, shift_ref)))
    ]
    qkv_load = lambda at: pltpu.make_async_copy(
        w_qkv_hbm.at[:, pl.ds(pl.multiple_of(at * width, width), width)], w_qkv.at[at], load_sem.at[5 + at])
    out_load = pltpu.make_async_copy(w_out_hbm, w_out, load_sem.at[8])
    cot_load = pltpu.make_async_copy(cot_hbm, cot_ref, load_sem.at[9])
    hidden_at = pl.ds(pl.multiple_of(column * some, some), some)
    mlp_loads = [
        pltpu.make_async_copy(source, target, load_sem.at[10 + at])
        for at, (source, target) in enumerate((
            (b_up_hbm.at[:, hidden_at], b_up_ref), (w_up_hbm.at[:, hidden_at], w_up),
            (w_down_hbm.at[hidden_at, :], w_down), (b_down_hbm, b_down_ref)))
    ]
    start_all(small + [qkv_load(at) for at in range(3)] + [cot_load, out_load] + mlp_loads)
    guests = greet(("dp", "seq"))
    for copy in small:
        copy.wait()
    pl.semaphore_wait(pltpu.get_barrier_semaphore(), guests)
    exchange = to_all("seq", lambda other: both.at[place], lambda step: both.at[place], seq_send, seq_recv)
    start_all(exchange)

    _, xhat, _ = layer_norm_rows(embed_ref[...])
    normed = (xhat * gain_ref[...] + shift_ref[...]).astype(BF16)
    normed_ref[...] = normed

    def project(at, _):
        qkv_load(at).wait()
        projected_ref[at] = dot(normed_ref[...], w_qkv[at])
        return 0

    lax.fori_loop(0, 3, project, 0)
    projected = [projected_ref[at] for at in range(3)]
    values = projected[2].astype(BF16)
    values_ref[...] = values
    fill = jnp.zeros((LANES - 3 * vocab, 6 * LANES), BF16)
    for group in range(HEADS // GROUP):
        columns = []
        for table in projected[:2]:
            heads = [head_at(group * GROUP + h) * HEAD_DIM for h in range(GROUP)]
            turned = jnp.concatenate([table[:, h : h + ROT] for h in heads], axis=1)
            plain = jnp.concatenate([table[:, h + ROT : h + HEAD_DIM] for h in heads], axis=1)
            columns += [turned, plain, roll_pairs(turned)]
        tab_ref[group] = jnp.concatenate([terms_of(jnp.concatenate(columns, axis=1), 3), fill], axis=0)
    out_load.wait()
    lane_head = iota((vocab, LANES), 1) // HEAD_DIM
    for at in range(EACH):
        part = values[:, at * LANES : (at + 1) * LANES]
        none = jnp.zeros_like(part)
        stacked = jnp.concatenate([jnp.where(lane_head == h, part, none) for h in range(PHASES)], axis=0)
        mixed = dot(stacked, w_out[at * LANES : (at + 1) * LANES, :]).astype(BF16)
        for h in range(PHASES):
            mixed_ref[(h * EACH + at) * vocab : (h * EACH + at + 1) * vocab, :] = mixed[h * vocab : (h + 1) * vocab, :]
    cot_load.wait()
    give_copy = lambda k: pltpu.make_async_remote_copy(
        src_ref=grad_ref.at[k], dst_ref=grad_ref.at[windows + k], send_sem=gift_send.at[k], recv_sem=gift_recv.at[k],
        device_id={"seq": mirror}, device_id_type=MESH)
    back_copy = lambda k: pltpu.make_async_remote_copy(
        src_ref=po_ref.at[windows + k, pl.ds(0, per_phase), :], dst_ref=po_in.at[k], send_sem=back_send.at[k],
        recv_sem=back_recv.at[k], device_id={"seq": mirror}, device_id_type=MESH)

    def grads_of(phase):
        mixed = mixed_ref[pl.ds(pl.multiple_of(phase * per_phase, per_phase), per_phase), :]

        def step(window, _):
            grad_ref[window] = dot_t(mixed, cot_ref[window]).astype(BF16)
            return 0

        lax.fori_loop(0, windows, step, 0)

    grads_of(0)
    for k in range(most):
        @pl.when(k < give)
        def _(k=k):
            give_copy(k).start()


    arrived(exchange)
    inverse = sum(
        jnp.where(iota((pairs, 1), 0) == p, F32(10000.0 ** (-2.0 * p / ROT)), 0.0) for p in range(pairs))
    tiles = ones_where(iota((vocab, LANES), 1) % vocab == iota((vocab, LANES), 0))
    spread = ones_where(iota((3 * pairs, LANES), 0) % pairs == iota((3 * pairs, LANES), 1) % ROT // 2)
    spread_t = ones_where(iota((LANES, 3 * pairs), 1) % pairs == iota((LANES, 3 * pairs), 0) % ROT // 2)
    cot_total, d_total, sum_total = (Total(*totals[at : at + 6], totals[at + 6 : at + 12]) for at in (0, 12, 24))

    def prepare(window, cot_sum):
        row = lambda at: jnp.concatenate([both[s, pl.ds(at, 1), :] for s in range(shards)], axis=1)
        oh_t = ones_where(iota((vocab, length), 0) == row(window))
        oh_t_ref[window] = oh_t
        oh_ref[window] = t_dot(oh_t, tiles).astype(BF16)
        angles = inverse * row(window + windows).astype(F32)
        for at, (value, ref) in enumerate(((jnp.cos(angles), cos_ref), (jnp.sin(angles), sin_ref))):
            terms = terms_of(value, 3)
            turn_ref[at, window] = terms
            ref[window] = t_dot(terms, spread)
        own_t = ones_where(iota((vocab, rows), 0) == both[place, pl.ds(window, 1), :])
        return cot_sum + dot(own_t, cot_ref[window])

    cot_sum = lax.fori_loop(0, windows, prepare, jnp.zeros((vocab, width), F32))
    d_rows = width // (dp * shards)
    cot_own_ref[...] = cot_sum
    for ref in (m_ref, agg_q_ref, agg_k_ref):
        ref[...] = jnp.zeros_like(ref)

    def item(part, phase, window, slot):
        first = part * rows
        span = first + rows
        lane_head = iota((rows, 2 * LANES), 1) % LANES // quarter
        halves = range(HALVES)
        owns, keys, keys_t = [], [], []
        cos, sin = cos_ref[window, :span, :], sin_ref[window, :span, :]
        for half in halves:
            table = tab_ref[phase * HALVES + half]
            raw = dot(oh_ref[window, first:span, :], table[:, : 3 * LANES])
            turned = raw[:, :LANES] * cos[first:, :] + raw[:, 2 * LANES :] * sin[first:, :]
            query = jnp.concatenate([turned, raw[:, LANES : 2 * LANES]], axis=1).astype(BF16)
            owns.append(jnp.concatenate(
                [jnp.where(lane_head == head, query, jnp.zeros_like(query)) for head in range(GROUP)], axis=0))
            raw = dot(oh_ref[window, :span, :], table[:, 3 * LANES :])
            turned = (raw[:, :LANES] * cos + raw[:, 2 * LANES :] * sin).astype(BF16)
            keys.append(jnp.concatenate([turned, raw[:, LANES : 2 * LANES].astype(BF16)], axis=1))
            keys_t.append(turned.T)
        grad = grad_ref[slot].astype(F32)
        lanes_of = lambda v, half: jnp.concatenate(
            [v[(half * GROUP + h) * vocab : (half * GROUP + h + 1) * vocab, :] for h in range(GROUP)], axis=1)
        rows_of = lambda v: [v[:, h * rows : (h + 1) * rows] for h in range(GROUP)]
        kept = iota((rows, GROUP * rows), 0) <= iota((rows, GROUP * rows), 1) % rows
        weights = []
        for half in halves:
            scores = dot_t(keys[half], owns[half]) * (HEAD_DIM**-0.5 * LOG2E)
            last = jnp.where(kept, scores[first:, :], -1e30)
            scores = jnp.concatenate([scores[:first, :], last], axis=0) if first else last
            weights.append(jnp.exp2(scores - jnp.max(scores, axis=0, keepdims=True)).astype(BF16))
        shares, terms, centered = [], [], []
        for half in halves:
            summed = dot(oh_t_ref[window, :, :span], weights[half])
            inverse = 1.0 / jnp.sum(summed, axis=0, keepdims=True)
            share = summed * inverse
            own_grad = lanes_of(grad, half)
            off = own_grad - jnp.sum(share * own_grad, axis=0, keepdims=True)
            shares += rows_of(share)
            terms += rows_of(share * off)
            centered.append((off * inverse).astype(BF16))
        d_scores = [
            (weights[half].astype(F32) * dot(oh_ref[window, :span, :vocab], centered[half])).astype(BF16)
            for half in halves]
        at = pl.ds(pl.multiple_of(phase * per_phase, per_phase), per_phase)
        po_ref[slot, at, :] = jnp.concatenate(shares, axis=0).astype(BF16)
        m_ref[at, :] += dot(jnp.concatenate(terms, axis=0).astype(BF16), oh_ref[window, first:span, :])
        d_query, d_keys = [], []
        for half in halves:
            for head in range(GROUP):
                d_query.append(dot(
                    keys_t[half][head * quarter : (head + 1) * quarter, :],
                    d_scores[half][:, head * rows : (head + 1) * rows]))
            d_keys.append(dot(d_scores[half], owns[half][:, :LANES]))
        parts = [(d * turn).astype(BF16) for turn in (cos, sin) for d in d_keys]
        agg_k_ref[phase] += dot(oh_t_ref[window, :, :span], jnp.concatenate(parts, axis=1))
        d_query = [jnp.concatenate(d_query[h : h + GROUP], axis=0) for h in range(0, EACH, GROUP)]
        turns = [dot(spread_t, turn_ref[at, window, :, first:span]) for at in range(2)]
        parts = [(d * turn).astype(BF16) for turn in turns for d in d_query]
        agg_q_ref[phase] += dot_t(oh_t_ref[window, :, first:span], jnp.concatenate(parts, axis=0))

    two_sends = e_in.shape[0] > 1
    e_rows = e_part.shape[1]

    def mixes_of(phase):
        at = pl.ds(pl.multiple_of(phase * per_phase, per_phase), per_phase)
        total = dot(po_ref[0, at, :], cot_ref[0])
        for window in range(1, windows):
            total += dot(po_ref[window, at, :], cot_ref[window])
        low_ref[at, :] = total.astype(BF16)

    def e_slice(phase, other):
        if two_sends:
            start = phase * per_phase + other * e_rows
        else:
            head = other * HEADS // dp
            start = (head % PHASES * EACH + head // PHASES) * vocab
        return pl.ds(pl.multiple_of(start, vocab), e_rows)

    def e1(phase):
        return to_all(
            "dp", lambda other: low_ref.at[e_slice(phase, other), :], lambda step: e_in.at[phase, step],
            e1_send.at[phase], e1_recv.at[phase])

    first_place = jnp.where(place == 0, F32(1.0), F32(0.0))

    def mlp_forward():
        for copy in mlp_loads:
            copy.wait()
        act, slope = gelu_and_slope(dot(normed_ref[...], w_up[...]) + b_up_ref[...])
        act_ref[...] = act.astype(BF16)
        slope_ref[...] = slope
        part = jnp.concatenate([cot_own_ref[...], dot(act_ref[...], w_down[...]) * first_place], axis=1)
        cot_total.load(part)
        cot_total.step1()

    def d_up_copies():
        return to_all("dp", lambda other: d_up_ref.at[column], lambda step: d_up_ref.at[column], d_up_send, d_up_recv)

    def mlp_backward():
        cot_total.finish()
        d_up = (slope_ref[...] * dot_t(cot_total.sums(0, width), w_down[...])).astype(BF16)
        d_up_ref[column] = d_up
        start_all(d_up_copies())
        d_total.load(dot_t(d_up, w_up[...]) * first_place)
        d_total.step1()

    turn = windows - give + take
    steps = turn + windows
    for k in range(most):
        @pl.when(k < take)
        def _(k=k):
            give_copy(k).wait_recv()

    def step(at, _):
        phase = jnp.where(at < turn, jnp.int32(0), jnp.int32(1))
        taken = jnp.where(at < windows - give, jnp.int32(0), jnp.int32(1)) * (1 - phase)
        window = phase * (at - turn) + (1 - phase) * ((1 - taken) * (give + at) + taken * (at - windows + give))
        slot = window + taken * windows
        whose = taken * mirror + (1 - taken) * place
        for part in range(shards):
            pl.when(whose == part)(partial(item, part, phase, window, slot))

        @pl.when(at == turn - 1)
        def _():
            for k in range(most):
                @pl.when(k < take)
                def _(k=k):
                    back_copy(k).start()

                @pl.when(k < give)
                def _(k=k):
                    give_copy(k).wait_send()
            grads_of(1)

        @pl.when(at == steps - 2)
        def _():
            for k in range(most):
                @pl.when(k < give)
                def _(k=k):
                    back_copy(k).wait_recv()
                    po_ref[k, :per_phase, :] = po_in[k]

        for when, work in enumerate((mlp_forward, cot_total.step2, cot_total.step3, mlp_backward, d_total.step2, d_total.step3)):
            pl.when(at == jnp.minimum(when, steps - 1))(work)

        @pl.when(at >= steps - 2)
        def _():
            done = at - (steps - 2)
            mixes_of(done)
            if two_sends:
                start_all(e1(done))

        return 0

    lax.fori_loop(0, steps, step, 0)
    if not two_sends:
        start_all(e1(0))

    lane_block = iota((vocab, LANES), 1) // quarter
    of_head = [[None] * HEADS for _ in range(3)]
    for group in range(HEADS // GROUP):
        phase, half = divmod(group, HALVES)
        query_plain = tab_ref[group, :vocab, LANES : 2 * LANES]
        key_plain = tab_ref[group, :vocab, 4 * LANES : 5 * LANES]
        mass = m_ref[group * GROUP * vocab : (group + 1) * GROUP * vocab, :].astype(BF16)
        block = iota((GROUP * vocab, LANES), 0) // vocab == iota((GROUP * vocab, LANES), 1) // quarter
        stacked = jnp.concatenate([key_plain] * GROUP, axis=0)
        plain_q = t_dot(mass, jnp.where(block, stacked, jnp.zeros_like(stacked)))[:vocab, :]
        mixed_k = dot(mass[:, :vocab], query_plain)
        plain_k = sum(
            jnp.where(lane_block == h, mixed_k[h * vocab : (h + 1) * vocab, :], 0.0) for h in range(GROUP))
        for at, ref, plain in ((0, agg_q_ref, plain_q), (1, agg_k_ref, plain_k)):
            cosine = ref[phase, :, half * LANES : (half + 1) * LANES]
            sine = ref[phase, :, (HALVES + half) * LANES : (HALVES + half + 1) * LANES]
            turned = cosine - roll_pairs(sine)
            for h in range(GROUP):
                of_head[at][head_at(group * GROUP + h)] = jnp.concatenate(
                    [turned[:, h * quarter : (h + 1) * quarter], plain[:, h * quarter : (h + 1) * quarter]], axis=1)
    columns = [jnp.concatenate(of_head[at], axis=1) * HEAD_DIM**-0.5 for at in range(2)]
    pieces = []
    lane_head = iota((vocab, LANES), 1) // HEAD_DIM
    for at in range(EACH):
        low = jnp.concatenate(
            [low_ref[(h * EACH + at) * vocab : (h * EACH + at + 1) * vocab, :] for h in range(PHASES)], axis=0)
        both_heads = dot_t(low, w_out[at * LANES : (at + 1) * LANES, :])
        pieces.append(jnp.where(lane_head == 0, both_heads[:vocab, :], both_heads[vocab:, :]))
    columns = jnp.concatenate(columns + pieces, axis=1)
    sum_total.load(columns)
    sum_total.step1()

    stores = [
        pltpu.make_async_copy(source, target, store_sem.at[at])
        for at, (source, target) in enumerate((
            (output_ref, output_hbm), (embed_grad_ref, embed_grad_hbm), (gain_grad_ref, gain_grad_hbm),
            (shift_grad_ref, shift_grad_hbm), (qkv_grad_ref, qkv_grad_hbm), (out_grad_ref, out_grad_hbm),
            (up_grad_ref, up_grad_hbm), (up_bias_grad_ref, up_bias_grad_hbm), (down_grad_ref, down_grad_hbm),
            (down_bias_grad_ref, down_bias_grad_hbm)))
    ]
    inputs, xhat, rstd = layer_norm_rows(embed_ref[...])
    base_ref[: HEADS * vocab, :] = mixed_ref[...]
    base_ref[HEADS * vocab :, :] = terms_of(inputs + cot_total.sums(width, width).astype(F32) + b_down_ref[...], 2)

    def finish_window(window, _):
        oh_t = ones_where(iota((vocab, rows), 0) == both[place, pl.ds(window, 1), :])
        output_ref[window] = t_dot(jnp.concatenate([po_ref[window], oh_t, oh_t], axis=0), base_ref[...]).astype(BF16)
        return 0

    lax.fori_loop(0, windows // 2, finish_window, 0)
    sum_total.step2()
    lax.fori_loop(windows // 2, windows, finish_window, 0)
    stores[0].start()
    f_rows = down_grad_ref.shape[0]
    cot_sum = cot_total.sums(0, width)
    pick = ones_where(iota((d_rows, width), 1) == iota((d_rows, width), 0) + index * d_rows)
    pick_f = ones_where(iota((f_rows, some), 1) == iota((f_rows, some), 0) + place * f_rows)
    normed_own = dot_t(pick, normed_ref[...]).astype(BF16)
    down_grad_ref[...] = dot(dot_t(pick_f, act_ref[...]).astype(BF16), cot_sum)
    stores[8].start()
    up_bias_grad_ref[...] = jnp.sum(dot_t(d_up_ref[column], pick_f), axis=0, keepdims=True)
    stores[7].start()
    own_columns = lambda value: jnp.sum(dot_t(terms_of(value, 3), pick), axis=0, keepdims=True)
    down_bias_grad_ref[...] = own_columns(cot_sum.astype(F32))
    stores[9].start()
    sum_total.step3()
    arrived(d_up_copies())
    for at in range(dp):
        up_grad_ref[:, at * some : (at + 1) * some] = dot(normed_own, d_up_ref[at])
    stores[6].start()
    d_total.finish()

    for phase in range(e_in.shape[0]):
        arrived(e1(phase))
        total = low_ref[e_slice(phase, column), :].astype(F32)
        for step in range(1, dp):
            total += e_in[phase, step].astype(F32)
        e_part[phase] = total.astype(BF16)
    kinds, own_rows = e_in2.shape[1:3]

    def e_own(other):
        head = (column * shards + other) * d_rows // HEAD_DIM - column * HEADS // dp
        if not two_sends:
            return pl.ds(0, 1), pl.ds(0, own_rows)
        first_kind = 0 if kinds == PHASES else lax.rem(head, PHASES)
        return pl.ds(first_kind, kinds), pl.ds(pl.multiple_of(head // PHASES * vocab, vocab), own_rows)

    e2 = to_all("seq", lambda other: e_part.at[e_own(other)], lambda step: e_in2.at[step], e2_send, e2_recv)
    start_all(e2)
    sum_total.finish()
    sums = sum_total.sums(0, 3 * width)
    d_normed = d_total.sums(0, width).astype(F32)
    for at in range(3):
        d_normed += dot_t(sums[:, at * width : (at + 1) * width], w_qkv[at])
    qkv_grad_ref[...] = dot(normed_own, sums)
    stores[4].start()
    gain_grad_ref[...] = own_columns(d_normed * xhat)
    stores[2].start()
    shift_grad_ref[...] = own_columns(d_normed)
    stores[3].start()
    scaled = d_normed * gain_ref[...]
    d_input = cot_sum.astype(F32) + rstd * (
        scaled
        - jnp.mean(scaled, axis=1, keepdims=True)
        - xhat * jnp.mean(scaled * xhat, axis=1, keepdims=True)
    )
    wide = dot_t(pick, terms_of(d_input, 3))
    embed_grad_ref[...] = wide[:, :vocab] + wide[:, vocab : 2 * vocab] + wide[:, 2 * vocab :]
    stores[1].start()
    arrived(e2)
    total = e_part[e_own(place)].astype(F32)
    for step in range(1, shards):
        total += e_in2[step].astype(F32)
    own = total.astype(BF16).reshape(kinds * own_rows, width)
    values_own = dot_t(pick, values_ref[...]).astype(BF16)
    row_head = iota((d_rows, vocab), 0) // HEAD_DIM
    left = jnp.concatenate([
        jnp.where(row_head == at * kinds + kind, values_own, jnp.zeros_like(values_own))
        for kind in range(kinds) for at in range(own_rows // vocab)], axis=1)
    out_grad_ref[...] = dot(left, own)
    stores[5].start()
    for copies in [exchange, e2, d_up_copies()] + [e1(phase) for phase in range(e_in.shape[0])]:
        for copy in copies:
            copy.wait_send()
    for k in range(most):
        @pl.when(k < take)
        def _(k=k):
            back_copy(k).wait_send()
    for total in (cot_total, d_total, sum_total):
        total.end()
    for store in stores:
        store.wait()


def copy_kernel(*refs):
    count = (len(refs) - 1) // 2
    copies = [pltpu.make_async_copy(refs[at], refs[count + at], refs[-1].at[at]) for at in range(count)]
    start_all(copies)
    for copy in copies:
        copy.wait()


def per_device(
    token_ids, positions, embed, ln_gain, ln_shift, w_qkv, w_out, w_up, b_up, w_down, b_down, cotangent
):
    vocab, width = embed.shape
    hidden = w_up.shape[1]
    windows, rows = token_ids.shape
    dp, seq = lax.axis_size("dp"), lax.axis_size("seq")
    length = seq * rows
    d_rows, f_rows = width // (dp * seq), hidden // (dp * seq)
    some = hidden // dp
    most = max(gifts(seq, windows))
    two_sends = dp <= EACH
    sends = PHASES if two_sends else 1
    e_rows = EACH // dp * vocab if two_sends else vocab
    own_heads = max(1, d_rows // HEAD_DIM)
    kinds = PHASES if own_heads > 1 else 1
    own_rows = own_heads // kinds * vocab
    vmem = pl.BlockSpec(memory_space=pltpu.VMEM)
    hbm = pl.BlockSpec(memory_space=pl.ANY)
    shape = jax.ShapeDtypeStruct
    sems = lambda *sizes: pltpu.SemaphoreType.DMA(sizes)
    gain, shift = ln_gain[None, :], ln_shift[None, :]
    results = [
        shape((windows, rows, width), BF16),
        shape((d_rows, vocab), F32),
        shape((1, d_rows), F32),
        shape((1, d_rows), F32),
        shape((d_rows, 3 * width), F32),
        shape((d_rows, width), F32),
        shape((d_rows, hidden), F32),
        shape((1, f_rows), F32),
        shape((f_rows, width), F32),
        shape((1, d_rows), F32),
    ]
    held = pl.pallas_call(
        main_kernel,
        in_specs=[hbm] * 12,
        out_specs=[hbm] * len(results),
        out_shape=results,
        scratch_shapes=[pltpu.VMEM(result.shape, result.dtype) for result in results] + [
            pltpu.VMEM((windows + most, HEADS * vocab, rows), BF16),
            pltpu.VMEM((vocab, width), BF16),
            pltpu.VMEM((vocab, width), BF16),
            pltpu.VMEM((HEADS * vocab, width), BF16),
            pltpu.VMEM(((HEADS + 2) * vocab, width), BF16),
            pltpu.VMEM((seq, 2 * windows, rows), jnp.int32),
            pltpu.VMEM((vocab, width), BF16),
            pltpu.VMEM((1, width), F32),
            pltpu.VMEM((1, width), F32),
            pltpu.VMEM((1, some), F32),
            pltpu.VMEM((1, width), F32),
            pltpu.VMEM((windows, rows, width), BF16),
            pltpu.VMEM((3, width, width), BF16),
            pltpu.VMEM((width, width), BF16),
            pltpu.VMEM((width, some), BF16),
            pltpu.VMEM((some, width), BF16),
            pltpu.VMEM((HEADS // GROUP, LANES, 6 * LANES), BF16),
            pltpu.VMEM((windows + most, EACH * vocab, rows), BF16),
            pltpu.VMEM((max(most, 1), EACH * vocab, rows), BF16),
            pltpu.VMEM((windows, vocab, length), BF16),
            pltpu.VMEM((windows, length, LANES), BF16),
            pltpu.VMEM((windows, length, LANES), F32),
            pltpu.VMEM((windows, length, LANES), F32),
            pltpu.VMEM((2, windows, 3 * ROT // 2, length), BF16),
            pltpu.VMEM((3, vocab, width), F32),
            pltpu.VMEM((HEADS * vocab, width), BF16),
            pltpu.VMEM((HEADS * vocab, LANES), F32),
            pltpu.VMEM((PHASES, vocab, 2 * HALVES * LANES), F32),
            pltpu.VMEM((PHASES, vocab, 2 * HALVES * LANES), F32),
            pltpu.VMEM((vocab, width), F32),
            pltpu.VMEM((vocab, some), BF16),
            pltpu.VMEM((vocab, some), F32),
            pltpu.VMEM((dp, vocab, some), BF16),
            pltpu.VMEM((sends, dp, e_rows, width), BF16),
            pltpu.VMEM((sends, e_rows, width), BF16),
            pltpu.VMEM((seq, kinds, own_rows, width), BF16),
            sems(14),
            sems(len(results)),
            sems(seq),
            sems(seq),
            sems(max(most, 1)),
            sems(max(most, 1)),
            sems(max(most, 1)),
            sems(max(most, 1)),
            sems(sends, dp),
            sems(sends, dp),
            sems(seq),
            sems(seq),
            sems(dp),
            sems(dp),
        ]
        + total_scratch(dp, seq, vocab, 2 * width // dp)
        + total_scratch(dp, seq, vocab, width // dp)
        + total_scratch(dp, seq, vocab, 3 * width // dp),
        compiler_params=pltpu.CompilerParams(
            vmem_limit_bytes=60 * 1024 * 1024, collective_id=1, has_side_effects=True),
    )(token_ids, positions, embed, gain, shift, b_up[None, :], b_down[None, :], cotangent, w_qkv, w_out, w_up, w_down)
    outs = pl.pallas_call(
        copy_kernel,
        in_specs=[hbm] * len(results),
        out_specs=[hbm] * len(results),
        out_shape=results,
        scratch_shapes=[sems(len(results))],
        compiler_params=pltpu.CompilerParams(vmem_limit_bytes=60 * 1024 * 1024),
    )(*held)
    flat = lambda v: v.reshape(-1)
    return (
        outs[0], outs[1], flat(outs[2]), flat(outs[3]), outs[4], outs[5], outs[6], flat(outs[7]), outs[8], flat(outs[9]),
    )


def solution(mesh):
    in_specs = (P("dp", "seq"), P("dp", "seq")) + (P(),) * 9 + (P("dp", "seq", None),)
    both = ("dp", "seq")
    out_specs = (
        P("dp", "seq", None),
        P(both, None),
        P(both),
        P(both),
        P(both, None),
        P(both, None),
        P(both, None),
        P(both),
        P(both, None),
        P(both),
    )
    return jax.shard_map(per_device, mesh=mesh, in_specs=in_specs, out_specs=out_specs, check_vma=False)
```

```python
from functools import partial

import jax
import jax.numpy as jnp
from jax import lax
from jax.experimental import pallas as pl
from jax.experimental.pallas import tpu as pltpu
from jax.sharding import PartitionSpec as P

HEADS = 16
HEAD_DIM = 64
ROT = 32
GROUP = 4
PHASES = 2
EACH = HEADS // PHASES
HALVES = EACH // GROUP
LANES = 128
ln_epsilon = 1e-05
LOG2E = 1.4426950408889634
F32 = jnp.float32
BF16 = jnp.bfloat16
MESH = pl.DeviceIdType.MESH


def dot(a, b):
    return lax.dot_general(a, b, (((1,), (0,)), ((), ())), preferred_element_type=F32)


def dot_t(a, b):
    return lax.dot_general(a, b, (((1,), (1,)), ((), ())), preferred_element_type=F32)


def t_dot(a, b):
    return lax.dot_general(a, b, (((0,), (0,)), ((), ())), preferred_element_type=F32)


def iota(shape, axis):
    return lax.broadcasted_iota(jnp.int32, shape, axis)


def ones_where(mask):
    return mask.astype(F32).astype(BF16)


def terms_of(value, count):
    parts = []
    for _ in range(count):
        high = value.astype(BF16)
        parts.append(high)
        value = value - high.astype(F32)
    return jnp.concatenate(parts, axis=0)


def roll_pairs(values):
    even = iota(values.shape, 1) % 2 == 0
    return jnp.where(even, -pltpu.roll(values, values.shape[1] - 1, 1), pltpu.roll(values, 1, 1))


def gelu_and_slope(u):
    c = 0.7978845608028654
    t = jnp.tanh(c * (u + 0.044715 * u * u * u))
    return 0.5 * u * (1.0 + t), 0.5 * (1.0 + t) + 0.5 * u * (1.0 - t * t) * c * (1.0 + 3 * 0.044715 * u * u)


def greet(axes):
    barrier = pltpu.get_barrier_semaphore()
    count = 0
    for axis in axes:
        size = lax.axis_size(axis)
        me = lax.axis_index(axis)
        for step in range(1, size):
            pl.semaphore_signal(barrier, inc=1, device_id={axis: lax.rem(me + step, size)}, device_id_type=MESH)
        count += size - 1
    return count


def to_all(axis, source, target, send_sem, recv_sem):
    size = lax.axis_size(axis)
    me = lax.axis_index(axis)
    copies = []
    for step in range(1, size):
        other = lax.rem(me + step, size)
        copies.append(pltpu.make_async_remote_copy(
            src_ref=source(other), dst_ref=target(step), send_sem=send_sem.at[step], recv_sem=recv_sem.at[step],
            device_id={axis: other}, device_id_type=MESH,
        ))
    return copies


def start_all(copies):
    for copy in copies:
        copy.start()


def arrived(copies):
    for copy in copies:
        copy.wait_recv()


class Total:
    def __init__(self, own, low, first, part, second, whole, sems):
        self.own, self.low, self.first, self.part = own, low, first, part
        self.second, self.whole, self.sems = second, whole, sems
        self.columns = low.shape[2]

    def load(self, value):
        for at in range(self.own.shape[0]):
            piece = value[:, at * self.columns : (at + 1) * self.columns]
            self.own[at] = piece
            self.low[at] = piece.astype(BF16)

    def one(self):
        return to_all("dp", lambda other: self.low.at[other], lambda step: self.first.at[step], *self.sems[0:2])

    def two(self):
        return to_all("seq", lambda other: self.part, lambda step: self.second.at[step], *self.sems[2:4])

    def three(self):
        column = lax.axis_index("dp")
        return to_all("dp", lambda other: self.whole.at[column], lambda step: self.whole.at[column], *self.sems[4:6])

    def step1(self):
        start_all(self.one())

    def step2(self):
        column = lax.axis_index("dp")
        arrived(self.one())
        value = self.own[column]
        for step in range(1, lax.axis_size("dp")):
            value += self.first[step].astype(F32)
        self.own[column] = value
        self.part[...] = value.astype(BF16)
        start_all(self.two())

    def step3(self):
        column = lax.axis_index("dp")
        arrived(self.two())
        value = self.own[column]
        for step in range(1, lax.axis_size("seq")):
            value += self.second[step].astype(F32)
        self.whole[column] = value.astype(BF16)
        start_all(self.three())

    def finish(self):
        arrived(self.three())

    def sums(self, start, size):
        whole = jnp.concatenate([self.whole[at] for at in range(self.whole.shape[0])], axis=1)
        return whole[:, start : start + size]

    def end(self):
        for copies in (self.one(), self.two(), self.three()):
            for copy in copies:
                copy.wait_send()


def total_scratch(dp, seq, rows, columns):
    return [
        pltpu.VMEM((dp, rows, columns), F32),
        pltpu.VMEM((dp, rows, columns), BF16),
        pltpu.VMEM((dp, rows, columns), BF16),
        pltpu.VMEM((rows, columns), BF16),
        pltpu.VMEM((seq, rows, columns), BF16),
        pltpu.VMEM((dp, rows, columns), BF16),
    ] + [pltpu.SemaphoreType.DMA((size,)) for size in (dp, dp, seq, seq, dp, dp)]


def layer_norm_rows(embed):
    inputs = embed.astype(F32)
    center = inputs - jnp.mean(inputs, axis=1, keepdims=True)
    spread = jnp.mean(center * center, axis=1, keepdims=True)
    rstd = lax.rsqrt(spread + ln_epsilon)
    return inputs, center * rstd, rstd


def head_at(slot):
    return slot % EACH * PHASES + slot // EACH


def gifts(shards, windows):
    counts = []
    for place in range(shards):
        mirror = shards - 1 - place
        spare = PHASES * windows * (place - mirror) / (2.0 * (place + 2))
        counts.append(min(windows, max(0, int(spare + 0.5))))
    return counts


def hooks(shards, windows, count):
    gives = gifts(shards, windows)
    found = []
    for place in range(shards):
        mirror = shards - 1 - place
        costs = [place + 2] * (windows - gives[place]) + [mirror + 2] * gives[mirror] + [place + 2] * windows
        row = []
        for at in range(count):
            spent, step = 0, 0
            while step < len(costs) - 1 and spent + costs[step] < (at + 1) * (shards + 1):
                spent += costs[step]
                step += 1
            row.append(step)
        found.append(row)
    return found


def main_kernel(
    ids_hbm, positions_hbm, embed_hbm, gain_hbm, shift_hbm, b_up_hbm, b_down_hbm, cot_hbm, w_qkv_hbm, w_out_hbm,
    w_up_hbm, w_down_hbm,
    output_hbm, embed_grad_hbm, gain_grad_hbm, shift_grad_hbm, qkv_grad_hbm, out_grad_hbm, up_grad_hbm,
    up_bias_grad_hbm, down_grad_hbm, down_bias_grad_hbm,
    output_ref, embed_grad_ref, gain_grad_ref, shift_grad_ref, qkv_grad_ref, out_grad_ref, up_grad_ref,
    up_bias_grad_ref, down_grad_ref, down_bias_grad_ref,
    po_ref, normed_ref, values_ref, mixed_ref, base_ref,
    both, embed_ref, gain_ref, shift_ref, b_up_ref, b_down_ref, cot_ref, w_qkv, w_out, w_up, w_down,
    tab_ref, grad_ref, po_in, oh_t_ref, oh_ref, cos_ref, sin_ref, turn_ref, projected_ref, low_ref, m_ref, agg_q_ref, agg_k_ref,
    cot_own_ref, act_ref, slope_ref, d_up_ref, e_in, e_part, e_in2,
    load_sem, store_sem, seq_send, seq_recv, gift_send, gift_recv, back_send, back_recv, e1_send, e1_recv, e2_send, e2_recv,
    d_up_send, d_up_recv, *totals,
):
    shards, twice_windows, rows = both.shape
    windows = twice_windows // 2
    vocab, width = embed_ref.shape
    length = shards * rows
    some = w_up.shape[1]
    dp = lax.axis_size("dp")
    column, place = lax.axis_index("dp"), lax.axis_index("seq")
    mirror = shards - 1 - place
    index = column * shards + place
    pairs = ROT // 2
    quarter = LANES // GROUP
    per_phase = EACH * vocab
    give_of = gifts(shards, windows)
    most = max(give_of)
    pick_count = lambda where: sum(
        jnp.where(where == at, jnp.int32(count), jnp.int32(0)) for at, count in enumerate(give_of) if count)
    give, take = pick_count(place), pick_count(mirror)

    small = [
        pltpu.make_async_copy(source, target, load_sem.at[at])
        for at, (source, target) in enumerate((
            (ids_hbm, both.at[place, pl.ds(0, windows), :]),
            (positions_hbm, both.at[place, pl.ds(windows, windows), :]),
            (embed_hbm, embed_ref), (gain_hbm, gain_ref), (shift_hbm, shift_ref)))
    ]
    qkv_load = lambda at: pltpu.make_async_copy(
        w_qkv_hbm.at[:, pl.ds(pl.multiple_of(at * width, width), width)], w_qkv.at[at], load_sem.at[5 + at])
    out_load = pltpu.make_async_copy(w_out_hbm, w_out, load_sem.at[8])
    cot_load = pltpu.make_async_copy(cot_hbm, cot_ref, load_sem.at[9])
    hidden_at = pl.ds(pl.multiple_of(column * some, some), some)
    mlp_loads = [
        pltpu.make_async_copy(source, target, load_sem.at[10 + at])
        for at, (source, target) in enumerate((
            (b_up_hbm.at[:, hidden_at], b_up_ref), (w_up_hbm.at[:, hidden_at], w_up),
            (w_down_hbm.at[hidden_at, :], w_down), (b_down_hbm, b_down_ref)))
    ]
    start_all(small + [qkv_load(at) for at in range(3)] + [cot_load, out_load] + mlp_loads)
    guests = greet(("dp", "seq"))
    for copy in small:
        copy.wait()
    pl.semaphore_wait(pltpu.get_barrier_semaphore(), guests)
    exchange = to_all("seq", lambda other: both.at[place], lambda step: both.at[place], seq_send, seq_recv)
    start_all(exchange)

    _, xhat, _ = layer_norm_rows(embed_ref[...])
    normed = (xhat * gain_ref[...] + shift_ref[...]).astype(BF16)
    normed_ref[...] = normed

    def project(at, _):
        qkv_load(at).wait()
        projected_ref[at] = dot(normed_ref[...], w_qkv[at])
        return 0

    lax.fori_loop(0, 3, project, 0)
    projected = [projected_ref[at] for at in range(3)]
    values = projected[2].astype(BF16)
    values_ref[...] = values
    fill = jnp.zeros((LANES - 3 * vocab, 6 * LANES), BF16)
    for group in range(HEADS // GROUP):
        columns = []
        for table in projected[:2]:
            heads = [head_at(group * GROUP + h) * HEAD_DIM for h in range(GROUP)]
            turned = jnp.concatenate([table[:, h : h + ROT] for h in heads], axis=1)
            plain = jnp.concatenate([table[:, h + ROT : h + HEAD_DIM] for h in heads], axis=1)
            columns += [turned, plain, roll_pairs(turned)]
        tab_ref[group] = jnp.concatenate([terms_of(jnp.concatenate(columns, axis=1), 3), fill], axis=0)
    out_load.wait()
    lane_head = iota((vocab, LANES), 1) // HEAD_DIM
    for at in range(EACH):
        part = values[:, at * LANES : (at + 1) * LANES]
        none = jnp.zeros_like(part)
        stacked = jnp.concatenate([jnp.where(lane_head == h, part, none) for h in range(PHASES)], axis=0)
        mixed = dot(stacked, w_out[at * LANES : (at + 1) * LANES, :]).astype(BF16)
        for h in range(PHASES):
            mixed_ref[(h * EACH + at) * vocab : (h * EACH + at + 1) * vocab, :] = mixed[h * vocab : (h + 1) * vocab, :]
    cot_load.wait()
    give_copy = lambda k: pltpu.make_async_remote_copy(
        src_ref=grad_ref.at[k], dst_ref=grad_ref.at[windows + k], send_sem=gift_send.at[k], recv_sem=gift_recv.at[k],
        device_id={"seq": mirror}, device_id_type=MESH)
    back_copy = lambda k: pltpu.make_async_remote_copy(
        src_ref=po_ref.at[windows + k, pl.ds(0, per_phase), :], dst_ref=po_in.at[k], send_sem=back_send.at[k],
        recv_sem=back_recv.at[k], device_id={"seq": mirror}, device_id_type=MESH)

    def grads_of(phase):
        mixed = mixed_ref[pl.ds(pl.multiple_of(phase * per_phase, per_phase), per_phase), :]

        def step(window, _):
            grad_ref[window] = dot_t(mixed, cot_ref[window]).astype(BF16)
            return 0

        lax.fori_loop(0, windows, step, 0)

    grads_of(0)
    for k in range(most):
        @pl.when(k < give)
        def _(k=k):
            give_copy(k).start()


    arrived(exchange)
    inverse = sum(
        jnp.where(iota((pairs, 1), 0) == p, F32(10000.0 ** (-2.0 * p / ROT)), 0.0) for p in range(pairs))
    tiles = ones_where(iota((vocab, LANES), 1) % vocab == iota((vocab, LANES), 0))
    spread = ones_where(iota((3 * pairs, LANES), 0) % pairs == iota((3 * pairs, LANES), 1) % ROT // 2)
    spread_t = ones_where(iota((LANES, 3 * pairs), 1) % pairs == iota((LANES, 3 * pairs), 0) % ROT // 2)
    cot_total, d_total, sum_total = (Total(*totals[at : at + 6], totals[at + 6 : at + 12]) for at in (0, 12, 24))

    def prepare(window, cot_sum):
        row = lambda at: jnp.concatenate([both[s, pl.ds(at, 1), :] for s in range(shards)], axis=1)
        oh_t = ones_where(iota((vocab, length), 0) == row(window))
        oh_t_ref[window] = oh_t
        oh_ref[window] = t_dot(oh_t, tiles).astype(BF16)
        angles = inverse * row(window + windows).astype(F32)
        for at, (value, ref) in enumerate(((jnp.cos(angles), cos_ref), (jnp.sin(angles), sin_ref))):
            terms = terms_of(value, 3)
            turn_ref[at, window] = terms
            ref[window] = t_dot(terms, spread)
        own_t = ones_where(iota((vocab, rows), 0) == both[place, pl.ds(window, 1), :])
        return cot_sum + dot(own_t, cot_ref[window])

    cot_sum = lax.fori_loop(0, windows, prepare, jnp.zeros((vocab, width), F32))
    d_rows = width // (dp * shards)
    cot_own_ref[...] = cot_sum
    for ref in (m_ref, agg_q_ref, agg_k_ref):
        ref[...] = jnp.zeros_like(ref)

    def item(part, phase, window, slot):
        first = part * rows
        span = first + rows
        lane_head = iota((rows, 2 * LANES), 1) % LANES // quarter
        halves = range(HALVES)
        owns, keys, keys_t = [], [], []
        cos, sin = cos_ref[window, :span, :], sin_ref[window, :span, :]
        for half in halves:
            table = tab_ref[phase * HALVES + half]
            raw = dot(oh_ref[window, first:span, :], table[:, : 3 * LANES])
            turned = raw[:, :LANES] * cos[first:, :] + raw[:, 2 * LANES :] * sin[first:, :]
            query = jnp.concatenate([turned, raw[:, LANES : 2 * LANES]], axis=1).astype(BF16)
            owns.append(jnp.concatenate(
                [jnp.where(lane_head == head, query, jnp.zeros_like(query)) for head in range(GROUP)], axis=0))
            raw = dot(oh_ref[window, :span, :], table[:, 3 * LANES :])
            turned = (raw[:, :LANES] * cos + raw[:, 2 * LANES :] * sin).astype(BF16)
            keys.append(jnp.concatenate([turned, raw[:, LANES : 2 * LANES].astype(BF16)], axis=1))
            keys_t.append(turned.T)
        grad = grad_ref[slot].astype(F32)
        lanes_of = lambda v, half: jnp.concatenate(
            [v[(half * GROUP + h) * vocab : (half * GROUP + h + 1) * vocab, :] for h in range(GROUP)], axis=1)
        rows_of = lambda v: [v[:, h * rows : (h + 1) * rows] for h in range(GROUP)]
        kept = iota((rows, GROUP * rows), 0) <= iota((rows, GROUP * rows), 1) % rows
        weights = []
        for half in halves:
            scores = dot_t(keys[half], owns[half]) * (HEAD_DIM**-0.5 * LOG2E)
            last = jnp.where(kept, scores[first:, :], -1e30)
            scores = jnp.concatenate([scores[:first, :], last], axis=0) if first else last
            weights.append(jnp.exp2(scores - jnp.max(scores, axis=0, keepdims=True)).astype(BF16))
        shares, terms, centered = [], [], []
        for half in halves:
            summed = dot(oh_t_ref[window, :, :span], weights[half])
            inverse = 1.0 / jnp.sum(summed, axis=0, keepdims=True)
            share = summed * inverse
            own_grad = lanes_of(grad, half)
            off = own_grad - jnp.sum(share * own_grad, axis=0, keepdims=True)
            shares += rows_of(share)
            terms += rows_of(share * off)
            centered.append((off * inverse).astype(BF16))
        d_scores = [
            (weights[half].astype(F32) * dot(oh_ref[window, :span, :vocab], centered[half])).astype(BF16)
            for half in halves]
        at = pl.ds(pl.multiple_of(phase * per_phase, per_phase), per_phase)
        po_ref[slot, at, :] = jnp.concatenate(shares, axis=0).astype(BF16)
        m_ref[at, :] += dot(jnp.concatenate(terms, axis=0).astype(BF16), oh_ref[window, first:span, :])
        d_query, d_keys = [], []
        for half in halves:
            for head in range(GROUP):
                d_query.append(dot(
                    keys_t[half][head * quarter : (head + 1) * quarter, :],
                    d_scores[half][:, head * rows : (head + 1) * rows]))
            d_keys.append(dot(d_scores[half], owns[half][:, :LANES]))
        parts = [(d * turn).astype(BF16) for turn in (cos, sin) for d in d_keys]
        agg_k_ref[phase] += dot(oh_t_ref[window, :, :span], jnp.concatenate(parts, axis=1))
        d_query = [jnp.concatenate(d_query[h : h + GROUP], axis=0) for h in range(0, EACH, GROUP)]
        turns = [dot(spread_t, turn_ref[at, window, :, first:span]) for at in range(2)]
        parts = [(d * turn).astype(BF16) for turn in turns for d in d_query]
        agg_q_ref[phase] += dot_t(oh_t_ref[window, :, first:span], jnp.concatenate(parts, axis=0))

    two_sends = e_in.shape[0] > 1
    e_rows = e_part.shape[1]

    def mixes_of(phase):
        at = pl.ds(pl.multiple_of(phase * per_phase, per_phase), per_phase)
        total = dot(po_ref[0, at, :], cot_ref[0])
        for window in range(1, windows):
            total += dot(po_ref[window, at, :], cot_ref[window])
        low_ref[at, :] = total.astype(BF16)

    def e_slice(phase, other):
        if two_sends:
            start = phase * per_phase + other * e_rows
        else:
            head = other * HEADS // dp
            start = (head % PHASES * EACH + head // PHASES) * vocab
        return pl.ds(pl.multiple_of(start, vocab), e_rows)

    def e1(phase):
        return to_all(
            "dp", lambda other: low_ref.at[e_slice(phase, other), :], lambda step: e_in.at[phase, step],
            e1_send.at[phase], e1_recv.at[phase])

    first_place = jnp.where(place == 0, F32(1.0), F32(0.0))

    def mlp_forward():
        for copy in mlp_loads:
            copy.wait()
        act, slope = gelu_and_slope(dot(normed_ref[...], w_up[...]) + b_up_ref[...])
        act_ref[...] = act.astype(BF16)
        slope_ref[...] = slope
        part = jnp.concatenate([cot_own_ref[...], dot(act_ref[...], w_down[...]) * first_place], axis=1)
        cot_total.load(part)
        cot_total.step1()

    def d_up_copies():
        return to_all("dp", lambda other: d_up_ref.at[column], lambda step: d_up_ref.at[column], d_up_send, d_up_recv)

    def mlp_backward():
        cot_total.finish()
        d_up = (slope_ref[...] * dot_t(cot_total.sums(0, width), w_down[...])).astype(BF16)
        d_up_ref[column] = d_up
        start_all(d_up_copies())
        d_total.load(dot_t(d_up, w_up[...]) * first_place)
        d_total.step1()

    turn = windows - give + take
    steps = turn + windows
    for k in range(most):
        @pl.when(k < take)
        def _(k=k):
            give_copy(k).wait_recv()

    works = (mlp_forward, cot_total.step2, cot_total.step3, mlp_backward, d_total.step2, d_total.step3)
    hooks_of = hooks(shards, windows, len(works))

    def step(at, _):
        phase = jnp.where(at < turn, jnp.int32(0), jnp.int32(1))
        taken = jnp.where(at < windows - give, jnp.int32(0), jnp.int32(1)) * (1 - phase)
        window = phase * (at - turn) + (1 - phase) * ((1 - taken) * (give + at) + taken * (at - windows + give))
        slot = window + taken * windows
        whose = taken * mirror + (1 - taken) * place
        for part in range(shards):
            pl.when(whose == part)(partial(item, part, phase, window, slot))

        @pl.when(at == turn - 1)
        def _():
            for k in range(most):
                @pl.when(k < take)
                def _(k=k):
                    back_copy(k).start()

                @pl.when(k < give)
                def _(k=k):
                    give_copy(k).wait_send()
            grads_of(1)

        @pl.when(at == steps - 2)
        def _():
            for k in range(most):
                @pl.when(k < give)
                def _(k=k):
                    back_copy(k).wait_recv()
                    po_ref[k, :per_phase, :] = po_in[k]

        for number, work in enumerate(works):
            when = sum(jnp.where(place == p, jnp.int32(hooks_of[p][number]), jnp.int32(0)) for p in range(shards))
            pl.when(at == when)(work)

        @pl.when(at >= steps - 2)
        def _():
            done = at - (steps - 2)
            mixes_of(done)
            if two_sends:
                start_all(e1(done))

        return 0

    lax.fori_loop(0, steps, step, 0)
    if not two_sends:
        start_all(e1(0))

    lane_block = iota((vocab, LANES), 1) // quarter
    of_head = [[None] * HEADS for _ in range(3)]
    for group in range(HEADS // GROUP):
        phase, half = divmod(group, HALVES)
        query_plain = tab_ref[group, :vocab, LANES : 2 * LANES]
        key_plain = tab_ref[group, :vocab, 4 * LANES : 5 * LANES]
        mass = m_ref[group * GROUP * vocab : (group + 1) * GROUP * vocab, :].astype(BF16)
        block = iota((GROUP * vocab, LANES), 0) // vocab == iota((GROUP * vocab, LANES), 1) // quarter
        stacked = jnp.concatenate([key_plain] * GROUP, axis=0)
        plain_q = t_dot(mass, jnp.where(block, stacked, jnp.zeros_like(stacked)))[:vocab, :]
        mixed_k = dot(mass[:, :vocab], query_plain)
        plain_k = sum(
            jnp.where(lane_block == h, mixed_k[h * vocab : (h + 1) * vocab, :], 0.0) for h in range(GROUP))
        for at, ref, plain in ((0, agg_q_ref, plain_q), (1, agg_k_ref, plain_k)):
            cosine = ref[phase, :, half * LANES : (half + 1) * LANES]
            sine = ref[phase, :, (HALVES + half) * LANES : (HALVES + half + 1) * LANES]
            turned = cosine - roll_pairs(sine)
            for h in range(GROUP):
                of_head[at][head_at(group * GROUP + h)] = jnp.concatenate(
                    [turned[:, h * quarter : (h + 1) * quarter], plain[:, h * quarter : (h + 1) * quarter]], axis=1)
    columns = [jnp.concatenate(of_head[at], axis=1) * HEAD_DIM**-0.5 for at in range(2)]
    pieces = []
    lane_head = iota((vocab, LANES), 1) // HEAD_DIM
    for at in range(EACH):
        low = jnp.concatenate(
            [low_ref[(h * EACH + at) * vocab : (h * EACH + at + 1) * vocab, :] for h in range(PHASES)], axis=0)
        both_heads = dot_t(low, w_out[at * LANES : (at + 1) * LANES, :])
        pieces.append(jnp.where(lane_head == 0, both_heads[:vocab, :], both_heads[vocab:, :]))
    columns = jnp.concatenate(columns + pieces, axis=1)
    sum_total.load(columns)
    sum_total.step1()

    stores = [
        pltpu.make_async_copy(source, target, store_sem.at[at])
        for at, (source, target) in enumerate((
            (output_ref, output_hbm), (embed_grad_ref, embed_grad_hbm), (gain_grad_ref, gain_grad_hbm),
            (shift_grad_ref, shift_grad_hbm), (qkv_grad_ref, qkv_grad_hbm), (out_grad_ref, out_grad_hbm),
            (up_grad_ref, up_grad_hbm), (up_bias_grad_ref, up_bias_grad_hbm), (down_grad_ref, down_grad_hbm),
            (down_bias_grad_ref, down_bias_grad_hbm)))
    ]
    inputs, xhat, rstd = layer_norm_rows(embed_ref[...])
    base_ref[: HEADS * vocab, :] = mixed_ref[...]
    base_ref[HEADS * vocab :, :] = terms_of(inputs + cot_total.sums(width, width).astype(F32) + b_down_ref[...], 2)

    def finish_window(window, _):
        oh_t = ones_where(iota((vocab, rows), 0) == both[place, pl.ds(window, 1), :])
        output_ref[window] = t_dot(jnp.concatenate([po_ref[window], oh_t, oh_t], axis=0), base_ref[...]).astype(BF16)
        return 0

    lax.fori_loop(0, windows // 2, finish_window, 0)
    sum_total.step2()
    lax.fori_loop(windows // 2, windows, finish_window, 0)
    stores[0].start()
    f_rows = down_grad_ref.shape[0]
    cot_sum = cot_total.sums(0, width)
    pick = ones_where(iota((d_rows, width), 1) == iota((d_rows, width), 0) + index * d_rows)
    pick_f = ones_where(iota((f_rows, some), 1) == iota((f_rows, some), 0) + place * f_rows)
    normed_own = dot_t(pick, normed_ref[...]).astype(BF16)
    down_grad_ref[...] = dot(dot_t(pick_f, act_ref[...]).astype(BF16), cot_sum)
    stores[8].start()
    up_bias_grad_ref[...] = jnp.sum(dot_t(d_up_ref[column], pick_f), axis=0, keepdims=True)
    stores[7].start()
    own_columns = lambda value: jnp.sum(dot_t(terms_of(value, 3), pick), axis=0, keepdims=True)
    down_bias_grad_ref[...] = own_columns(cot_sum.astype(F32))
    stores[9].start()
    sum_total.step3()
    arrived(d_up_copies())
    for at in range(dp):
        up_grad_ref[:, at * some : (at + 1) * some] = dot(normed_own, d_up_ref[at])
    stores[6].start()
    d_total.finish()

    for phase in range(e_in.shape[0]):
        arrived(e1(phase))
        total = low_ref[e_slice(phase, column), :].astype(F32)
        for step in range(1, dp):
            total += e_in[phase, step].astype(F32)
        e_part[phase] = total.astype(BF16)
    kinds, own_rows = e_in2.shape[1:3]

    def e_own(other):
        head = (column * shards + other) * d_rows // HEAD_DIM - column * HEADS // dp
        if not two_sends:
            return pl.ds(0, 1), pl.ds(0, own_rows)
        first_kind = 0 if kinds == PHASES else lax.rem(head, PHASES)
        return pl.ds(first_kind, kinds), pl.ds(pl.multiple_of(head // PHASES * vocab, vocab), own_rows)

    e2 = to_all("seq", lambda other: e_part.at[e_own(other)], lambda step: e_in2.at[step], e2_send, e2_recv)
    start_all(e2)
    sum_total.finish()
    sums = sum_total.sums(0, 3 * width)
    d_normed = d_total.sums(0, width).astype(F32)
    for at in range(3):
        d_normed += dot_t(sums[:, at * width : (at + 1) * width], w_qkv[at])
    qkv_grad_ref[...] = dot(normed_own, sums)
    stores[4].start()
    gain_grad_ref[...] = own_columns(d_normed * xhat)
    stores[2].start()
    shift_grad_ref[...] = own_columns(d_normed)
    stores[3].start()
    scaled = d_normed * gain_ref[...]
    d_input = cot_sum.astype(F32) + rstd * (
        scaled
        - jnp.mean(scaled, axis=1, keepdims=True)
        - xhat * jnp.mean(scaled * xhat, axis=1, keepdims=True)
    )
    wide = dot_t(pick, terms_of(d_input, 3))
    embed_grad_ref[...] = wide[:, :vocab] + wide[:, vocab : 2 * vocab] + wide[:, 2 * vocab :]
    stores[1].start()
    arrived(e2)
    total = e_part[e_own(place)].astype(F32)
    for step in range(1, shards):
        total += e_in2[step].astype(F32)
    own = total.astype(BF16).reshape(kinds * own_rows, width)
    values_own = dot_t(pick, values_ref[...]).astype(BF16)
    row_head = iota((d_rows, vocab), 0) // HEAD_DIM
    left = jnp.concatenate([
        jnp.where(row_head == at * kinds + kind, values_own, jnp.zeros_like(values_own))
        for kind in range(kinds) for at in range(own_rows // vocab)], axis=1)
    out_grad_ref[...] = dot(left, own)
    stores[5].start()
    for copies in [exchange, e2, d_up_copies()] + [e1(phase) for phase in range(e_in.shape[0])]:
        for copy in copies:
            copy.wait_send()
    for k in range(most):
        @pl.when(k < take)
        def _(k=k):
            back_copy(k).wait_send()
    for total in (cot_total, d_total, sum_total):
        total.end()
    for store in stores:
        store.wait()


def copy_kernel(count, *refs):
    sources, targets, held = refs[:count], refs[count : 2 * count], refs[2 * count : 3 * count]
    in_sem, out_sem = refs[3 * count :]
    pieces = []
    for source, target, through in zip(sources, targets, held):
        if len(source.shape) == 3:
            pieces += [(source.at[at], through.at[at], target.at[at]) for at in range(source.shape[0])]
        else:
            pieces.append((source, through, target))
    loads = [pltpu.make_async_copy(s, t, in_sem.at[at]) for at, (s, t, _) in enumerate(pieces)]
    stores = [pltpu.make_async_copy(t, o, out_sem.at[at]) for at, (_, t, o) in enumerate(pieces)]
    start_all(loads)
    for load, store in zip(loads, stores):
        load.wait()
        store.start()
    for store in stores:
        store.wait()


def per_device(
    token_ids, positions, embed, ln_gain, ln_shift, w_qkv, w_out, w_up, b_up, w_down, b_down, cotangent
):
    vocab, width = embed.shape
    hidden = w_up.shape[1]
    windows, rows = token_ids.shape
    dp, seq = lax.axis_size("dp"), lax.axis_size("seq")
    length = seq * rows
    d_rows, f_rows = width // (dp * seq), hidden // (dp * seq)
    some = hidden // dp
    most = max(gifts(seq, windows))
    two_sends = dp <= EACH
    sends = PHASES if two_sends else 1
    e_rows = EACH // dp * vocab if two_sends else vocab
    own_heads = max(1, d_rows // HEAD_DIM)
    kinds = PHASES if own_heads > 1 else 1
    own_rows = own_heads // kinds * vocab
    vmem = pl.BlockSpec(memory_space=pltpu.VMEM)
    hbm = pl.BlockSpec(memory_space=pl.ANY)
    shape = jax.ShapeDtypeStruct
    sems = lambda *sizes: pltpu.SemaphoreType.DMA(sizes)
    gain, shift = ln_gain[None, :], ln_shift[None, :]
    results = [
        shape((windows, rows, width), BF16),
        shape((d_rows, vocab), F32),
        shape((1, d_rows), F32),
        shape((1, d_rows), F32),
        shape((d_rows, 3 * width), F32),
        shape((d_rows, width), F32),
        shape((d_rows, hidden), F32),
        shape((1, f_rows), F32),
        shape((f_rows, width), F32),
        shape((1, d_rows), F32),
    ]
    held = pl.pallas_call(
        main_kernel,
        in_specs=[hbm] * 12,
        out_specs=[hbm] * len(results),
        out_shape=results,
        scratch_shapes=[pltpu.VMEM(result.shape, result.dtype) for result in results] + [
            pltpu.VMEM((windows + most, HEADS * vocab, rows), BF16),
            pltpu.VMEM((vocab, width), BF16),
            pltpu.VMEM((vocab, width), BF16),
            pltpu.VMEM((HEADS * vocab, width), BF16),
            pltpu.VMEM(((HEADS + 2) * vocab, width), BF16),
            pltpu.VMEM((seq, 2 * windows, rows), jnp.int32),
            pltpu.VMEM((vocab, width), BF16),
            pltpu.VMEM((1, width), F32),
            pltpu.VMEM((1, width), F32),
            pltpu.VMEM((1, some), F32),
            pltpu.VMEM((1, width), F32),
            pltpu.VMEM((windows, rows, width), BF16),
            pltpu.VMEM((3, width, width), BF16),
            pltpu.VMEM((width, width), BF16),
            pltpu.VMEM((width, some), BF16),
            pltpu.VMEM((some, width), BF16),
            pltpu.VMEM((HEADS // GROUP, LANES, 6 * LANES), BF16),
            pltpu.VMEM((windows + most, EACH * vocab, rows), BF16),
            pltpu.VMEM((max(most, 1), EACH * vocab, rows), BF16),
            pltpu.VMEM((windows, vocab, length), BF16),
            pltpu.VMEM((windows, length, LANES), BF16),
            pltpu.VMEM((windows, length, LANES), F32),
            pltpu.VMEM((windows, length, LANES), F32),
            pltpu.VMEM((2, windows, 3 * ROT // 2, length), BF16),
            pltpu.VMEM((3, vocab, width), F32),
            pltpu.VMEM((HEADS * vocab, width), BF16),
            pltpu.VMEM((HEADS * vocab, LANES), F32),
            pltpu.VMEM((PHASES, vocab, 2 * HALVES * LANES), F32),
            pltpu.VMEM((PHASES, vocab, 2 * HALVES * LANES), F32),
            pltpu.VMEM((vocab, width), F32),
            pltpu.VMEM((vocab, some), BF16),
            pltpu.VMEM((vocab, some), F32),
            pltpu.VMEM((dp, vocab, some), BF16),
            pltpu.VMEM((sends, dp, e_rows, width), BF16),
            pltpu.VMEM((sends, e_rows, width), BF16),
            pltpu.VMEM((seq, kinds, own_rows, width), BF16),
            sems(14),
            sems(len(results)),
            sems(seq),
            sems(seq),
            sems(max(most, 1)),
            sems(max(most, 1)),
            sems(max(most, 1)),
            sems(max(most, 1)),
            sems(sends, dp),
            sems(sends, dp),
            sems(seq),
            sems(seq),
            sems(dp),
            sems(dp),
        ]
        + total_scratch(dp, seq, vocab, 2 * width // dp)
        + total_scratch(dp, seq, vocab, width // dp)
        + total_scratch(dp, seq, vocab, 3 * width // dp),
        compiler_params=pltpu.CompilerParams(
            vmem_limit_bytes=60 * 1024 * 1024, collective_id=1, has_side_effects=True),
    )(token_ids, positions, embed, gain, shift, b_up[None, :], b_down[None, :], cotangent, w_qkv, w_out, w_up, w_down)
    outs = pl.pallas_call(
        partial(copy_kernel, len(results)),
        in_specs=[hbm] * len(results),
        out_specs=[hbm] * len(results),
        out_shape=results,
        scratch_shapes=[pltpu.VMEM(result.shape, result.dtype) for result in results]
        + [sems(windows + len(results))] * 2,
        compiler_params=pltpu.CompilerParams(vmem_limit_bytes=60 * 1024 * 1024),
    )(*held)
    flat = lambda v: v.reshape(-1)
    return (
        outs[0], outs[1], flat(outs[2]), flat(outs[3]), outs[4], outs[5], outs[6], flat(outs[7]), outs[8], flat(outs[9]),
    )


def solution(mesh):
    in_specs = (P("dp", "seq"), P("dp", "seq")) + (P(),) * 9 + (P("dp", "seq", None),)
    both = ("dp", "seq")
    out_specs = (
        P("dp", "seq", None),
        P(both, None),
        P(both),
        P(both),
        P(both, None),
        P(both, None),
        P(both, None),
        P(both),
        P(both, None),
        P(both),
    )
    return jax.shard_map(per_device, mesh=mesh, in_specs=in_specs, out_specs=out_specs, check_vma=False)
```

```python
from functools import partial

import jax
import jax.numpy as jnp
from jax import lax
from jax.experimental import pallas as pl
from jax.experimental.pallas import tpu as pltpu
from jax.sharding import PartitionSpec as P

HEADS = 16
HEAD_DIM = 64
ROT = 32
GROUP = 4
PHASES = 2
EACH = HEADS // PHASES
HALVES = EACH // GROUP
LANES = 128
ln_epsilon = 1e-05
LOG2E = 1.4426950408889634
F32 = jnp.float32
BF16 = jnp.bfloat16
F8 = jnp.float8_e4m3fn
MESH = pl.DeviceIdType.MESH


def dot(a, b):
    return lax.dot_general(a, b, (((1,), (0,)), ((), ())), preferred_element_type=F32)


def dot_t(a, b):
    return lax.dot_general(a, b, (((1,), (1,)), ((), ())), preferred_element_type=F32)


def t_dot(a, b):
    return lax.dot_general(a, b, (((0,), (0,)), ((), ())), preferred_element_type=F32)


def iota(shape, axis):
    return lax.broadcasted_iota(jnp.int32, shape, axis)


def ones_where(mask):
    return mask.astype(F32).astype(BF16)


def terms_of(value, count):
    parts = []
    for _ in range(count):
        high = value.astype(BF16)
        parts.append(high)
        value = value - high.astype(F32)
    return jnp.concatenate(parts, axis=0)


def roll_pairs(values):
    even = iota(values.shape, 1) % 2 == 0
    return jnp.where(even, -pltpu.roll(values, values.shape[1] - 1, 1), pltpu.roll(values, 1, 1))


def gelu_and_slope(u):
    c = 0.7978845608028654
    t = jnp.tanh(c * (u + 0.044715 * u * u * u))
    return 0.5 * u * (1.0 + t), 0.5 * (1.0 + t) + 0.5 * u * (1.0 - t * t) * c * (1.0 + 3 * 0.044715 * u * u)


def greet(axes):
    barrier = pltpu.get_barrier_semaphore()
    count = 0
    for axis in axes:
        size = lax.axis_size(axis)
        me = lax.axis_index(axis)
        for step in range(1, size):
            pl.semaphore_signal(barrier, inc=1, device_id={axis: lax.rem(me + step, size)}, device_id_type=MESH)
        count += size - 1
    return count


def to_all(axis, source, target, send_sem, recv_sem):
    size = lax.axis_size(axis)
    me = lax.axis_index(axis)
    copies = []
    for step in range(1, size):
        other = lax.rem(me + step, size)
        copies.append(pltpu.make_async_remote_copy(
            src_ref=source(other), dst_ref=target(step), send_sem=send_sem.at[step], recv_sem=recv_sem.at[step],
            device_id={axis: other}, device_id_type=MESH,
        ))
    return copies


def start_all(copies):
    for copy in copies:
        copy.start()


def arrived(copies):
    for copy in copies:
        copy.wait_recv()


class Total:
    def __init__(self, own, low, first, part, second, whole, sems):
        self.own, self.low, self.first, self.part = own, low, first, part
        self.second, self.whole, self.sems = second, whole, sems
        self.columns = low.shape[2]

    def load(self, value):
        for at in range(self.own.shape[0]):
            piece = value[:, at * self.columns : (at + 1) * self.columns]
            self.own[at] = piece
            self.low[at] = piece.astype(BF16)

    def one(self):
        return to_all("dp", lambda other: self.low.at[other], lambda step: self.first.at[step], *self.sems[0:2])

    def two(self):
        return to_all("seq", lambda other: self.part, lambda step: self.second.at[step], *self.sems[2:4])

    def three(self):
        column = lax.axis_index("dp")
        return to_all("dp", lambda other: self.whole.at[column], lambda step: self.whole.at[column], *self.sems[4:6])

    def step1(self):
        start_all(self.one())

    def step2(self):
        column = lax.axis_index("dp")
        arrived(self.one())
        value = self.own[column]
        for step in range(1, lax.axis_size("dp")):
            value += self.first[step].astype(F32)
        self.own[column] = value
        self.part[...] = value.astype(BF16)
        start_all(self.two())

    def step3(self):
        column = lax.axis_index("dp")
        arrived(self.two())
        value = self.own[column]
        for step in range(1, lax.axis_size("seq")):
            value += self.second[step].astype(F32)
        self.whole[column] = value.astype(BF16)
        start_all(self.three())

    def finish(self):
        arrived(self.three())

    def sums(self, start, size):
        whole = jnp.concatenate([self.whole[at] for at in range(self.whole.shape[0])], axis=1)
        return whole[:, start : start + size]

    def end(self):
        for copies in (self.one(), self.two(), self.three()):
            for copy in copies:
                copy.wait_send()


def total_scratch(dp, seq, rows, columns):
    return [
        pltpu.VMEM((dp, rows, columns), F32),
        pltpu.VMEM((dp, rows, columns), BF16),
        pltpu.VMEM((dp, rows, columns), BF16),
        pltpu.VMEM((rows, columns), BF16),
        pltpu.VMEM((seq, rows, columns), BF16),
        pltpu.VMEM((dp, rows, columns), BF16),
    ] + [pltpu.SemaphoreType.DMA((size,)) for size in (dp, dp, seq, seq, dp, dp)]


def layer_norm_rows(embed):
    inputs = embed.astype(F32)
    center = inputs - jnp.mean(inputs, axis=1, keepdims=True)
    spread = jnp.mean(center * center, axis=1, keepdims=True)
    rstd = lax.rsqrt(spread + ln_epsilon)
    return inputs, center * rstd, rstd


def head_at(slot):
    return slot % EACH * PHASES + slot // EACH


def gifts(shards, windows):
    counts = []
    for place in range(shards):
        mirror = shards - 1 - place
        spare = PHASES * windows * (place - mirror) / (2.0 * (place + 2))
        counts.append(min(windows, max(0, int(spare + 0.5))))
    return counts


def hooks(shards, windows, count):
    gives = gifts(shards, windows)
    found = []
    for place in range(shards):
        mirror = shards - 1 - place
        costs = [place + 2] * (windows - gives[place]) + [mirror + 2] * gives[mirror] + [place + 2] * windows
        row = []
        for at in range(count):
            spent, step = 0, 0
            while step < len(costs) - 1 and spent + costs[step] < (at + 1) * (shards + 1):
                spent += costs[step]
                step += 1
            row.append(step)
        found.append(row)
    return found


def main_kernel(
    ids_hbm, positions_hbm, embed_hbm, gain_hbm, shift_hbm, b_up_hbm, b_down_hbm, cot_hbm, w_qkv_hbm, w_out_hbm,
    w_up_hbm, w_down_hbm,
    output_hbm, embed_grad_hbm, gain_grad_hbm, shift_grad_hbm, qkv_grad_hbm, out_grad_hbm, up_grad_hbm,
    up_bias_grad_hbm, down_grad_hbm, down_bias_grad_hbm,
    output_ref, embed_grad_ref, gain_grad_ref, shift_grad_ref, qkv_grad_ref, out_grad_ref, up_grad_ref,
    up_bias_grad_ref, down_grad_ref, down_bias_grad_ref,
    po_ref, normed_ref, values_ref, mixed_ref, base_ref,
    both, embed_ref, gain_ref, shift_ref, b_up_ref, b_down_ref, cot_ref, w_qkv, w_out, w_up, w_down,
    tab_ref, grad_ref, po_in, oh_t_ref, oh_ref, oh8_ref, own_ref, keys_t_ref, weights_ref, center_ref, back_ref, cos_ref, sin_ref, turn_ref, projected_ref, low_ref, m_ref, agg_q_ref, agg_k_ref,
    cot_own_ref, act_ref, slope_ref, d_up_ref, e_in, e_part, e_in2,
    load_sem, store_sem, seq_send, seq_recv, gift_send, gift_recv, back_send, back_recv, e1_send, e1_recv, e2_send, e2_recv,
    d_up_send, d_up_recv, *totals,
):
    shards, twice_windows, rows = both.shape
    windows = twice_windows // 2
    vocab, width = embed_ref.shape
    length = shards * rows
    some = w_up.shape[1]
    dp = lax.axis_size("dp")
    column, place = lax.axis_index("dp"), lax.axis_index("seq")
    mirror = shards - 1 - place
    index = column * shards + place
    pairs = ROT // 2
    quarter = LANES // GROUP
    per_phase = EACH * vocab
    give_of = gifts(shards, windows)
    most = max(give_of)
    pick_count = lambda where: sum(
        jnp.where(where == at, jnp.int32(count), jnp.int32(0)) for at, count in enumerate(give_of) if count)
    give, take = pick_count(place), pick_count(mirror)

    small = [
        pltpu.make_async_copy(source, target, load_sem.at[at])
        for at, (source, target) in enumerate((
            (ids_hbm, both.at[place, pl.ds(0, windows), :]),
            (positions_hbm, both.at[place, pl.ds(windows, windows), :]),
            (embed_hbm, embed_ref), (gain_hbm, gain_ref), (shift_hbm, shift_ref)))
    ]
    qkv_load = lambda at: pltpu.make_async_copy(
        w_qkv_hbm.at[:, pl.ds(pl.multiple_of(at * width, width), width)], w_qkv.at[at], load_sem.at[5 + at])
    out_load = pltpu.make_async_copy(w_out_hbm, w_out, load_sem.at[8])
    cot_load = pltpu.make_async_copy(cot_hbm, cot_ref, load_sem.at[9])
    hidden_at = pl.ds(pl.multiple_of(column * some, some), some)
    mlp_loads = [
        pltpu.make_async_copy(source, target, load_sem.at[10 + at])
        for at, (source, target) in enumerate((
            (b_up_hbm.at[:, hidden_at], b_up_ref), (w_up_hbm.at[:, hidden_at], w_up),
            (w_down_hbm.at[hidden_at, :], w_down), (b_down_hbm, b_down_ref)))
    ]
    start_all(small + [qkv_load(at) for at in range(3)] + [cot_load, out_load] + mlp_loads)
    guests = greet(("dp", "seq"))
    for copy in small:
        copy.wait()
    _, xhat, _ = layer_norm_rows(embed_ref[...])
    normed = (xhat * gain_ref[...] + shift_ref[...]).astype(BF16)
    normed_ref[...] = normed

    def project(at, _):
        qkv_load(at).wait()
        projected_ref[at] = dot(normed_ref[...], w_qkv[at])
        return 0

    lax.fori_loop(0, 3, project, 0)
    pl.semaphore_wait(pltpu.get_barrier_semaphore(), guests)
    exchange = to_all("seq", lambda other: both.at[place], lambda step: both.at[place], seq_send, seq_recv)
    start_all(exchange)
    projected = [projected_ref[at] for at in range(3)]
    values = projected[2].astype(BF16)
    values_ref[...] = values
    fill = jnp.zeros((LANES - 3 * vocab, 6 * LANES), BF16)
    for group in range(HEADS // GROUP):
        columns = []
        for table in projected[:2]:
            heads = [head_at(group * GROUP + h) * HEAD_DIM for h in range(GROUP)]
            turned = jnp.concatenate([table[:, h : h + ROT] for h in heads], axis=1)
            plain = jnp.concatenate([table[:, h + ROT : h + HEAD_DIM] for h in heads], axis=1)
            columns += [turned, plain, roll_pairs(turned)]
        tab_ref[group] = jnp.concatenate([terms_of(jnp.concatenate(columns, axis=1), 3), fill], axis=0)
    out_load.wait()
    lane_head = iota((vocab, LANES), 1) // HEAD_DIM
    for at in range(EACH):
        part = values[:, at * LANES : (at + 1) * LANES]
        none = jnp.zeros_like(part)
        stacked = jnp.concatenate([jnp.where(lane_head == h, part, none) for h in range(PHASES)], axis=0)
        mixed = dot(stacked, w_out[at * LANES : (at + 1) * LANES, :]).astype(BF16)
        for h in range(PHASES):
            mixed_ref[(h * EACH + at) * vocab : (h * EACH + at + 1) * vocab, :] = mixed[h * vocab : (h + 1) * vocab, :]
    cot_load.wait()
    give_copy = lambda k: pltpu.make_async_remote_copy(
        src_ref=grad_ref.at[k], dst_ref=grad_ref.at[windows + k], send_sem=gift_send.at[k], recv_sem=gift_recv.at[k],
        device_id={"seq": mirror}, device_id_type=MESH)
    back_copy = lambda k: pltpu.make_async_remote_copy(
        src_ref=po_ref.at[windows + k, pl.ds(0, per_phase), :], dst_ref=po_in.at[k], send_sem=back_send.at[k],
        recv_sem=back_recv.at[k], device_id={"seq": mirror}, device_id_type=MESH)

    def grads_of(phase):
        mixed = mixed_ref[pl.ds(pl.multiple_of(phase * per_phase, per_phase), per_phase), :]

        def step(window, _):
            grad_ref[window] = dot_t(mixed, cot_ref[window]).astype(BF16)
            return 0

        lax.fori_loop(0, windows, step, 0)

    grads_of(0)
    for k in range(most):
        @pl.when(k < give)
        def _(k=k):
            give_copy(k).start()


    arrived(exchange)
    inverse = sum(
        jnp.where(iota((pairs, 1), 0) == p, F32(10000.0 ** (-2.0 * p / ROT)), 0.0) for p in range(pairs))
    tiles = ones_where(iota((vocab, LANES), 1) % vocab == iota((vocab, LANES), 0))
    spread = ones_where(iota((3 * pairs, LANES), 0) % pairs == iota((3 * pairs, LANES), 1) % ROT // 2)
    spread_t = ones_where(iota((LANES, 3 * pairs), 1) % pairs == iota((LANES, 3 * pairs), 0) % ROT // 2)
    cot_total, d_total, sum_total = (Total(*totals[at : at + 6], totals[at + 6 : at + 12]) for at in (0, 12, 24))

    def prepare(window, cot_sum):
        row = lambda at: jnp.concatenate([both[s, pl.ds(at, 1), :] for s in range(shards)], axis=1)
        oh_t = ones_where(iota((vocab, length), 0) == row(window))
        oh_t_ref[window] = oh_t
        tiled = t_dot(oh_t, tiles)
        oh_ref[window] = tiled.astype(BF16)
        oh8_ref[window] = tiled[:, : 3 * vocab].astype(F8)
        angles = inverse * row(window + windows).astype(F32)
        for at, (value, ref) in enumerate(((jnp.cos(angles), cos_ref), (jnp.sin(angles), sin_ref))):
            terms = terms_of(value, 3)
            turn_ref[at, window] = terms
            ref[window] = t_dot(terms, spread)
        own_t = ones_where(iota((vocab, rows), 0) == both[place, pl.ds(window, 1), :])
        return cot_sum + dot(own_t, cot_ref[window])

    cot_sum = lax.fori_loop(0, windows, prepare, jnp.zeros((vocab, width), F32))
    d_rows = width // (dp * shards)
    cot_own_ref[...] = cot_sum
    for ref in (m_ref, agg_q_ref, agg_k_ref):
        ref[...] = jnp.zeros_like(ref)

    halves = range(HALVES)

    def forward(part, phase, window, slot, keep):
        first = part * rows
        span = first + rows
        lane_head = iota((rows, 2 * LANES), 1) % LANES // quarter
        owns, keys, keys_t = [], [], []
        cos, sin = cos_ref[window, :span, :], sin_ref[window, :span, :]
        for half in halves:
            table = tab_ref[phase * HALVES + half]
            raw = dot(oh_ref[window, first:span, :], table[:, : 3 * LANES])
            turned = raw[:, :LANES] * cos[first:, :] + raw[:, 2 * LANES :] * sin[first:, :]
            query = jnp.concatenate([turned, raw[:, LANES : 2 * LANES]], axis=1).astype(BF16)
            owns.append(jnp.concatenate(
                [jnp.where(lane_head == head, query, jnp.zeros_like(query)) for head in range(GROUP)], axis=0))
            raw = dot(oh_ref[window, :span, :], table[:, 3 * LANES :])
            turned = (raw[:, :LANES] * cos + raw[:, 2 * LANES :] * sin).astype(BF16)
            keys.append(jnp.concatenate([turned, raw[:, LANES : 2 * LANES].astype(BF16)], axis=1))
            keys_t.append(turned.T)
        grad = grad_ref[slot].astype(F32)
        lanes_of = lambda v, half: jnp.concatenate(
            [v[(half * GROUP + h) * vocab : (half * GROUP + h + 1) * vocab, :] for h in range(GROUP)], axis=1)
        rows_of = lambda v: [v[:, h * rows : (h + 1) * rows] for h in range(GROUP)]
        kept = iota((rows, GROUP * rows), 0) <= iota((rows, GROUP * rows), 1) % rows
        weights = []
        for half in halves:
            scores = dot_t(keys[half], owns[half]) * (HEAD_DIM**-0.5 * LOG2E)
            last = jnp.where(kept, scores[first:, :], -1e30)
            scores = jnp.concatenate([scores[:first, :], last], axis=0) if first else last
            weights.append(jnp.exp2(scores - jnp.max(scores, axis=0, keepdims=True)).astype(BF16))
        shares, terms, centers, backs = [], [], [], []
        for half in halves:
            summed = dot(oh_t_ref[window, :, :span], weights[half])
            inverse = 1.0 / jnp.sum(summed, axis=0, keepdims=True)
            share = summed * inverse
            own_grad = lanes_of(grad, half)
            off = own_grad - jnp.sum(share * own_grad, axis=0, keepdims=True)
            shares += rows_of(share)
            terms += rows_of(share * off)
            off = off * inverse
            power = 6.0 - jnp.floor(jnp.log2(jnp.maximum(jnp.max(jnp.abs(off), axis=0, keepdims=True), 1e-30)))
            backs.append(jnp.exp2(-power))
            off = off * jnp.exp2(power)
            pieces = []
            for _ in range(3):
                pieces.append(off.astype(F8))
                off = off - pieces[-1].astype(F32)
            centers.append(jnp.concatenate(pieces, axis=0))
        at = pl.ds(pl.multiple_of(phase * per_phase, per_phase), per_phase)
        po_ref[slot, at, :] = jnp.concatenate(shares, axis=0).astype(BF16)
        m_ref[at, :] += dot(jnp.concatenate(terms, axis=0).astype(BF16), oh_ref[window, first:span, :])
        owns = [own[:, :LANES] for own in owns]
        if not keep:
            return owns, keys_t, weights, centers, backs
        for half in halves:
            own_ref[half] = owns[half]
            keys_t_ref[half, :, :span] = keys_t[half]
            weights_ref[half, :span, :] = weights[half]
            center_ref[half] = centers[half]
            back_ref[half] = backs[half]

    def kept_of(part):
        span = (part + 1) * rows
        return (
            [own_ref[half] for half in halves], [keys_t_ref[half, :, :span] for half in halves],
            [weights_ref[half, :span, :] for half in halves], [center_ref[half] for half in halves],
            [back_ref[half] for half in halves])

    def backward(part, phase, window, held):
        owns, keys_t, weights, centers, backs = held
        first = part * rows
        span = first + rows
        cos, sin = cos_ref[window, :span, :], sin_ref[window, :span, :]
        d_query, d_keys = [], []
        for half in halves:
            back = backs[half]
            d_scores = (
                weights[half].astype(F32) * dot(oh8_ref[window, :span, :], centers[half])
            ).astype(BF16)
            for head in range(GROUP):
                d_query.append(
                    dot(keys_t[half][head * quarter : (head + 1) * quarter, :],
                        d_scores[:, head * rows : (head + 1) * rows])
                    * back[:, head * rows : (head + 1) * rows])
            own = owns[half].astype(F32) * jnp.broadcast_to(back, (LANES, GROUP * rows)).T
            d_keys.append(dot(d_scores, own.astype(BF16)))
        parts = [(d * turn).astype(BF16) for turn in (cos, sin) for d in d_keys]
        agg_k_ref[phase] += dot(oh_t_ref[window, :, :span], jnp.concatenate(parts, axis=1))
        d_query = [jnp.concatenate(d_query[h : h + GROUP], axis=0) for h in range(0, EACH, GROUP)]
        turns = [dot(spread_t, turn_ref[at, window, :, first:span]) for at in range(2)]
        parts = [(d * turn).astype(BF16) for turn in turns for d in d_query]
        agg_q_ref[phase] += dot_t(oh_t_ref[window, :, first:span], jnp.concatenate(parts, axis=0))

    two_sends = e_in.shape[0] > 1
    e_rows = e_part.shape[1]

    def mixes_of(phase):
        at = pl.ds(pl.multiple_of(phase * per_phase, per_phase), per_phase)
        total = dot(po_ref[0, at, :], cot_ref[0])
        for window in range(1, windows):
            total += dot(po_ref[window, at, :], cot_ref[window])
        low_ref[at, :] = total.astype(BF16)

    def e_slice(phase, other):
        if two_sends:
            start = phase * per_phase + other * e_rows
        else:
            head = other * HEADS // dp
            start = (head % PHASES * EACH + head // PHASES) * vocab
        return pl.ds(pl.multiple_of(start, vocab), e_rows)

    def e1(phase):
        return to_all(
            "dp", lambda other: low_ref.at[e_slice(phase, other), :], lambda step: e_in.at[phase, step],
            e1_send.at[phase], e1_recv.at[phase])

    first_place = jnp.where(place == 0, F32(1.0), F32(0.0))

    def mlp_forward():
        for copy in mlp_loads:
            copy.wait()
        act, slope = gelu_and_slope(dot(normed_ref[...], w_up[...]) + b_up_ref[...])
        act_ref[...] = act.astype(BF16)
        slope_ref[...] = slope
        part = jnp.concatenate([cot_own_ref[...], dot(act_ref[...], w_down[...]) * first_place], axis=1)
        cot_total.load(part)
        cot_total.step1()

    def d_up_copies():
        return to_all("dp", lambda other: d_up_ref.at[column], lambda step: d_up_ref.at[column], d_up_send, d_up_recv)

    def mlp_backward():
        cot_total.finish()
        d_up = (slope_ref[...] * dot_t(cot_total.sums(0, width), w_down[...])).astype(BF16)
        d_up_ref[column] = d_up
        start_all(d_up_copies())
        d_total.load(dot_t(d_up, w_up[...]) * first_place)
        d_total.step1()

    turn = windows - give + take
    steps = turn + windows
    for k in range(most):
        @pl.when(k < take)
        def _(k=k):
            give_copy(k).wait_recv()

    works = (mlp_forward, cot_total.step2, cot_total.step3, mlp_backward, d_total.step2, d_total.step3)
    hooks_of = hooks(shards, windows, len(works))

    def step(at, _):
        phase = jnp.where(at < turn, jnp.int32(0), jnp.int32(1))
        taken = jnp.where(at < windows - give, jnp.int32(0), jnp.int32(1)) * (1 - phase)
        window = phase * (at - turn) + (1 - phase) * ((1 - taken) * (give + at) + taken * (at - windows + give))
        slot = window + taken * windows
        whose = taken * mirror + (1 - taken) * place
        for part in range(shards):
            @pl.when(whose == part)
            def _(part=part):
                backward(part, phase, window, forward(part, phase, window, slot, False))

        @pl.when(at >= steps - 2)
        def _():
            done = at - (steps - 2)

            @pl.when(done == 0)
            def _():
                for k in range(most):
                    @pl.when(k < give)
                    def _(k=k):
                        back_copy(k).wait_recv()
                        po_ref[k, :per_phase, :] = po_in[k]

            mixes_of(done)
            if two_sends:
                @pl.when(done == 0)
                def _():
                    start_all(e1(0))

        @pl.when(at == turn - 1)
        def _():
            for k in range(most):
                @pl.when(k < take)
                def _(k=k):
                    back_copy(k).start()

                @pl.when(k < give)
                def _(k=k):
                    give_copy(k).wait_send()
            grads_of(1)

        for number, work in enumerate(works):
            when = sum(jnp.where(place == p, jnp.int32(hooks_of[p][number]), jnp.int32(0)) for p in range(shards))
            pl.when(at == when)(work)

        return 0

    lax.fori_loop(0, steps, step, 0)
    lane_block = iota((vocab, LANES), 1) // quarter
    of_head = [[None] * HEADS for _ in range(3)]
    for group in range(HEADS // GROUP):
        phase, half = divmod(group, HALVES)
        query_plain = tab_ref[group, :vocab, LANES : 2 * LANES]
        key_plain = tab_ref[group, :vocab, 4 * LANES : 5 * LANES]
        mass = m_ref[group * GROUP * vocab : (group + 1) * GROUP * vocab, :].astype(BF16)
        block = iota((GROUP * vocab, LANES), 0) // vocab == iota((GROUP * vocab, LANES), 1) // quarter
        stacked = jnp.concatenate([key_plain] * GROUP, axis=0)
        plain_q = t_dot(mass, jnp.where(block, stacked, jnp.zeros_like(stacked)))[:vocab, :]
        mixed_k = dot(mass[:, :vocab], query_plain)
        plain_k = sum(
            jnp.where(lane_block == h, mixed_k[h * vocab : (h + 1) * vocab, :], 0.0) for h in range(GROUP))
        for at, ref, plain in ((0, agg_q_ref, plain_q), (1, agg_k_ref, plain_k)):
            cosine = ref[phase, :, half * LANES : (half + 1) * LANES]
            sine = ref[phase, :, (HALVES + half) * LANES : (HALVES + half + 1) * LANES]
            turned = cosine - roll_pairs(sine)
            for h in range(GROUP):
                of_head[at][head_at(group * GROUP + h)] = jnp.concatenate(
                    [turned[:, h * quarter : (h + 1) * quarter], plain[:, h * quarter : (h + 1) * quarter]], axis=1)
    columns = [jnp.concatenate(of_head[at], axis=1) * HEAD_DIM**-0.5 for at in range(2)]
    pieces = []
    lane_head = iota((vocab, LANES), 1) // HEAD_DIM
    for at in range(EACH):
        low = jnp.concatenate(
            [low_ref[(h * EACH + at) * vocab : (h * EACH + at + 1) * vocab, :] for h in range(PHASES)], axis=0)
        both_heads = dot_t(low, w_out[at * LANES : (at + 1) * LANES, :])
        pieces.append(jnp.where(lane_head == 0, both_heads[:vocab, :], both_heads[vocab:, :]))
    columns = jnp.concatenate(columns + pieces, axis=1)
    sum_total.load(columns)
    sum_total.step1()
    start_all(e1(1 if two_sends else 0))

    stores = [
        pltpu.make_async_copy(source, target, store_sem.at[at])
        for at, (source, target) in enumerate((
            (output_ref, output_hbm), (embed_grad_ref, embed_grad_hbm), (gain_grad_ref, gain_grad_hbm),
            (shift_grad_ref, shift_grad_hbm), (qkv_grad_ref, qkv_grad_hbm), (out_grad_ref, out_grad_hbm),
            (up_grad_ref, up_grad_hbm), (up_bias_grad_ref, up_bias_grad_hbm), (down_grad_ref, down_grad_hbm),
            (down_bias_grad_ref, down_bias_grad_hbm)))
    ]
    inputs, xhat, rstd = layer_norm_rows(embed_ref[...])
    base_ref[: HEADS * vocab, :] = mixed_ref[...]
    base_ref[HEADS * vocab :, :] = terms_of(inputs + cot_total.sums(width, width).astype(F32) + b_down_ref[...], 2)

    def finish_window(window, _):
        oh_t = ones_where(iota((vocab, rows), 0) == both[place, pl.ds(window, 1), :])
        output_ref[window] = t_dot(jnp.concatenate([po_ref[window], oh_t, oh_t], axis=0), base_ref[...]).astype(BF16)
        return 0

    lax.fori_loop(0, windows // 2, finish_window, 0)
    sum_total.step2()
    lax.fori_loop(windows // 2, windows, finish_window, 0)
    stores[0].start()
    f_rows = down_grad_ref.shape[0]
    cot_sum = cot_total.sums(0, width)
    pick = ones_where(iota((d_rows, width), 1) == iota((d_rows, width), 0) + index * d_rows)
    pick_f = ones_where(iota((f_rows, some), 1) == iota((f_rows, some), 0) + place * f_rows)
    normed_own = dot_t(pick, normed_ref[...]).astype(BF16)
    down_grad_ref[...] = dot(dot_t(pick_f, act_ref[...]).astype(BF16), cot_sum)
    stores[8].start()
    up_bias_grad_ref[...] = jnp.sum(dot_t(d_up_ref[column], pick_f), axis=0, keepdims=True)
    stores[7].start()
    own_columns = lambda value: jnp.sum(dot_t(terms_of(value, 3), pick), axis=0, keepdims=True)
    down_bias_grad_ref[...] = own_columns(cot_sum.astype(F32))
    stores[9].start()
    sum_total.step3()
    for phase in range(e_in.shape[0]):
        arrived(e1(phase))
        total = low_ref[e_slice(phase, column), :].astype(F32)
        for step in range(1, dp):
            total += e_in[phase, step].astype(F32)
        e_part[phase] = total.astype(BF16)
    kinds, own_rows = e_in2.shape[1:3]

    def e_own(other):
        head = (column * shards + other) * d_rows // HEAD_DIM - column * HEADS // dp
        if not two_sends:
            return pl.ds(0, 1), pl.ds(0, own_rows)
        first_kind = 0 if kinds == PHASES else lax.rem(head, PHASES)
        return pl.ds(first_kind, kinds), pl.ds(pl.multiple_of(head // PHASES * vocab, vocab), own_rows)

    e2 = to_all("seq", lambda other: e_part.at[e_own(other)], lambda step: e_in2.at[step], e2_send, e2_recv)
    start_all(e2)
    arrived(d_up_copies())
    for at in range(dp):
        up_grad_ref[:, at * some : (at + 1) * some] = dot(normed_own, d_up_ref[at])
    stores[6].start()
    d_total.finish()

    sum_total.finish()
    sums = sum_total.sums(0, 3 * width)
    d_normed = d_total.sums(0, width).astype(F32)
    for at in range(3):
        d_normed += dot_t(sums[:, at * width : (at + 1) * width], w_qkv[at])
    qkv_grad_ref[...] = dot(normed_own, sums)
    stores[4].start()
    gain_grad_ref[...] = own_columns(d_normed * xhat)
    stores[2].start()
    shift_grad_ref[...] = own_columns(d_normed)
    stores[3].start()
    scaled = d_normed * gain_ref[...]
    d_input = cot_sum.astype(F32) + rstd * (
        scaled
        - jnp.mean(scaled, axis=1, keepdims=True)
        - xhat * jnp.mean(scaled * xhat, axis=1, keepdims=True)
    )
    wide = dot_t(pick, terms_of(d_input, 3))
    embed_grad_ref[...] = wide[:, :vocab] + wide[:, vocab : 2 * vocab] + wide[:, 2 * vocab :]
    stores[1].start()
    arrived(e2)
    total = e_part[e_own(place)].astype(F32)
    for step in range(1, shards):
        total += e_in2[step].astype(F32)
    own = total.astype(BF16).reshape(kinds * own_rows, width)
    values_own = dot_t(pick, values_ref[...]).astype(BF16)
    row_head = iota((d_rows, vocab), 0) // HEAD_DIM
    left = jnp.concatenate([
        jnp.where(row_head == at * kinds + kind, values_own, jnp.zeros_like(values_own))
        for kind in range(kinds) for at in range(own_rows // vocab)], axis=1)
    out_grad_ref[...] = dot(left, own)
    stores[5].start()
    for copies in [exchange, e2, d_up_copies()] + [e1(phase) for phase in range(e_in.shape[0])]:
        for copy in copies:
            copy.wait_send()
    for k in range(most):
        @pl.when(k < take)
        def _(k=k):
            back_copy(k).wait_send()
    for total in (cot_total, d_total, sum_total):
        total.end()
    for store in stores:
        store.wait()


def copy_kernel(count, *refs):
    sources, targets, held = refs[:count], refs[count : 2 * count], refs[2 * count : 3 * count]
    in_sem, out_sem = refs[3 * count :]
    pieces = []
    for source, target, through in zip(sources, targets, held):
        if len(source.shape) == 3:
            pieces += [(source.at[at], through.at[at], target.at[at]) for at in range(source.shape[0])]
        else:
            pieces.append((source, through, target))
    loads = [pltpu.make_async_copy(s, t, in_sem.at[at]) for at, (s, t, _) in enumerate(pieces)]
    stores = [pltpu.make_async_copy(t, o, out_sem.at[at]) for at, (_, t, o) in enumerate(pieces)]
    start_all(loads)
    for load, store in zip(loads, stores):
        load.wait()
        store.start()
    for store in stores:
        store.wait()


def per_device(
    token_ids, positions, embed, ln_gain, ln_shift, w_qkv, w_out, w_up, b_up, w_down, b_down, cotangent
):
    vocab, width = embed.shape
    hidden = w_up.shape[1]
    windows, rows = token_ids.shape
    dp, seq = lax.axis_size("dp"), lax.axis_size("seq")
    length = seq * rows
    d_rows, f_rows = width // (dp * seq), hidden // (dp * seq)
    some = hidden // dp
    most = max(gifts(seq, windows))
    two_sends = dp <= EACH
    sends = PHASES if two_sends else 1
    e_rows = EACH // dp * vocab if two_sends else vocab
    own_heads = max(1, d_rows // HEAD_DIM)
    kinds = PHASES if own_heads > 1 else 1
    own_rows = own_heads // kinds * vocab
    vmem = pl.BlockSpec(memory_space=pltpu.VMEM)
    hbm = pl.BlockSpec(memory_space=pl.ANY)
    shape = jax.ShapeDtypeStruct
    sems = lambda *sizes: pltpu.SemaphoreType.DMA(sizes)
    gain, shift = ln_gain[None, :], ln_shift[None, :]
    results = [
        shape((windows, rows, width), BF16),
        shape((d_rows, vocab), F32),
        shape((1, d_rows), F32),
        shape((1, d_rows), F32),
        shape((d_rows, 3 * width), F32),
        shape((d_rows, width), F32),
        shape((d_rows, hidden), F32),
        shape((1, f_rows), F32),
        shape((f_rows, width), F32),
        shape((1, d_rows), F32),
    ]
    held = pl.pallas_call(
        main_kernel,
        in_specs=[hbm] * 12,
        out_specs=[hbm] * len(results),
        out_shape=results,
        scratch_shapes=[pltpu.VMEM(result.shape, result.dtype) for result in results] + [
            pltpu.VMEM((windows + most, HEADS * vocab, rows), BF16),
            pltpu.VMEM((vocab, width), BF16),
            pltpu.VMEM((vocab, width), BF16),
            pltpu.VMEM((HEADS * vocab, width), BF16),
            pltpu.VMEM(((HEADS + 2) * vocab, width), BF16),
            pltpu.VMEM((seq, 2 * windows, rows), jnp.int32),
            pltpu.VMEM((vocab, width), BF16),
            pltpu.VMEM((1, width), F32),
            pltpu.VMEM((1, width), F32),
            pltpu.VMEM((1, some), F32),
            pltpu.VMEM((1, width), F32),
            pltpu.VMEM((windows, rows, width), BF16),
            pltpu.VMEM((3, width, width), BF16),
            pltpu.VMEM((width, width), BF16),
            pltpu.VMEM((width, some), BF16),
            pltpu.VMEM((some, width), BF16),
            pltpu.VMEM((HEADS // GROUP, LANES, 6 * LANES), BF16),
            pltpu.VMEM((windows + most, EACH * vocab, rows), BF16),
            pltpu.VMEM((max(most, 1), EACH * vocab, rows), BF16),
            pltpu.VMEM((windows, vocab, length), BF16),
            pltpu.VMEM((windows, length, LANES), BF16),
            pltpu.VMEM((windows, length, 3 * vocab), F8),
            pltpu.VMEM((HALVES, GROUP * rows, LANES), BF16),
            pltpu.VMEM((HALVES, LANES, length), BF16),
            pltpu.VMEM((HALVES, length, GROUP * rows), BF16),
            pltpu.VMEM((HALVES, 3 * vocab, GROUP * rows), F8),
            pltpu.VMEM((HALVES, 1, GROUP * rows), F32),
            pltpu.VMEM((windows, length, LANES), F32),
            pltpu.VMEM((windows, length, LANES), F32),
            pltpu.VMEM((2, windows, 3 * ROT // 2, length), BF16),
            pltpu.VMEM((3, vocab, width), F32),
            pltpu.VMEM((HEADS * vocab, width), BF16),
            pltpu.VMEM((HEADS * vocab, LANES), F32),
            pltpu.VMEM((PHASES, vocab, 2 * HALVES * LANES), F32),
            pltpu.VMEM((PHASES, vocab, 2 * HALVES * LANES), F32),
            pltpu.VMEM((vocab, width), F32),
            pltpu.VMEM((vocab, some), BF16),
            pltpu.VMEM((vocab, some), F32),
            pltpu.VMEM((dp, vocab, some), BF16),
            pltpu.VMEM((sends, dp, e_rows, width), BF16),
            pltpu.VMEM((sends, e_rows, width), BF16),
            pltpu.VMEM((seq, kinds, own_rows, width), BF16),
            sems(14),
            sems(len(results)),
            sems(seq),
            sems(seq),
            sems(max(most, 1)),
            sems(max(most, 1)),
            sems(max(most, 1)),
            sems(max(most, 1)),
            sems(sends, dp),
            sems(sends, dp),
            sems(seq),
            sems(seq),
            sems(dp),
            sems(dp),
        ]
        + total_scratch(dp, seq, vocab, 2 * width // dp)
        + total_scratch(dp, seq, vocab, width // dp)
        + total_scratch(dp, seq, vocab, 3 * width // dp),
        compiler_params=pltpu.CompilerParams(
            vmem_limit_bytes=60 * 1024 * 1024, collective_id=1, has_side_effects=True),
    )(token_ids, positions, embed, gain, shift, b_up[None, :], b_down[None, :], cotangent, w_qkv, w_out, w_up, w_down)
    outs = pl.pallas_call(
        partial(copy_kernel, len(results)),
        in_specs=[hbm] * len(results),
        out_specs=[hbm] * len(results),
        out_shape=results,
        scratch_shapes=[pltpu.VMEM(result.shape, result.dtype) for result in results]
        + [sems(windows + len(results))] * 2,
        compiler_params=pltpu.CompilerParams(vmem_limit_bytes=60 * 1024 * 1024),
    )(*held)
    flat = lambda v: v.reshape(-1)
    return (
        outs[0], outs[1], flat(outs[2]), flat(outs[3]), outs[4], outs[5], outs[6], flat(outs[7]), outs[8], flat(outs[9]),
    )


def solution(mesh):
    in_specs = (P("dp", "seq"), P("dp", "seq")) + (P(),) * 9 + (P("dp", "seq", None),)
    both = ("dp", "seq")
    out_specs = (
        P("dp", "seq", None),
        P(both, None),
        P(both),
        P(both),
        P(both, None),
        P(both, None),
        P(both, None),
        P(both),
        P(both, None),
        P(both),
    )
    return jax.shard_map(per_device, mesh=mesh, in_specs=in_specs, out_specs=out_specs, check_vma=False)
```

```python
from functools import partial

import jax
import jax.numpy as jnp
from jax import lax
from jax.experimental import pallas as pl
from jax.experimental.pallas import tpu as pltpu
from jax.sharding import PartitionSpec as P

HEADS = 16
HEAD_DIM = 64
ROT = 32
GROUP = 4
PHASES = 2
EACH = HEADS // PHASES
HALVES = EACH // GROUP
LANES = 128
ln_epsilon = 1e-05
LOG2E = 1.4426950408889634
F32 = jnp.float32
BF16 = jnp.bfloat16
F8 = jnp.float8_e4m3fn
MESH = pl.DeviceIdType.MESH


def dot(a, b):
    return lax.dot_general(a, b, (((1,), (0,)), ((), ())), preferred_element_type=F32)


def dot_t(a, b):
    return lax.dot_general(a, b, (((1,), (1,)), ((), ())), preferred_element_type=F32)


def t_dot(a, b):
    return lax.dot_general(a, b, (((0,), (0,)), ((), ())), preferred_element_type=F32)


def iota(shape, axis):
    return lax.broadcasted_iota(jnp.int32, shape, axis)


def ones_where(mask):
    return mask.astype(F32).astype(BF16)


def terms_of(value, count):
    parts = []
    for _ in range(count):
        high = value.astype(BF16)
        parts.append(high)
        value = value - high.astype(F32)
    return jnp.concatenate(parts, axis=0)


def roll_pairs(values):
    even = iota(values.shape, 1) % 2 == 0
    return jnp.where(even, -pltpu.roll(values, values.shape[1] - 1, 1), pltpu.roll(values, 1, 1))


def gelu_and_slope(u):
    c = 0.7978845608028654
    t = jnp.tanh(c * (u + 0.044715 * u * u * u))
    return 0.5 * u * (1.0 + t), 0.5 * (1.0 + t) + 0.5 * u * (1.0 - t * t) * c * (1.0 + 3 * 0.044715 * u * u)


def greet(axes):
    barrier = pltpu.get_barrier_semaphore()
    count = 0
    for axis in axes:
        size = lax.axis_size(axis)
        me = lax.axis_index(axis)
        for step in range(1, size):
            pl.semaphore_signal(barrier, inc=1, device_id={axis: lax.rem(me + step, size)}, device_id_type=MESH)
        count += size - 1
    return count


def to_all(axis, source, target, send_sem, recv_sem):
    size = lax.axis_size(axis)
    me = lax.axis_index(axis)
    copies = []
    for step in range(1, size):
        other = lax.rem(me + step, size)
        copies.append(pltpu.make_async_remote_copy(
            src_ref=source(other), dst_ref=target(step), send_sem=send_sem.at[step], recv_sem=recv_sem.at[step],
            device_id={axis: other}, device_id_type=MESH,
        ))
    return copies


def start_all(copies):
    for copy in copies:
        copy.start()


def arrived(copies):
    for copy in copies:
        copy.wait_recv()


class Total:
    def __init__(self, own, low, first, part, second, whole, sems):
        self.own, self.low, self.first, self.part = own, low, first, part
        self.second, self.whole, self.sems = second, whole, sems
        self.columns = low.shape[2]

    def load(self, value):
        for at in range(self.own.shape[0]):
            piece = value[:, at * self.columns : (at + 1) * self.columns]
            self.own[at] = piece
            self.low[at] = piece.astype(BF16)

    def one(self):
        return to_all("dp", lambda other: self.low.at[other], lambda step: self.first.at[step], *self.sems[0:2])

    def two(self):
        return to_all("seq", lambda other: self.part, lambda step: self.second.at[step], *self.sems[2:4])

    def three(self):
        column = lax.axis_index("dp")
        return to_all("dp", lambda other: self.whole.at[column], lambda step: self.whole.at[column], *self.sems[4:6])

    def step1(self):
        start_all(self.one())

    def step2(self):
        column = lax.axis_index("dp")
        arrived(self.one())
        value = self.own[column]
        for step in range(1, lax.axis_size("dp")):
            value += self.first[step].astype(F32)
        self.own[column] = value
        self.part[...] = value.astype(BF16)
        start_all(self.two())

    def step3(self):
        column = lax.axis_index("dp")
        arrived(self.two())
        value = self.own[column]
        for step in range(1, lax.axis_size("seq")):
            value += self.second[step].astype(F32)
        self.whole[column] = value.astype(BF16)
        start_all(self.three())

    def finish(self):
        arrived(self.three())

    def sums(self, start, size):
        whole = jnp.concatenate([self.whole[at] for at in range(self.whole.shape[0])], axis=1)
        return whole[:, start : start + size]

    def end(self):
        for copies in (self.one(), self.two(), self.three()):
            for copy in copies:
                copy.wait_send()


def total_scratch(dp, seq, rows, columns):
    return [
        pltpu.VMEM((dp, rows, columns), F32),
        pltpu.VMEM((dp, rows, columns), BF16),
        pltpu.VMEM((dp, rows, columns), BF16),
        pltpu.VMEM((rows, columns), BF16),
        pltpu.VMEM((seq, rows, columns), BF16),
        pltpu.VMEM((dp, rows, columns), BF16),
    ] + [pltpu.SemaphoreType.DMA((size,)) for size in (dp, dp, seq, seq, dp, dp)]


def layer_norm_rows(embed):
    inputs = embed.astype(F32)
    center = inputs - jnp.mean(inputs, axis=1, keepdims=True)
    spread = jnp.mean(center * center, axis=1, keepdims=True)
    rstd = lax.rsqrt(spread + ln_epsilon)
    return inputs, center * rstd, rstd


def head_at(slot):
    return slot % EACH * PHASES + slot // EACH


def gifts(shards, windows):
    counts = []
    for place in range(shards):
        mirror = shards - 1 - place
        spare = PHASES * windows * (place - mirror) / (2.0 * (place + 2))
        counts.append(min(windows, max(0, int(spare + 0.5))))
    return counts


def hooks(shards, windows, count):
    gives = gifts(shards, windows)
    found = []
    for place in range(shards):
        mirror = shards - 1 - place
        costs = [place + 2] * (windows - gives[place]) + [mirror + 2] * gives[mirror] + [place + 2] * windows
        row = []
        for at in range(count):
            spent, step = 0, 0
            while step < len(costs) - 1 and spent + costs[step] < (at + 1) * (shards + 1):
                spent += costs[step]
                step += 1
            row.append(step)
        found.append(row)
    return found


def main_kernel(
    ids_hbm, positions_hbm, embed_hbm, gain_hbm, shift_hbm, b_up_hbm, b_down_hbm, cot_hbm, w_qkv_hbm, w_out_hbm,
    w_up_hbm, w_down_hbm,
    output_hbm, embed_grad_hbm, gain_grad_hbm, shift_grad_hbm, qkv_grad_hbm, out_grad_hbm, up_grad_hbm,
    up_bias_grad_hbm, down_grad_hbm, down_bias_grad_hbm,
    output_ref, embed_grad_ref, gain_grad_ref, shift_grad_ref, qkv_grad_ref, out_grad_ref, up_grad_ref,
    up_bias_grad_ref, down_grad_ref, down_bias_grad_ref,
    po_ref, normed_ref, values_ref, mixed_ref, base_ref,
    both, embed_ref, gain_ref, shift_ref, b_up_ref, b_down_ref, cot_ref, w_qkv, w_out, w_up, w_down,
    tab_ref, grad_ref, po_in, oh_t_ref, oh_ref, oh8_ref, own_ref, keys_t_ref, weights_ref, center_ref, back_ref, cos_ref, sin_ref, turn_ref, projected_ref, low_ref, m_ref, agg_q_ref, agg_k_ref,
    cot_own_ref, act_ref, slope_ref, d_up_ref, e_in, e_part, e_in2,
    load_sem, store_sem, seq_send, seq_recv, gift_send, gift_recv, back_send, back_recv, e1_send, e1_recv, e2_send, e2_recv,
    d_up_send, d_up_recv, *totals,
):
    shards, twice_windows, rows = both.shape
    windows = twice_windows // 2
    vocab, width = embed_ref.shape
    length = shards * rows
    some = w_up.shape[1]
    dp = lax.axis_size("dp")
    column, place = lax.axis_index("dp"), lax.axis_index("seq")
    mirror = shards - 1 - place
    index = column * shards + place
    pairs = ROT // 2
    quarter = LANES // GROUP
    per_phase = EACH * vocab
    give_of = gifts(shards, windows)
    most = max(give_of)
    pick_count = lambda where: sum(
        jnp.where(where == at, jnp.int32(count), jnp.int32(0)) for at, count in enumerate(give_of) if count)
    give, take = pick_count(place), pick_count(mirror)

    small = [
        pltpu.make_async_copy(source, target, load_sem.at[at])
        for at, (source, target) in enumerate((
            (ids_hbm, both.at[place, pl.ds(0, windows), :]),
            (positions_hbm, both.at[place, pl.ds(windows, windows), :]),
            (embed_hbm, embed_ref), (gain_hbm, gain_ref), (shift_hbm, shift_ref)))
    ]
    qkv_load = lambda at: pltpu.make_async_copy(
        w_qkv_hbm.at[:, pl.ds(pl.multiple_of(at * width, width), width)], w_qkv.at[at], load_sem.at[5 + at])
    out_load = pltpu.make_async_copy(w_out_hbm, w_out, load_sem.at[8])
    cot_load = pltpu.make_async_copy(cot_hbm, cot_ref, load_sem.at[9])
    hidden_at = pl.ds(pl.multiple_of(column * some, some), some)
    mlp_loads = [
        pltpu.make_async_copy(source, target, load_sem.at[10 + at])
        for at, (source, target) in enumerate((
            (b_up_hbm.at[:, hidden_at], b_up_ref), (w_up_hbm.at[:, hidden_at], w_up),
            (w_down_hbm.at[hidden_at, :], w_down), (b_down_hbm, b_down_ref)))
    ]
    start_all(small + [qkv_load(at) for at in range(3)] + [cot_load, out_load] + mlp_loads)
    guests = greet(("dp", "seq"))
    for copy in small:
        copy.wait()
    _, xhat, _ = layer_norm_rows(embed_ref[...])
    normed = (xhat * gain_ref[...] + shift_ref[...]).astype(BF16)
    normed_ref[...] = normed

    def project(at, _):
        qkv_load(at).wait()
        projected_ref[at] = dot(normed_ref[...], w_qkv[at])
        return 0

    lax.fori_loop(0, 3, project, 0)
    pl.semaphore_wait(pltpu.get_barrier_semaphore(), guests)
    exchange = to_all("seq", lambda other: both.at[place], lambda step: both.at[place], seq_send, seq_recv)
    start_all(exchange)
    projected = [projected_ref[at] for at in range(3)]
    values = projected[2].astype(BF16)
    values_ref[...] = values
    fill = jnp.zeros((LANES - 3 * vocab, 6 * LANES), BF16)
    for group in range(HEADS // GROUP):
        columns = []
        for table in projected[:2]:
            heads = [head_at(group * GROUP + h) * HEAD_DIM for h in range(GROUP)]
            turned = jnp.concatenate([table[:, h : h + ROT] for h in heads], axis=1)
            plain = jnp.concatenate([table[:, h + ROT : h + HEAD_DIM] for h in heads], axis=1)
            columns += [turned, plain, roll_pairs(turned)]
        tab_ref[group] = jnp.concatenate([terms_of(jnp.concatenate(columns, axis=1), 3), fill], axis=0)
    out_load.wait()
    lane_head = iota((vocab, LANES), 1) // HEAD_DIM
    for at in range(EACH):
        part = values[:, at * LANES : (at + 1) * LANES]
        none = jnp.zeros_like(part)
        stacked = jnp.concatenate([jnp.where(lane_head == h, part, none) for h in range(PHASES)], axis=0)
        mixed = dot(stacked, w_out[at * LANES : (at + 1) * LANES, :]).astype(BF16)
        for h in range(PHASES):
            mixed_ref[(h * EACH + at) * vocab : (h * EACH + at + 1) * vocab, :] = mixed[h * vocab : (h + 1) * vocab, :]
    cot_load.wait()
    give_copy = lambda k: pltpu.make_async_remote_copy(
        src_ref=grad_ref.at[k], dst_ref=grad_ref.at[windows + k], send_sem=gift_send.at[k], recv_sem=gift_recv.at[k],
        device_id={"seq": mirror}, device_id_type=MESH)
    back_copy = lambda k: pltpu.make_async_remote_copy(
        src_ref=po_ref.at[windows + k, pl.ds(0, per_phase), :], dst_ref=po_in.at[k], send_sem=back_send.at[k],
        recv_sem=back_recv.at[k], device_id={"seq": mirror}, device_id_type=MESH)

    def grads_of(phase):
        mixed = mixed_ref[pl.ds(pl.multiple_of(phase * per_phase, per_phase), per_phase), :]

        def step(window, _):
            grad_ref[window] = dot_t(mixed, cot_ref[window]).astype(BF16)
            return 0

        lax.fori_loop(0, windows, step, 0)

    grads_of(0)
    for k in range(most):
        @pl.when(k < give)
        def _(k=k):
            give_copy(k).start()


    arrived(exchange)
    inverse = sum(
        jnp.where(iota((pairs, 1), 0) == p, F32(10000.0 ** (-2.0 * p / ROT)), 0.0) for p in range(pairs))
    tiles = ones_where(iota((vocab, LANES), 1) % vocab == iota((vocab, LANES), 0))
    spread = ones_where(iota((3 * pairs, LANES), 0) % pairs == iota((3 * pairs, LANES), 1) % ROT // 2)
    spread_t = ones_where(iota((LANES, 3 * pairs), 1) % pairs == iota((LANES, 3 * pairs), 0) % ROT // 2)
    cot_total, d_total, sum_total = (Total(*totals[at : at + 6], totals[at + 6 : at + 12]) for at in (0, 12, 24))

    def prepare(window, cot_sum):
        row = lambda at: jnp.concatenate([both[s, pl.ds(at, 1), :] for s in range(shards)], axis=1)
        oh_t = ones_where(iota((vocab, length), 0) == row(window))
        oh_t_ref[window] = oh_t
        tiled = t_dot(oh_t, tiles)
        oh_ref[window] = tiled.astype(BF16)
        oh8_ref[window] = tiled[:, : 3 * vocab].astype(F8)
        angles = inverse * row(window + windows).astype(F32)
        for at, (value, ref) in enumerate(((jnp.cos(angles), cos_ref), (jnp.sin(angles), sin_ref))):
            terms = terms_of(value, 3)
            turn_ref[at, window] = terms
            ref[window] = t_dot(terms, spread)
        own_t = ones_where(iota((vocab, rows), 0) == both[place, pl.ds(window, 1), :])
        return cot_sum + dot(own_t, cot_ref[window])

    cot_sum = lax.fori_loop(0, windows, prepare, jnp.zeros((vocab, width), F32))
    d_rows = width // (dp * shards)
    cot_own_ref[...] = cot_sum
    for ref in (m_ref, agg_q_ref, agg_k_ref):
        ref[...] = jnp.zeros_like(ref)

    halves = range(HALVES)

    def forward(part, phase, window, slot, keep):
        first = part * rows
        span = first + rows
        lane_head = iota((rows, 2 * LANES), 1) % LANES // quarter
        owns, keys, keys_t = [], [], []
        cos, sin = cos_ref[window, :span, :], sin_ref[window, :span, :]
        for half in halves:
            table = tab_ref[phase * HALVES + half]
            raw = dot(oh_ref[window, first:span, :], table[:, : 3 * LANES])
            turned = raw[:, :LANES] * cos[first:, :] + raw[:, 2 * LANES :] * sin[first:, :]
            query = jnp.concatenate([turned, raw[:, LANES : 2 * LANES]], axis=1).astype(BF16)
            owns.append(jnp.concatenate(
                [jnp.where(lane_head == head, query, jnp.zeros_like(query)) for head in range(GROUP)], axis=0))
            raw = dot(oh_ref[window, :span, :], table[:, 3 * LANES :])
            turned = (raw[:, :LANES] * cos + raw[:, 2 * LANES :] * sin).astype(BF16)
            keys.append(jnp.concatenate([turned, raw[:, LANES : 2 * LANES].astype(BF16)], axis=1))
            keys_t.append(turned.T)
        grad = grad_ref[slot].astype(F32)
        lanes_of = lambda v, half: jnp.concatenate(
            [v[(half * GROUP + h) * vocab : (half * GROUP + h + 1) * vocab, :] for h in range(GROUP)], axis=1)
        rows_of = lambda v: [v[:, h * rows : (h + 1) * rows] for h in range(GROUP)]
        kept = iota((rows, GROUP * rows), 0) <= iota((rows, GROUP * rows), 1) % rows
        weights = []
        for half in halves:
            scores = dot_t(keys[half], owns[half]) * (HEAD_DIM**-0.5 * LOG2E)
            last = jnp.where(kept, scores[first:, :], -1e30)
            scores = jnp.concatenate([scores[:first, :], last], axis=0) if first else last
            weights.append(jnp.exp2(scores - jnp.max(scores, axis=0, keepdims=True)).astype(BF16))
        shares, terms, centers, backs = [], [], [], []
        for half in halves:
            summed = dot(oh_t_ref[window, :, :span], weights[half])
            inverse = 1.0 / jnp.sum(summed, axis=0, keepdims=True)
            share = summed * inverse
            own_grad = lanes_of(grad, half)
            off = own_grad - jnp.sum(share * own_grad, axis=0, keepdims=True)
            shares += rows_of(share)
            terms += rows_of(share * off)
            off = off * inverse
            power = 6.0 - jnp.floor(jnp.log2(jnp.maximum(jnp.max(jnp.abs(off), axis=0, keepdims=True), 1e-30)))
            backs.append(jnp.exp2(-power))
            off = off * jnp.exp2(power)
            pieces = []
            for _ in range(3):
                pieces.append(off.astype(F8))
                off = off - pieces[-1].astype(F32)
            centers.append(jnp.concatenate(pieces, axis=0))
        at = pl.ds(pl.multiple_of(phase * per_phase, per_phase), per_phase)
        po_ref[slot, at, :] = jnp.concatenate(shares, axis=0).astype(BF16)
        m_ref[at, :] += dot(jnp.concatenate(terms, axis=0).astype(BF16), oh_ref[window, first:span, :])
        owns = [own[:, :LANES] for own in owns]
        if not keep:
            return owns, keys_t, weights, centers, backs
        for half in halves:
            own_ref[half] = owns[half]
            keys_t_ref[half, :, :span] = keys_t[half]
            weights_ref[half, :span, :] = weights[half]
            center_ref[half] = centers[half]
            back_ref[half] = backs[half]

    def kept_of(part):
        span = (part + 1) * rows
        return (
            [own_ref[half] for half in halves], [keys_t_ref[half, :, :span] for half in halves],
            [weights_ref[half, :span, :] for half in halves], [center_ref[half] for half in halves],
            [back_ref[half] for half in halves])

    def backward(part, phase, window, held):
        owns, keys_t, weights, centers, backs = held
        first = part * rows
        span = first + rows
        cos, sin = cos_ref[window, :span, :], sin_ref[window, :span, :]
        d_query, d_keys = [], []
        for half in halves:
            back = backs[half]
            d_scores = (
                weights[half].astype(F32) * dot(oh8_ref[window, :span, :], centers[half])
            ).astype(BF16)
            for head in range(GROUP):
                d_query.append(
                    dot(keys_t[half][head * quarter : (head + 1) * quarter, :],
                        d_scores[:, head * rows : (head + 1) * rows])
                    * back[:, head * rows : (head + 1) * rows])
            own = owns[half].astype(F32) * jnp.broadcast_to(back, (LANES, GROUP * rows)).T
            d_keys.append(dot(d_scores, own.astype(BF16)))
        parts = [(d * turn).astype(BF16) for turn in (cos, sin) for d in d_keys]
        agg_k_ref[phase] += dot(oh_t_ref[window, :, :span], jnp.concatenate(parts, axis=1))
        d_query = [jnp.concatenate(d_query[h : h + GROUP], axis=0) for h in range(0, EACH, GROUP)]
        turns = [dot(spread_t, turn_ref[at, window, :, first:span]) for at in range(2)]
        parts = [(d * turn).astype(BF16) for turn in turns for d in d_query]
        agg_q_ref[phase] += dot_t(oh_t_ref[window, :, first:span], jnp.concatenate(parts, axis=0))

    two_sends = e_in.shape[0] > 1
    e_rows = e_part.shape[1]

    def mixes_of(phase):
        at = pl.ds(pl.multiple_of(phase * per_phase, per_phase), per_phase)
        total = dot(po_ref[0, at, :], cot_ref[0])
        for window in range(1, windows):
            total += dot(po_ref[window, at, :], cot_ref[window])
        low_ref[at, :] = total.astype(BF16)

    def e_slice(phase, other):
        if two_sends:
            start = phase * per_phase + other * e_rows
        else:
            head = other * HEADS // dp
            start = (head % PHASES * EACH + head // PHASES) * vocab
        return pl.ds(pl.multiple_of(start, vocab), e_rows)

    def e1(phase):
        return to_all(
            "dp", lambda other: low_ref.at[e_slice(phase, other), :], lambda step: e_in.at[phase, step],
            e1_send.at[phase], e1_recv.at[phase])

    first_place = jnp.where(place == 0, F32(1.0), F32(0.0))

    def mlp_forward():
        for copy in mlp_loads:
            copy.wait()
        act, slope = gelu_and_slope(dot(normed_ref[...], w_up[...]) + b_up_ref[...])
        act_ref[...] = act.astype(BF16)
        slope_ref[...] = slope
        part = jnp.concatenate([cot_own_ref[...], dot(act_ref[...], w_down[...]) * first_place], axis=1)
        cot_total.load(part)
        cot_total.step1()

    def d_up_copies():
        return to_all("dp", lambda other: d_up_ref.at[column], lambda step: d_up_ref.at[column], d_up_send, d_up_recv)

    def mlp_backward():
        cot_total.finish()
        d_up = (slope_ref[...] * dot_t(cot_total.sums(0, width), w_down[...])).astype(BF16)
        d_up_ref[column] = d_up
        start_all(d_up_copies())
        d_total.load(dot_t(d_up, w_up[...]) * first_place)
        d_total.step1()

    turn = windows - give + take
    steps = turn + windows
    mlp_forward()
    works = (cot_total.step2, cot_total.step3, mlp_backward, d_total.step2, d_total.step3)
    hooks_of = hooks(shards, windows, len(works))

    def step(at, _):
        phase = jnp.where(at < turn, jnp.int32(0), jnp.int32(1))
        taken = jnp.where(at < windows - give, jnp.int32(0), jnp.int32(1)) * (1 - phase)
        window = phase * (at - turn) + (1 - phase) * ((1 - taken) * (give + at) + taken * (at - windows + give))
        slot = window + taken * windows
        whose = taken * mirror + (1 - taken) * place
        for k in range(most):
            @pl.when((k < take) & (at == windows - give + k))
            def _(k=k):
                give_copy(k).wait_recv()

        for part in range(shards):
            @pl.when(whose == part)
            def _(part=part):
                backward(part, phase, window, forward(part, phase, window, slot, False))

        @pl.when(at >= steps - 2)
        def _():
            done = at - (steps - 2)

            @pl.when(done == 0)
            def _():
                for k in range(most):
                    @pl.when(k < give)
                    def _(k=k):
                        back_copy(k).wait_recv()
                        po_ref[k, :per_phase, :] = po_in[k]

            mixes_of(done)
            if two_sends:
                @pl.when(done == 0)
                def _():
                    start_all(e1(0))

        for k in range(most):
            @pl.when((k < take) & (at == windows - give + k))
            def _(k=k):
                back_copy(k).start()

        @pl.when(at == turn - 1)
        def _():
            for k in range(most):
                @pl.when(k < give)
                def _(k=k):
                    give_copy(k).wait_send()
            grads_of(1)

        for number, work in enumerate(works):
            when = sum(jnp.where(place == p, jnp.int32(hooks_of[p][number]), jnp.int32(0)) for p in range(shards))
            pl.when(at == when)(work)

        return 0

    lax.fori_loop(0, steps, step, 0)
    lane_block = iota((vocab, LANES), 1) // quarter
    of_head = [[None] * HEADS for _ in range(3)]
    for group in range(HEADS // GROUP):
        phase, half = divmod(group, HALVES)
        query_plain = tab_ref[group, :vocab, LANES : 2 * LANES]
        key_plain = tab_ref[group, :vocab, 4 * LANES : 5 * LANES]
        mass = m_ref[group * GROUP * vocab : (group + 1) * GROUP * vocab, :].astype(BF16)
        block = iota((GROUP * vocab, LANES), 0) // vocab == iota((GROUP * vocab, LANES), 1) // quarter
        stacked = jnp.concatenate([key_plain] * GROUP, axis=0)
        plain_q = t_dot(mass, jnp.where(block, stacked, jnp.zeros_like(stacked)))[:vocab, :]
        mixed_k = dot(mass[:, :vocab], query_plain)
        plain_k = sum(
            jnp.where(lane_block == h, mixed_k[h * vocab : (h + 1) * vocab, :], 0.0) for h in range(GROUP))
        for at, ref, plain in ((0, agg_q_ref, plain_q), (1, agg_k_ref, plain_k)):
            cosine = ref[phase, :, half * LANES : (half + 1) * LANES]
            sine = ref[phase, :, (HALVES + half) * LANES : (HALVES + half + 1) * LANES]
            turned = cosine - roll_pairs(sine)
            for h in range(GROUP):
                of_head[at][head_at(group * GROUP + h)] = jnp.concatenate(
                    [turned[:, h * quarter : (h + 1) * quarter], plain[:, h * quarter : (h + 1) * quarter]], axis=1)
    columns = [jnp.concatenate(of_head[at], axis=1) * HEAD_DIM**-0.5 for at in range(2)]
    pieces = []
    lane_head = iota((vocab, LANES), 1) // HEAD_DIM
    for at in range(EACH):
        low = jnp.concatenate(
            [low_ref[(h * EACH + at) * vocab : (h * EACH + at + 1) * vocab, :] for h in range(PHASES)], axis=0)
        both_heads = dot_t(low, w_out[at * LANES : (at + 1) * LANES, :])
        pieces.append(jnp.where(lane_head == 0, both_heads[:vocab, :], both_heads[vocab:, :]))
    columns = jnp.concatenate(columns + pieces, axis=1)
    sum_total.load(columns)
    sum_total.step1()
    start_all(e1(1 if two_sends else 0))

    stores = [
        pltpu.make_async_copy(source, target, store_sem.at[at])
        for at, (source, target) in enumerate((
            (output_ref, output_hbm), (embed_grad_ref, embed_grad_hbm), (gain_grad_ref, gain_grad_hbm),
            (shift_grad_ref, shift_grad_hbm), (qkv_grad_ref, qkv_grad_hbm), (out_grad_ref, out_grad_hbm),
            (up_grad_ref, up_grad_hbm), (up_bias_grad_ref, up_bias_grad_hbm), (down_grad_ref, down_grad_hbm),
            (down_bias_grad_ref, down_bias_grad_hbm)))
    ]
    inputs, xhat, rstd = layer_norm_rows(embed_ref[...])
    base_ref[: HEADS * vocab, :] = mixed_ref[...]
    base_ref[HEADS * vocab :, :] = terms_of(inputs + cot_total.sums(width, width).astype(F32) + b_down_ref[...], 2)

    def finish_window(window, _):
        oh_t = ones_where(iota((vocab, rows), 0) == both[place, pl.ds(window, 1), :])
        output_ref[window] = t_dot(jnp.concatenate([po_ref[window], oh_t, oh_t], axis=0), base_ref[...]).astype(BF16)
        return 0

    lax.fori_loop(0, windows // 2, finish_window, 0)
    sum_total.step2()
    lax.fori_loop(windows // 2, windows, finish_window, 0)
    stores[0].start()
    f_rows = down_grad_ref.shape[0]
    cot_sum = cot_total.sums(0, width)
    pick = ones_where(iota((d_rows, width), 1) == iota((d_rows, width), 0) + index * d_rows)
    pick_f = ones_where(iota((f_rows, some), 1) == iota((f_rows, some), 0) + place * f_rows)
    normed_own = dot_t(pick, normed_ref[...]).astype(BF16)
    down_grad_ref[...] = dot(dot_t(pick_f, act_ref[...]).astype(BF16), cot_sum)
    stores[8].start()
    up_bias_grad_ref[...] = jnp.sum(dot_t(d_up_ref[column], pick_f), axis=0, keepdims=True)
    stores[7].start()
    own_columns = lambda value: jnp.sum(dot_t(terms_of(value, 3), pick), axis=0, keepdims=True)
    down_bias_grad_ref[...] = own_columns(cot_sum.astype(F32))
    stores[9].start()
    sum_total.step3()
    for phase in range(e_in.shape[0]):
        arrived(e1(phase))
        total = low_ref[e_slice(phase, column), :].astype(F32)
        for step in range(1, dp):
            total += e_in[phase, step].astype(F32)
        e_part[phase] = total.astype(BF16)
    kinds, own_rows = e_in2.shape[1:3]

    def e_own(other):
        head = (column * shards + other) * d_rows // HEAD_DIM - column * HEADS // dp
        if not two_sends:
            return pl.ds(0, 1), pl.ds(0, own_rows)
        first_kind = 0 if kinds == PHASES else lax.rem(head, PHASES)
        return pl.ds(first_kind, kinds), pl.ds(pl.multiple_of(head // PHASES * vocab, vocab), own_rows)

    e2 = to_all("seq", lambda other: e_part.at[e_own(other)], lambda step: e_in2.at[step], e2_send, e2_recv)
    start_all(e2)
    arrived(d_up_copies())
    for at in range(dp):
        up_grad_ref[:, at * some : (at + 1) * some] = dot(normed_own, d_up_ref[at])
    stores[6].start()
    d_total.finish()

    sum_total.finish()
    sums = sum_total.sums(0, 3 * width)
    d_normed = d_total.sums(0, width).astype(F32)
    for at in range(3):
        d_normed += dot_t(sums[:, at * width : (at + 1) * width], w_qkv[at])
    qkv_grad_ref[...] = dot(normed_own, sums)
    stores[4].start()
    gain_grad_ref[...] = own_columns(d_normed * xhat)
    stores[2].start()
    shift_grad_ref[...] = own_columns(d_normed)
    stores[3].start()
    scaled = d_normed * gain_ref[...]
    d_input = cot_sum.astype(F32) + rstd * (
        scaled
        - jnp.mean(scaled, axis=1, keepdims=True)
        - xhat * jnp.mean(scaled * xhat, axis=1, keepdims=True)
    )
    wide = dot_t(pick, terms_of(d_input, 3))
    embed_grad_ref[...] = wide[:, :vocab] + wide[:, vocab : 2 * vocab] + wide[:, 2 * vocab :]
    stores[1].start()
    arrived(e2)
    total = e_part[e_own(place)].astype(F32)
    for step in range(1, shards):
        total += e_in2[step].astype(F32)
    own = total.astype(BF16).reshape(kinds * own_rows, width)
    values_own = dot_t(pick, values_ref[...]).astype(BF16)
    row_head = iota((d_rows, vocab), 0) // HEAD_DIM
    left = jnp.concatenate([
        jnp.where(row_head == at * kinds + kind, values_own, jnp.zeros_like(values_own))
        for kind in range(kinds) for at in range(own_rows // vocab)], axis=1)
    out_grad_ref[...] = dot(left, own)
    stores[5].start()
    for copies in [exchange, e2, d_up_copies()] + [e1(phase) for phase in range(e_in.shape[0])]:
        for copy in copies:
            copy.wait_send()
    for k in range(most):
        @pl.when(k < take)
        def _(k=k):
            back_copy(k).wait_send()
    for total in (cot_total, d_total, sum_total):
        total.end()
    for store in stores:
        store.wait()


def copy_kernel(count, *refs):
    sources, targets, held = refs[:count], refs[count : 2 * count], refs[2 * count : 3 * count]
    in_sem, out_sem = refs[3 * count :]
    pieces = []
    for source, target, through in zip(sources, targets, held):
        if len(source.shape) == 3:
            pieces += [(source.at[at], through.at[at], target.at[at]) for at in range(source.shape[0])]
        else:
            pieces.append((source, through, target))
    loads = [pltpu.make_async_copy(s, t, in_sem.at[at]) for at, (s, t, _) in enumerate(pieces)]
    stores = [pltpu.make_async_copy(t, o, out_sem.at[at]) for at, (_, t, o) in enumerate(pieces)]
    start_all(loads)
    for load, store in zip(loads, stores):
        load.wait()
        store.start()
    for store in stores:
        store.wait()


def per_device(
    token_ids, positions, embed, ln_gain, ln_shift, w_qkv, w_out, w_up, b_up, w_down, b_down, cotangent
):
    vocab, width = embed.shape
    hidden = w_up.shape[1]
    windows, rows = token_ids.shape
    dp, seq = lax.axis_size("dp"), lax.axis_size("seq")
    length = seq * rows
    d_rows, f_rows = width // (dp * seq), hidden // (dp * seq)
    some = hidden // dp
    most = max(gifts(seq, windows))
    two_sends = dp <= EACH
    sends = PHASES if two_sends else 1
    e_rows = EACH // dp * vocab if two_sends else vocab
    own_heads = max(1, d_rows // HEAD_DIM)
    kinds = PHASES if own_heads > 1 else 1
    own_rows = own_heads // kinds * vocab
    vmem = pl.BlockSpec(memory_space=pltpu.VMEM)
    hbm = pl.BlockSpec(memory_space=pl.ANY)
    shape = jax.ShapeDtypeStruct
    sems = lambda *sizes: pltpu.SemaphoreType.DMA(sizes)
    gain, shift = ln_gain[None, :], ln_shift[None, :]
    results = [
        shape((windows, rows, width), BF16),
        shape((d_rows, vocab), F32),
        shape((1, d_rows), F32),
        shape((1, d_rows), F32),
        shape((d_rows, 3 * width), F32),
        shape((d_rows, width), F32),
        shape((d_rows, hidden), F32),
        shape((1, f_rows), F32),
        shape((f_rows, width), F32),
        shape((1, d_rows), F32),
    ]
    held = pl.pallas_call(
        main_kernel,
        in_specs=[hbm] * 12,
        out_specs=[hbm] * len(results),
        out_shape=results,
        scratch_shapes=[pltpu.VMEM(result.shape, result.dtype) for result in results] + [
            pltpu.VMEM((windows + most, HEADS * vocab, rows), BF16),
            pltpu.VMEM((vocab, width), BF16),
            pltpu.VMEM((vocab, width), BF16),
            pltpu.VMEM((HEADS * vocab, width), BF16),
            pltpu.VMEM(((HEADS + 2) * vocab, width), BF16),
            pltpu.VMEM((seq, 2 * windows, rows), jnp.int32),
            pltpu.VMEM((vocab, width), BF16),
            pltpu.VMEM((1, width), F32),
            pltpu.VMEM((1, width), F32),
            pltpu.VMEM((1, some), F32),
            pltpu.VMEM((1, width), F32),
            pltpu.VMEM((windows, rows, width), BF16),
            pltpu.VMEM((3, width, width), BF16),
            pltpu.VMEM((width, width), BF16),
            pltpu.VMEM((width, some), BF16),
            pltpu.VMEM((some, width), BF16),
            pltpu.VMEM((HEADS // GROUP, LANES, 6 * LANES), BF16),
            pltpu.VMEM((windows + most, EACH * vocab, rows), BF16),
            pltpu.VMEM((max(most, 1), EACH * vocab, rows), BF16),
            pltpu.VMEM((windows, vocab, length), BF16),
            pltpu.VMEM((windows, length, LANES), BF16),
            pltpu.VMEM((windows, length, 3 * vocab), F8),
            pltpu.VMEM((HALVES, GROUP * rows, LANES), BF16),
            pltpu.VMEM((HALVES, LANES, length), BF16),
            pltpu.VMEM((HALVES, length, GROUP * rows), BF16),
            pltpu.VMEM((HALVES, 3 * vocab, GROUP * rows), F8),
            pltpu.VMEM((HALVES, 1, GROUP * rows), F32),
            pltpu.VMEM((windows, length, LANES), F32),
            pltpu.VMEM((windows, length, LANES), F32),
            pltpu.VMEM((2, windows, 3 * ROT // 2, length), BF16),
            pltpu.VMEM((3, vocab, width), F32),
            pltpu.VMEM((HEADS * vocab, width), BF16),
            pltpu.VMEM((HEADS * vocab, LANES), F32),
            pltpu.VMEM((PHASES, vocab, 2 * HALVES * LANES), F32),
            pltpu.VMEM((PHASES, vocab, 2 * HALVES * LANES), F32),
            pltpu.VMEM((vocab, width), F32),
            pltpu.VMEM((vocab, some), BF16),
            pltpu.VMEM((vocab, some), F32),
            pltpu.VMEM((dp, vocab, some), BF16),
            pltpu.VMEM((sends, dp, e_rows, width), BF16),
            pltpu.VMEM((sends, e_rows, width), BF16),
            pltpu.VMEM((seq, kinds, own_rows, width), BF16),
            sems(14),
            sems(len(results)),
            sems(seq),
            sems(seq),
            sems(max(most, 1)),
            sems(max(most, 1)),
            sems(max(most, 1)),
            sems(max(most, 1)),
            sems(sends, dp),
            sems(sends, dp),
            sems(seq),
            sems(seq),
            sems(dp),
            sems(dp),
        ]
        + total_scratch(dp, seq, vocab, 2 * width // dp)
        + total_scratch(dp, seq, vocab, width // dp)
        + total_scratch(dp, seq, vocab, 3 * width // dp),
        compiler_params=pltpu.CompilerParams(
            vmem_limit_bytes=60 * 1024 * 1024, collective_id=1, has_side_effects=True),
    )(token_ids, positions, embed, gain, shift, b_up[None, :], b_down[None, :], cotangent, w_qkv, w_out, w_up, w_down)
    outs = pl.pallas_call(
        partial(copy_kernel, len(results)),
        in_specs=[hbm] * len(results),
        out_specs=[hbm] * len(results),
        out_shape=results,
        scratch_shapes=[pltpu.VMEM(result.shape, result.dtype) for result in results]
        + [sems(windows + len(results))] * 2,
        compiler_params=pltpu.CompilerParams(vmem_limit_bytes=60 * 1024 * 1024),
    )(*held)
    flat = lambda v: v.reshape(-1)
    return (
        outs[0], outs[1], flat(outs[2]), flat(outs[3]), outs[4], outs[5], outs[6], flat(outs[7]), outs[8], flat(outs[9]),
    )


def solution(mesh):
    in_specs = (P("dp", "seq"), P("dp", "seq")) + (P(),) * 9 + (P("dp", "seq", None),)
    both = ("dp", "seq")
    out_specs = (
        P("dp", "seq", None),
        P(both, None),
        P(both),
        P(both),
        P(both, None),
        P(both, None),
        P(both, None),
        P(both),
        P(both, None),
        P(both),
    )
    return jax.shard_map(per_device, mesh=mesh, in_specs=in_specs, out_specs=out_specs, check_vma=False)
```

```python
from functools import partial

import jax
import jax.numpy as jnp
from jax import lax
from jax.experimental import pallas as pl
from jax.experimental.pallas import tpu as pltpu
from jax.sharding import PartitionSpec as P

HEADS = 16
HEAD_DIM = 64
ROT = 32
GROUP = 4
PHASES = 2
EACH = HEADS // PHASES
HALVES = EACH // GROUP
LANES = 128
ln_epsilon = 1e-05
LOG2E = 1.4426950408889634
F32 = jnp.float32
BF16 = jnp.bfloat16
F8 = jnp.float8_e4m3fn
MESH = pl.DeviceIdType.MESH


def dot(a, b):
    return lax.dot_general(a, b, (((1,), (0,)), ((), ())), preferred_element_type=F32)


def dot_t(a, b):
    return lax.dot_general(a, b, (((1,), (1,)), ((), ())), preferred_element_type=F32)


def t_dot(a, b):
    return lax.dot_general(a, b, (((0,), (0,)), ((), ())), preferred_element_type=F32)


def iota(shape, axis):
    return lax.broadcasted_iota(jnp.int32, shape, axis)


def ones_where(mask):
    return mask.astype(F32).astype(BF16)


def terms_of(value, count):
    parts = []
    for _ in range(count):
        high = value.astype(BF16)
        parts.append(high)
        value = value - high.astype(F32)
    return jnp.concatenate(parts, axis=0)


def roll_pairs(values):
    even = iota(values.shape, 1) % 2 == 0
    return jnp.where(even, -pltpu.roll(values, values.shape[1] - 1, 1), pltpu.roll(values, 1, 1))


def gelu_and_slope(u):
    c = 0.7978845608028654
    t = jnp.tanh(c * (u + 0.044715 * u * u * u))
    return 0.5 * u * (1.0 + t), 0.5 * (1.0 + t) + 0.5 * u * (1.0 - t * t) * c * (1.0 + 3 * 0.044715 * u * u)


def greet(axes):
    barrier = pltpu.get_barrier_semaphore()
    count = 0
    for axis in axes:
        size = lax.axis_size(axis)
        me = lax.axis_index(axis)
        for step in range(1, size):
            pl.semaphore_signal(barrier, inc=1, device_id={axis: lax.rem(me + step, size)}, device_id_type=MESH)
        count += size - 1
    return count


def to_all(axis, source, target, send_sem, recv_sem):
    size = lax.axis_size(axis)
    me = lax.axis_index(axis)
    copies = []
    for step in range(1, size):
        other = lax.rem(me + step, size)
        copies.append(pltpu.make_async_remote_copy(
            src_ref=source(other), dst_ref=target(step), send_sem=send_sem.at[step], recv_sem=recv_sem.at[step],
            device_id={axis: other}, device_id_type=MESH,
        ))
    return copies


def start_all(copies):
    for copy in copies:
        copy.start()


def arrived(copies):
    for copy in copies:
        copy.wait_recv()


class Total:
    def __init__(self, own, low, first, part, second, whole, sems):
        self.own, self.low, self.first, self.part = own, low, first, part
        self.second, self.whole, self.sems = second, whole, sems
        self.columns = low.shape[2]

    def load(self, value):
        for at in range(self.own.shape[0]):
            piece = value[:, at * self.columns : (at + 1) * self.columns]
            self.own[at] = piece
            self.low[at] = piece.astype(BF16)

    def one(self):
        return to_all("dp", lambda other: self.low.at[other], lambda step: self.first.at[step], *self.sems[0:2])

    def two(self):
        return to_all("seq", lambda other: self.part, lambda step: self.second.at[step], *self.sems[2:4])

    def three(self):
        column = lax.axis_index("dp")
        return to_all("dp", lambda other: self.whole.at[column], lambda step: self.whole.at[column], *self.sems[4:6])

    def step1(self):
        start_all(self.one())

    def step2(self):
        column = lax.axis_index("dp")
        value = self.own[column]
        for step, copy in enumerate(self.one(), 1):
            copy.wait_recv()
            value += self.first[step].astype(F32)
        self.own[column] = value
        self.part[...] = value.astype(BF16)
        start_all(self.two())

    def step3(self):
        column = lax.axis_index("dp")
        value = self.own[column]
        for step, copy in enumerate(self.two(), 1):
            copy.wait_recv()
            value += self.second[step].astype(F32)
        self.whole[column] = value.astype(BF16)
        start_all(self.three())

    def finish(self):
        arrived(self.three())

    def sums(self, start, size):
        whole = jnp.concatenate([self.whole[at] for at in range(self.whole.shape[0])], axis=1)
        return whole[:, start : start + size]

    def end(self):
        for copies in (self.one(), self.two(), self.three()):
            for copy in copies:
                copy.wait_send()


def total_scratch(dp, seq, rows, columns):
    return [
        pltpu.VMEM((dp, rows, columns), F32),
        pltpu.VMEM((dp, rows, columns), BF16),
        pltpu.VMEM((dp, rows, columns), BF16),
        pltpu.VMEM((rows, columns), BF16),
        pltpu.VMEM((seq, rows, columns), BF16),
        pltpu.VMEM((dp, rows, columns), BF16),
    ] + [pltpu.SemaphoreType.DMA((size,)) for size in (dp, dp, seq, seq, dp, dp)]


def layer_norm_rows(embed):
    inputs = embed.astype(F32)
    center = inputs - jnp.mean(inputs, axis=1, keepdims=True)
    spread = jnp.mean(center * center, axis=1, keepdims=True)
    rstd = lax.rsqrt(spread + ln_epsilon)
    return inputs, center * rstd, rstd


def head_at(slot):
    return slot % EACH * PHASES + slot // EACH


def gifts(shards, windows):
    counts = []
    for place in range(shards):
        mirror = shards - 1 - place
        spare = PHASES * windows * (place - mirror) / (2.0 * (place + 2))
        counts.append(min(windows, max(0, int(spare + 0.5))))
    return counts


def hooks(shards, windows, count):
    gives = gifts(shards, windows)
    found = []
    for place in range(shards):
        mirror = shards - 1 - place
        costs = [place + 2] * (windows - gives[place]) + [mirror + 2] * gives[mirror] + [place + 2] * windows
        row = []
        for at in range(count):
            spent, step = 0, 0
            while step < len(costs) - 1 and spent + costs[step] < (at + 1) * (shards + 1):
                spent += costs[step]
                step += 1
            row.append(step)
        found.append(row)
    return found


def main_kernel(
    ids_hbm, positions_hbm, embed_hbm, gain_hbm, shift_hbm, b_up_hbm, b_down_hbm, cot_hbm, w_qkv_hbm, w_out_hbm,
    w_up_hbm, w_down_hbm,
    output_hbm, embed_grad_hbm, gain_grad_hbm, shift_grad_hbm, qkv_grad_hbm, out_grad_hbm, up_grad_hbm,
    up_bias_grad_hbm, down_grad_hbm, down_bias_grad_hbm,
    output_ref, embed_grad_ref, gain_grad_ref, shift_grad_ref, qkv_grad_ref, out_grad_ref, up_grad_ref,
    up_bias_grad_ref, down_grad_ref, down_bias_grad_ref,
    po_ref, normed_ref, values_ref, mixed_ref, base_ref,
    both, embed_ref, gain_ref, shift_ref, b_up_ref, b_down_ref, cot_ref, w_qkv, w_out, w_up, w_down,
    tab_ref, grad_ref, po_in, oh_t_ref, oh_ref, oh8_ref, own_ref, keys_t_ref, weights_ref, center_ref, back_ref, cos_ref, sin_ref, turn_ref, projected_ref, low_ref, m_ref, agg_q_ref, agg_k_ref,
    cot_own_ref, act_ref, slope_ref, d_up_ref, e_in, e_part, e_in2,
    load_sem, store_sem, seq_send, seq_recv, gift_send, gift_recv, back_send, back_recv, e1_send, e1_recv, e2_send, e2_recv,
    d_up_send, d_up_recv, *totals,
):
    shards, twice_windows, rows = both.shape
    windows = twice_windows // 2
    vocab, width = embed_ref.shape
    length = shards * rows
    some = w_up.shape[1]
    dp = lax.axis_size("dp")
    column, place = lax.axis_index("dp"), lax.axis_index("seq")
    mirror = shards - 1 - place
    index = column * shards + place
    pairs = ROT // 2
    quarter = LANES // GROUP
    per_phase = EACH * vocab
    give_of = gifts(shards, windows)
    most = max(give_of)
    pick_count = lambda where: sum(
        jnp.where(where == at, jnp.int32(count), jnp.int32(0)) for at, count in enumerate(give_of) if count)
    give, take = pick_count(place), pick_count(mirror)

    small = [
        pltpu.make_async_copy(source, target, load_sem.at[at])
        for at, (source, target) in enumerate((
            (ids_hbm, both.at[place, pl.ds(0, windows), :]),
            (positions_hbm, both.at[place, pl.ds(windows, windows), :]),
            (embed_hbm, embed_ref), (gain_hbm, gain_ref), (shift_hbm, shift_ref)))
    ]
    qkv_load = lambda at: pltpu.make_async_copy(
        w_qkv_hbm.at[:, pl.ds(pl.multiple_of(at * width, width), width)], w_qkv.at[at], load_sem.at[5 + at])
    out_load = pltpu.make_async_copy(w_out_hbm, w_out, load_sem.at[8])
    cot_load = pltpu.make_async_copy(cot_hbm, cot_ref, load_sem.at[9])
    hidden_at = pl.ds(pl.multiple_of(column * some, some), some)
    mlp_loads = [
        pltpu.make_async_copy(source, target, load_sem.at[10 + at])
        for at, (source, target) in enumerate((
            (b_up_hbm.at[:, hidden_at], b_up_ref), (w_up_hbm.at[:, hidden_at], w_up),
            (w_down_hbm.at[hidden_at, :], w_down), (b_down_hbm, b_down_ref)))
    ]
    start_all(small + [qkv_load(at) for at in range(3)] + [cot_load, out_load] + mlp_loads)
    guests = greet(("dp", "seq"))
    for copy in small:
        copy.wait()
    _, xhat, _ = layer_norm_rows(embed_ref[...])
    normed = (xhat * gain_ref[...] + shift_ref[...]).astype(BF16)
    normed_ref[...] = normed

    def project(at, _):
        qkv_load(at).wait()
        projected_ref[at] = dot(normed_ref[...], w_qkv[at])
        return 0

    lax.fori_loop(0, 3, project, 0)
    pl.semaphore_wait(pltpu.get_barrier_semaphore(), guests)
    exchange = to_all("seq", lambda other: both.at[place], lambda step: both.at[place], seq_send, seq_recv)
    start_all(exchange)
    projected = [projected_ref[at] for at in range(3)]
    values = projected[2].astype(BF16)
    values_ref[...] = values
    fill = jnp.zeros((LANES - 3 * vocab, 6 * LANES), BF16)
    for group in range(HEADS // GROUP):
        columns = []
        for table in projected[:2]:
            heads = [head_at(group * GROUP + h) * HEAD_DIM for h in range(GROUP)]
            turned = jnp.concatenate([table[:, h : h + ROT] for h in heads], axis=1)
            plain = jnp.concatenate([table[:, h + ROT : h + HEAD_DIM] for h in heads], axis=1)
            columns += [turned, plain, roll_pairs(turned)]
        tab_ref[group] = jnp.concatenate([terms_of(jnp.concatenate(columns, axis=1), 3), fill], axis=0)
    out_load.wait()
    lane_head = iota((vocab, LANES), 1) // HEAD_DIM
    for at in range(EACH):
        part = values[:, at * LANES : (at + 1) * LANES]
        none = jnp.zeros_like(part)
        stacked = jnp.concatenate([jnp.where(lane_head == h, part, none) for h in range(PHASES)], axis=0)
        mixed = dot(stacked, w_out[at * LANES : (at + 1) * LANES, :]).astype(BF16)
        for h in range(PHASES):
            mixed_ref[(h * EACH + at) * vocab : (h * EACH + at + 1) * vocab, :] = mixed[h * vocab : (h + 1) * vocab, :]
    cot_load.wait()
    give_copy = lambda k: pltpu.make_async_remote_copy(
        src_ref=grad_ref.at[k], dst_ref=grad_ref.at[windows + k], send_sem=gift_send.at[k], recv_sem=gift_recv.at[k],
        device_id={"seq": mirror}, device_id_type=MESH)
    back_copy = lambda k: pltpu.make_async_remote_copy(
        src_ref=po_ref.at[windows + k, pl.ds(0, per_phase), :], dst_ref=po_in.at[k], send_sem=back_send.at[k],
        recv_sem=back_recv.at[k], device_id={"seq": mirror}, device_id_type=MESH)

    def grads_of(phase):
        mixed = mixed_ref[pl.ds(pl.multiple_of(phase * per_phase, per_phase), per_phase), :]

        def step(window, _):
            grad_ref[window] = dot_t(mixed, cot_ref[window]).astype(BF16)
            return 0

        lax.fori_loop(0, windows, step, 0)

    grads_of(0)
    for k in range(most):
        @pl.when(k < give)
        def _(k=k):
            give_copy(k).start()


    arrived(exchange)
    inverse = sum(
        jnp.where(iota((pairs, 1), 0) == p, F32(10000.0 ** (-2.0 * p / ROT)), 0.0) for p in range(pairs))
    tiles = ones_where(iota((vocab, LANES), 1) % vocab == iota((vocab, LANES), 0))
    spread = ones_where(iota((3 * pairs, LANES), 0) % pairs == iota((3 * pairs, LANES), 1) % ROT // 2)
    spread_t = ones_where(iota((LANES, 3 * pairs), 1) % pairs == iota((LANES, 3 * pairs), 0) % ROT // 2)
    cot_total, d_total, sum_total = (Total(*totals[at : at + 6], totals[at + 6 : at + 12]) for at in (0, 12, 24))

    def prepare(window, cot_sum):
        row = lambda at: jnp.concatenate([both[s, pl.ds(at, 1), :] for s in range(shards)], axis=1)
        oh_t = ones_where(iota((vocab, length), 0) == row(window))
        oh_t_ref[window] = oh_t
        tiled = t_dot(oh_t, tiles)
        oh_ref[window] = tiled.astype(BF16)
        oh8_ref[window] = tiled[:, : 3 * vocab].astype(F8)
        angles = inverse * row(window + windows).astype(F32)
        for at, (value, ref) in enumerate(((jnp.cos(angles), cos_ref), (jnp.sin(angles), sin_ref))):
            terms = terms_of(value, 3)
            turn_ref[at, window] = terms
            ref[window] = t_dot(terms, spread)
        own_t = ones_where(iota((vocab, rows), 0) == both[place, pl.ds(window, 1), :])
        return cot_sum + dot(own_t, cot_ref[window])

    cot_sum = lax.fori_loop(0, windows, prepare, jnp.zeros((vocab, width), F32))
    d_rows = width // (dp * shards)
    cot_own_ref[...] = cot_sum
    for ref in (m_ref, agg_q_ref, agg_k_ref):
        ref[...] = jnp.zeros_like(ref)

    halves = range(HALVES)

    def forward(part, phase, window, slot, keep):
        first = part * rows
        span = first + rows
        lane_head = iota((rows, 2 * LANES), 1) % LANES // quarter
        owns, keys, keys_t = [], [], []
        cos, sin = cos_ref[window, :span, :], sin_ref[window, :span, :]
        for half in halves:
            table = tab_ref[phase * HALVES + half]
            raw = dot(oh_ref[window, first:span, :], table[:, : 3 * LANES])
            turned = raw[:, :LANES] * cos[first:, :] + raw[:, 2 * LANES :] * sin[first:, :]
            query = jnp.concatenate([turned, raw[:, LANES : 2 * LANES]], axis=1).astype(BF16)
            owns.append(jnp.concatenate(
                [jnp.where(lane_head == head, query, jnp.zeros_like(query)) for head in range(GROUP)], axis=0))
            raw = dot(oh_ref[window, :span, :], table[:, 3 * LANES :])
            turned = (raw[:, :LANES] * cos + raw[:, 2 * LANES :] * sin).astype(BF16)
            keys.append(jnp.concatenate([turned, raw[:, LANES : 2 * LANES].astype(BF16)], axis=1))
            keys_t.append(turned.T)
        grad = grad_ref[slot].astype(F32)
        lanes_of = lambda v, half: jnp.concatenate(
            [v[(half * GROUP + h) * vocab : (half * GROUP + h + 1) * vocab, :] for h in range(GROUP)], axis=1)
        rows_of = lambda v: [v[:, h * rows : (h + 1) * rows] for h in range(GROUP)]
        kept = iota((rows, GROUP * rows), 0) <= iota((rows, GROUP * rows), 1) % rows
        weights = []
        for half in halves:
            scores = dot_t(keys[half], owns[half]) * (HEAD_DIM**-0.5 * LOG2E)
            last = jnp.where(kept, scores[first:, :], -1e30)
            scores = jnp.concatenate([scores[:first, :], last], axis=0) if first else last
            weights.append(jnp.exp2(scores - jnp.max(scores, axis=0, keepdims=True)).astype(BF16))
        shares, terms, centers, backs = [], [], [], []
        for half in halves:
            summed = dot(oh_t_ref[window, :, :span], weights[half])
            inverse = 1.0 / jnp.sum(summed, axis=0, keepdims=True)
            share = summed * inverse
            own_grad = lanes_of(grad, half)
            off = own_grad - jnp.sum(share * own_grad, axis=0, keepdims=True)
            shares += rows_of(share)
            terms += rows_of(share * off)
            off = off * inverse
            power = 6.0 - jnp.floor(jnp.log2(jnp.maximum(jnp.max(jnp.abs(off), axis=0, keepdims=True), 1e-30)))
            backs.append(jnp.exp2(-power))
            off = off * jnp.exp2(power)
            pieces = []
            for _ in range(3):
                pieces.append(off.astype(F8))
                off = off - pieces[-1].astype(F32)
            centers.append(jnp.concatenate(pieces, axis=0))
        at = pl.ds(pl.multiple_of(phase * per_phase, per_phase), per_phase)
        po_ref[slot, at, :] = jnp.concatenate(shares, axis=0).astype(BF16)
        m_ref[at, :] += dot(jnp.concatenate(terms, axis=0).astype(BF16), oh_ref[window, first:span, :])
        owns = [own[:, :LANES] for own in owns]
        if not keep:
            return owns, keys_t, weights, centers, backs
        for half in halves:
            own_ref[half] = owns[half]
            keys_t_ref[half, :, :span] = keys_t[half]
            weights_ref[half, :span, :] = weights[half]
            center_ref[half] = centers[half]
            back_ref[half] = backs[half]

    def kept_of(part):
        span = (part + 1) * rows
        return (
            [own_ref[half] for half in halves], [keys_t_ref[half, :, :span] for half in halves],
            [weights_ref[half, :span, :] for half in halves], [center_ref[half] for half in halves],
            [back_ref[half] for half in halves])

    def backward(part, phase, window, held):
        owns, keys_t, weights, centers, backs = held
        first = part * rows
        span = first + rows
        cos, sin = cos_ref[window, :span, :], sin_ref[window, :span, :]
        d_query, d_keys = [], []
        for half in halves:
            back = backs[half]
            d_scores = (
                weights[half].astype(F32) * dot(oh8_ref[window, :span, :], centers[half])
            ).astype(BF16)
            for head in range(GROUP):
                d_query.append(
                    dot(keys_t[half][head * quarter : (head + 1) * quarter, :],
                        d_scores[:, head * rows : (head + 1) * rows])
                    * back[:, head * rows : (head + 1) * rows])
            own = owns[half].astype(F32) * jnp.broadcast_to(back, (LANES, GROUP * rows)).T
            d_keys.append(dot(d_scores, own.astype(BF16)))
        parts = [(d * turn).astype(BF16) for turn in (cos, sin) for d in d_keys]
        agg_k_ref[phase] += dot(oh_t_ref[window, :, :span], jnp.concatenate(parts, axis=1))
        d_query = [jnp.concatenate(d_query[h : h + GROUP], axis=0) for h in range(0, EACH, GROUP)]
        turns = [dot(spread_t, turn_ref[at, window, :, first:span]) for at in range(2)]
        parts = [(d * turn).astype(BF16) for turn in turns for d in d_query]
        agg_q_ref[phase] += dot_t(oh_t_ref[window, :, first:span], jnp.concatenate(parts, axis=0))

    two_sends = e_in.shape[0] > 1
    e_rows = e_part.shape[1]

    def mixes_of(phase):
        at = pl.ds(pl.multiple_of(phase * per_phase, per_phase), per_phase)
        total = dot(po_ref[0, at, :], cot_ref[0])
        for window in range(1, windows):
            total += dot(po_ref[window, at, :], cot_ref[window])
        low_ref[at, :] = total.astype(BF16)

    def e_slice(phase, other):
        if two_sends:
            start = phase * per_phase + other * e_rows
        else:
            head = other * HEADS // dp
            start = (head % PHASES * EACH + head // PHASES) * vocab
        return pl.ds(pl.multiple_of(start, vocab), e_rows)

    def e1(phase):
        return to_all(
            "dp", lambda other: low_ref.at[e_slice(phase, other), :], lambda step: e_in.at[phase, step],
            e1_send.at[phase], e1_recv.at[phase])

    first_place = jnp.where(place == 0, F32(1.0), F32(0.0))

    def mlp_forward():
        for copy in mlp_loads:
            copy.wait()
        act, slope = gelu_and_slope(dot(normed_ref[...], w_up[...]) + b_up_ref[...])
        act_ref[...] = act.astype(BF16)
        slope_ref[...] = slope
        part = jnp.concatenate([cot_own_ref[...], dot(act_ref[...], w_down[...]) * first_place], axis=1)
        cot_total.load(part)
        cot_total.step1()

    def d_up_copies():
        return to_all("dp", lambda other: d_up_ref.at[column], lambda step: d_up_ref.at[column], d_up_send, d_up_recv)

    def mlp_backward():
        cot_total.finish()
        d_up = (slope_ref[...] * dot_t(cot_total.sums(0, width), w_down[...])).astype(BF16)
        d_up_ref[column] = d_up
        start_all(d_up_copies())
        d_total.load(dot_t(d_up, w_up[...]) * first_place)
        d_total.step1()

    turn = windows - give + take
    steps = turn + windows
    mlp_forward()
    works = (cot_total.step2, cot_total.step3, mlp_backward, d_total.step2, d_total.step3)
    hooks_of = hooks(shards, windows, len(works))

    def step(at, _):
        phase = jnp.where(at < turn, jnp.int32(0), jnp.int32(1))
        taken = jnp.where(at < windows - give, jnp.int32(0), jnp.int32(1)) * (1 - phase)
        window = phase * (at - turn) + (1 - phase) * ((1 - taken) * (give + at) + taken * (at - windows + give))
        slot = window + taken * windows
        whose = taken * mirror + (1 - taken) * place
        for k in range(most):
            @pl.when((k < take) & (at == windows - give + k))
            def _(k=k):
                give_copy(k).wait_recv()

        for part in range(shards):
            @pl.when(whose == part)
            def _(part=part):
                backward(part, phase, window, forward(part, phase, window, slot, False))

        @pl.when(at >= steps - 2)
        def _():
            done = at - (steps - 2)

            @pl.when(done == 0)
            def _():
                for k in range(most):
                    @pl.when(k < give)
                    def _(k=k):
                        back_copy(k).wait_recv()
                        po_ref[k, :per_phase, :] = po_in[k]

            mixes_of(done)
            if two_sends:
                @pl.when(done == 0)
                def _():
                    start_all(e1(0))

        for k in range(most):
            @pl.when((k < take) & (at == windows - give + k))
            def _(k=k):
                back_copy(k).start()

        @pl.when(at == turn - 1)
        def _():
            for k in range(most):
                @pl.when(k < give)
                def _(k=k):
                    give_copy(k).wait_send()
            grads_of(1)

        for number, work in enumerate(works):
            when = sum(jnp.where(place == p, jnp.int32(hooks_of[p][number]), jnp.int32(0)) for p in range(shards))
            pl.when(at == when)(work)

        return 0

    lax.fori_loop(0, steps, step, 0)
    lane_block = iota((vocab, LANES), 1) // quarter
    of_head = [[None] * HEADS for _ in range(3)]
    for group in range(HEADS // GROUP):
        phase, half = divmod(group, HALVES)
        query_plain = tab_ref[group, :vocab, LANES : 2 * LANES]
        key_plain = tab_ref[group, :vocab, 4 * LANES : 5 * LANES]
        mass = m_ref[group * GROUP * vocab : (group + 1) * GROUP * vocab, :].astype(BF16)
        block = iota((GROUP * vocab, LANES), 0) // vocab == iota((GROUP * vocab, LANES), 1) // quarter
        stacked = jnp.concatenate([key_plain] * GROUP, axis=0)
        plain_q = t_dot(mass, jnp.where(block, stacked, jnp.zeros_like(stacked)))[:vocab, :]
        mixed_k = dot(mass[:, :vocab], query_plain)
        plain_k = sum(
            jnp.where(lane_block == h, mixed_k[h * vocab : (h + 1) * vocab, :], 0.0) for h in range(GROUP))
        for at, ref, plain in ((0, agg_q_ref, plain_q), (1, agg_k_ref, plain_k)):
            cosine = ref[phase, :, half * LANES : (half + 1) * LANES]
            sine = ref[phase, :, (HALVES + half) * LANES : (HALVES + half + 1) * LANES]
            turned = cosine - roll_pairs(sine)
            for h in range(GROUP):
                of_head[at][head_at(group * GROUP + h)] = jnp.concatenate(
                    [turned[:, h * quarter : (h + 1) * quarter], plain[:, h * quarter : (h + 1) * quarter]], axis=1)
    columns = [jnp.concatenate(of_head[at], axis=1) * HEAD_DIM**-0.5 for at in range(2)]
    pieces = []
    lane_head = iota((vocab, LANES), 1) // HEAD_DIM
    for at in range(EACH):
        low = jnp.concatenate(
            [low_ref[(h * EACH + at) * vocab : (h * EACH + at + 1) * vocab, :] for h in range(PHASES)], axis=0)
        both_heads = dot_t(low, w_out[at * LANES : (at + 1) * LANES, :])
        pieces.append(jnp.where(lane_head == 0, both_heads[:vocab, :], both_heads[vocab:, :]))
    columns = jnp.concatenate(columns + pieces, axis=1)
    sum_total.load(columns)
    sum_total.step1()
    start_all(e1(1 if two_sends else 0))

    stores = [
        pltpu.make_async_copy(source, target, store_sem.at[at])
        for at, (source, target) in enumerate((
            (output_ref, output_hbm), (embed_grad_ref, embed_grad_hbm), (gain_grad_ref, gain_grad_hbm),
            (shift_grad_ref, shift_grad_hbm), (qkv_grad_ref, qkv_grad_hbm), (out_grad_ref, out_grad_hbm),
            (up_grad_ref, up_grad_hbm), (up_bias_grad_ref, up_bias_grad_hbm), (down_grad_ref, down_grad_hbm),
            (down_bias_grad_ref, down_bias_grad_hbm)))
    ]
    inputs, xhat, rstd = layer_norm_rows(embed_ref[...])
    base_ref[: HEADS * vocab, :] = mixed_ref[...]
    base_ref[HEADS * vocab :, :] = terms_of(inputs + cot_total.sums(width, width).astype(F32) + b_down_ref[...], 2)

    def finish_window(window, _):
        oh_t = ones_where(iota((vocab, rows), 0) == both[place, pl.ds(window, 1), :])
        output_ref[window] = t_dot(jnp.concatenate([po_ref[window], oh_t, oh_t], axis=0), base_ref[...]).astype(BF16)
        return 0

    lax.fori_loop(0, windows // 2, finish_window, 0)
    sum_total.step2()
    lax.fori_loop(windows // 2, windows, finish_window, 0)
    stores[0].start()
    f_rows = down_grad_ref.shape[0]
    cot_sum = cot_total.sums(0, width)
    pick = ones_where(iota((d_rows, width), 1) == iota((d_rows, width), 0) + index * d_rows)
    pick_f = ones_where(iota((f_rows, some), 1) == iota((f_rows, some), 0) + place * f_rows)
    normed_own = dot_t(pick, normed_ref[...]).astype(BF16)
    down_grad_ref[...] = dot(dot_t(pick_f, act_ref[...]).astype(BF16), cot_sum)
    stores[8].start()
    up_bias_grad_ref[...] = jnp.sum(dot_t(d_up_ref[column], pick_f), axis=0, keepdims=True)
    stores[7].start()
    own_columns = lambda value: jnp.sum(dot_t(terms_of(value, 3), pick), axis=0, keepdims=True)
    down_bias_grad_ref[...] = own_columns(cot_sum.astype(F32))
    stores[9].start()
    sum_total.step3()
    for phase in range(e_in.shape[0]):
        arrived(e1(phase))
        total = low_ref[e_slice(phase, column), :].astype(F32)
        for step in range(1, dp):
            total += e_in[phase, step].astype(F32)
        e_part[phase] = total.astype(BF16)
    kinds, own_rows = e_in2.shape[1:3]

    def e_own(other):
        head = (column * shards + other) * d_rows // HEAD_DIM - column * HEADS // dp
        if not two_sends:
            return pl.ds(0, 1), pl.ds(0, own_rows)
        first_kind = 0 if kinds == PHASES else lax.rem(head, PHASES)
        return pl.ds(first_kind, kinds), pl.ds(pl.multiple_of(head // PHASES * vocab, vocab), own_rows)

    e2 = to_all("seq", lambda other: e_part.at[e_own(other)], lambda step: e_in2.at[step], e2_send, e2_recv)
    start_all(e2)
    arrived(d_up_copies())
    for at in range(dp):
        up_grad_ref[:, at * some : (at + 1) * some] = dot(normed_own, d_up_ref[at])
    stores[6].start()
    d_total.finish()

    sum_total.finish()
    sums = sum_total.sums(0, 3 * width)
    d_normed = d_total.sums(0, width).astype(F32)
    for at in range(3):
        d_normed += dot_t(sums[:, at * width : (at + 1) * width], w_qkv[at])
    qkv_grad_ref[...] = dot(normed_own, sums)
    stores[4].start()
    gain_grad_ref[...] = own_columns(d_normed * xhat)
    stores[2].start()
    shift_grad_ref[...] = own_columns(d_normed)
    stores[3].start()
    scaled = d_normed * gain_ref[...]
    d_input = cot_sum.astype(F32) + rstd * (
        scaled
        - jnp.mean(scaled, axis=1, keepdims=True)
        - xhat * jnp.mean(scaled * xhat, axis=1, keepdims=True)
    )
    wide = dot_t(pick, terms_of(d_input, 3))
    embed_grad_ref[...] = wide[:, :vocab] + wide[:, vocab : 2 * vocab] + wide[:, 2 * vocab :]
    stores[1].start()
    arrived(e2)
    total = e_part[e_own(place)].astype(F32)
    for step in range(1, shards):
        total += e_in2[step].astype(F32)
    own = total.astype(BF16).reshape(kinds * own_rows, width)
    values_own = dot_t(pick, values_ref[...]).astype(BF16)
    row_head = iota((d_rows, vocab), 0) // HEAD_DIM
    left = jnp.concatenate([
        jnp.where(row_head == at * kinds + kind, values_own, jnp.zeros_like(values_own))
        for kind in range(kinds) for at in range(own_rows // vocab)], axis=1)
    out_grad_ref[...] = dot(left, own)
    stores[5].start()
    for copies in [exchange, e2, d_up_copies()] + [e1(phase) for phase in range(e_in.shape[0])]:
        for copy in copies:
            copy.wait_send()
    for k in range(most):
        @pl.when(k < take)
        def _(k=k):
            back_copy(k).wait_send()
    for total in (cot_total, d_total, sum_total):
        total.end()
    for store in stores:
        store.wait()


def copy_kernel(count, *refs):
    sources, targets, held = refs[:count], refs[count : 2 * count], refs[2 * count : 3 * count]
    in_sem, out_sem = refs[3 * count :]
    pieces = []
    for source, target, through in zip(sources, targets, held):
        if len(source.shape) == 3:
            pieces += [(source.at[at], through.at[at], target.at[at]) for at in range(source.shape[0])]
        else:
            pieces.append((source, through, target))
    loads = [pltpu.make_async_copy(s, t, in_sem.at[at]) for at, (s, t, _) in enumerate(pieces)]
    stores = [pltpu.make_async_copy(t, o, out_sem.at[at]) for at, (_, t, o) in enumerate(pieces)]
    start_all(loads)
    for load, store in zip(loads, stores):
        load.wait()
        store.start()
    for store in stores:
        store.wait()


def per_device(
    token_ids, positions, embed, ln_gain, ln_shift, w_qkv, w_out, w_up, b_up, w_down, b_down, cotangent
):
    vocab, width = embed.shape
    hidden = w_up.shape[1]
    windows, rows = token_ids.shape
    dp, seq = lax.axis_size("dp"), lax.axis_size("seq")
    length = seq * rows
    d_rows, f_rows = width // (dp * seq), hidden // (dp * seq)
    some = hidden // dp
    most = max(gifts(seq, windows))
    two_sends = dp <= EACH
    sends = PHASES if two_sends else 1
    e_rows = EACH // dp * vocab if two_sends else vocab
    own_heads = max(1, d_rows // HEAD_DIM)
    kinds = PHASES if own_heads > 1 else 1
    own_rows = own_heads // kinds * vocab
    vmem = pl.BlockSpec(memory_space=pltpu.VMEM)
    hbm = pl.BlockSpec(memory_space=pl.ANY)
    shape = jax.ShapeDtypeStruct
    sems = lambda *sizes: pltpu.SemaphoreType.DMA(sizes)
    gain, shift = ln_gain[None, :], ln_shift[None, :]
    results = [
        shape((windows, rows, width), BF16),
        shape((d_rows, vocab), F32),
        shape((1, d_rows), F32),
        shape((1, d_rows), F32),
        shape((d_rows, 3 * width), F32),
        shape((d_rows, width), F32),
        shape((d_rows, hidden), F32),
        shape((1, f_rows), F32),
        shape((f_rows, width), F32),
        shape((1, d_rows), F32),
    ]
    held = pl.pallas_call(
        main_kernel,
        in_specs=[hbm] * 12,
        out_specs=[hbm] * len(results),
        out_shape=results,
        scratch_shapes=[pltpu.VMEM(result.shape, result.dtype) for result in results] + [
            pltpu.VMEM((windows + most, HEADS * vocab, rows), BF16),
            pltpu.VMEM((vocab, width), BF16),
            pltpu.VMEM((vocab, width), BF16),
            pltpu.VMEM((HEADS * vocab, width), BF16),
            pltpu.VMEM(((HEADS + 2) * vocab, width), BF16),
            pltpu.VMEM((seq, 2 * windows, rows), jnp.int32),
            pltpu.VMEM((vocab, width), BF16),
            pltpu.VMEM((1, width), F32),
            pltpu.VMEM((1, width), F32),
            pltpu.VMEM((1, some), F32),
            pltpu.VMEM((1, width), F32),
            pltpu.VMEM((windows, rows, width), BF16),
            pltpu.VMEM((3, width, width), BF16),
            pltpu.VMEM((width, width), BF16),
            pltpu.VMEM((width, some), BF16),
            pltpu.VMEM((some, width), BF16),
            pltpu.VMEM((HEADS // GROUP, LANES, 6 * LANES), BF16),
            pltpu.VMEM((windows + most, EACH * vocab, rows), BF16),
            pltpu.VMEM((max(most, 1), EACH * vocab, rows), BF16),
            pltpu.VMEM((windows, vocab, length), BF16),
            pltpu.VMEM((windows, length, LANES), BF16),
            pltpu.VMEM((windows, length, 3 * vocab), F8),
            pltpu.VMEM((HALVES, GROUP * rows, LANES), BF16),
            pltpu.VMEM((HALVES, LANES, length), BF16),
            pltpu.VMEM((HALVES, length, GROUP * rows), BF16),
            pltpu.VMEM((HALVES, 3 * vocab, GROUP * rows), F8),
            pltpu.VMEM((HALVES, 1, GROUP * rows), F32),
            pltpu.VMEM((windows, length, LANES), F32),
            pltpu.VMEM((windows, length, LANES), F32),
            pltpu.VMEM((2, windows, 3 * ROT // 2, length), BF16),
            pltpu.VMEM((3, vocab, width), F32),
            pltpu.VMEM((HEADS * vocab, width), BF16),
            pltpu.VMEM((HEADS * vocab, LANES), F32),
            pltpu.VMEM((PHASES, vocab, 2 * HALVES * LANES), F32),
            pltpu.VMEM((PHASES, vocab, 2 * HALVES * LANES), F32),
            pltpu.VMEM((vocab, width), F32),
            pltpu.VMEM((vocab, some), BF16),
            pltpu.VMEM((vocab, some), F32),
            pltpu.VMEM((dp, vocab, some), BF16),
            pltpu.VMEM((sends, dp, e_rows, width), BF16),
            pltpu.VMEM((sends, e_rows, width), BF16),
            pltpu.VMEM((seq, kinds, own_rows, width), BF16),
            sems(14),
            sems(len(results)),
            sems(seq),
            sems(seq),
            sems(max(most, 1)),
            sems(max(most, 1)),
            sems(max(most, 1)),
            sems(max(most, 1)),
            sems(sends, dp),
            sems(sends, dp),
            sems(seq),
            sems(seq),
            sems(dp),
            sems(dp),
        ]
        + total_scratch(dp, seq, vocab, 2 * width // dp)
        + total_scratch(dp, seq, vocab, width // dp)
        + total_scratch(dp, seq, vocab, 3 * width // dp),
        compiler_params=pltpu.CompilerParams(
            vmem_limit_bytes=60 * 1024 * 1024, collective_id=1, has_side_effects=True),
    )(token_ids, positions, embed, gain, shift, b_up[None, :], b_down[None, :], cotangent, w_qkv, w_out, w_up, w_down)
    outs = pl.pallas_call(
        partial(copy_kernel, len(results)),
        in_specs=[hbm] * len(results),
        out_specs=[hbm] * len(results),
        out_shape=results,
        scratch_shapes=[pltpu.VMEM(result.shape, result.dtype) for result in results]
        + [sems(windows + len(results))] * 2,
        compiler_params=pltpu.CompilerParams(vmem_limit_bytes=60 * 1024 * 1024),
    )(*held)
    flat = lambda v: v.reshape(-1)
    return (
        outs[0], outs[1], flat(outs[2]), flat(outs[3]), outs[4], outs[5], outs[6], flat(outs[7]), outs[8], flat(outs[9]),
    )


def solution(mesh):
    in_specs = (P("dp", "seq"), P("dp", "seq")) + (P(),) * 9 + (P("dp", "seq", None),)
    both = ("dp", "seq")
    out_specs = (
        P("dp", "seq", None),
        P(both, None),
        P(both),
        P(both),
        P(both, None),
        P(both, None),
        P(both, None),
        P(both),
        P(both, None),
        P(both),
    )
    return jax.shard_map(per_device, mesh=mesh, in_specs=in_specs, out_specs=out_specs, check_vma=False)
```
